32 devices in a mesh: wide: 8 (over z, x), blk: 4 (over y, core).
Axes of the slice: x: 2, y: 2, z: 4, core: 2. Of those that a mesh axis runs over, the one named last changes fastest.
Arguments:
- amplitudes: bfloat16 [32, 32, 8, 4096], P('blk', 'wide'), may hold values from -6 to 6
- integrals: bfloat16 [8, 2, 2048, 4096], P('wide', None, 'blk'), may hold values from -0.09375 to 0.09375
- owner: int32 [8], replicated, may hold values from 0 to 7, each once
- targets: int32 [8, 2], replicated, may hold values from 0 to 7, all different within a row
- counts: int32 [8], replicated, may hold values from 1 to 2, 12 in all
Outputs:
- ladder: bfloat16 [8, 32, 32, 2048], P(None, 'blk', 'wide')
The draws below stay inside these ranges and needn't reach their ends.
Inputs may be any that keep to these rules, and one draw needn't show every extreme that they name: Each contracted tile has its own owner slot. `targets`: the output tiles of one contracted tile are distinct, and every output tile is named by some contracted tile. The counts sum to 12 and one of them is 2.
All inputs are finite; a program needn't handle non-finite values.
Results may differ from the reference program's by a relative error of at most 0.0044.
Values may be sent and summed in bfloat16 or wider, within the bound.
No kernel may reach another device: no remote copies, remote signals or barrier semaphores. Data moves between devices by JAX's collectives and lax.ppermute only.
A program may use at most 128 MiB of HBM per device.

```python
import math
import jax
import jax.numpy as jnp
import numpy as np
from jax import lax

TW = 4096
NI = 32
NJ = 32
AB = 2048
KMAX = 2
NT = 8
NP = 8


def shard_levels(key, shape, pieces, smallest, top_value):
    factor_of, own = 1.0, jax.random.fold_in(key, 6)
    for position, shards_of in pieces:
        steps = jnp.exp(jax.random.uniform(jax.random.fold_in(own, position), (shards_of,), jnp.float32, smallest / len(pieces), top_value / len(pieces)))
        factor_of = factor_of * jnp.repeat(steps, shape[position] // shards_of).reshape([-1 if axis == position else 1 for axis in range(len(shape))])
    return factor_of


def distinct(key, rows, count, top, lift):
    sequence = jax.random.permutation(jax.random.fold_in(key, 1), count)
    pull = sequence
    for power in range(3):
        pull = pull * pull // count
    pull = pull * lift // count
    chance = jax.random.randint(jax.random.fold_in(key, 2), (rows, count), 0, 4096) + pull
    fixed_rows = jax.random.permutation(jax.random.fold_in(key, 3), rows)[jnp.arange(count) % rows]
    chance = jnp.where(jnp.arange(rows)[:, None] == fixed_rows[None, :], 1 << 14, chance)
    score = chance * count + jnp.arange(count)
    return lax.top_k(score.astype(jnp.int32), top)[1].astype(jnp.int32)


def profile(count, total, most, slope):
    weights = [(1 << 20) // math.isqrt(rank ** slope) + 1 for rank in range(2, count + 1)]
    rest, holding = total - most - (count - 1), [1] * (count - 1)
    while rest > 0:
        movable = [i for i in range(count - 1) if holding[i] < most]
        mass, left = sum([weights[i] for i in movable]), rest
        for i in movable:
            more = min(most - holding[i], max(1, left * weights[i] // mass), rest)
            holding[i] = holding[i] + more
            rest = rest - more
    return np.array([most] + holding)


def uneven(rng, amount, total, most, lean):
    if amount == 2:
        one = jax.random.randint(rng, (), max(1, total - most), min(most, total - 1) + 1)
        return jnp.stack([one, total - one])
    sizes = jnp.asarray(profile(amount, total, most, lean), jnp.int32)
    couples = (amount - 1) // 2
    source_of, sink = sizes[1:1 + 2 * couples:2], sizes[2:2 + 2 * couples:2]
    slack = jnp.minimum(source_of - 1, most - sink)
    shifted = jax.random.randint(jax.random.fold_in(rng, 1), (couples,), 0, 1 << 20) % (slack + 1)
    sizes = sizes.at[1:1 + 2 * couples:2].set(source_of - shifted).at[2:2 + 2 * couples:2].set(sink + shifted)
    return sizes[jax.random.permutation(jax.random.fold_in(rng, 2), amount)]


def gaussian(own_key, dims, spread, bound, split=(), held_as=jnp.bfloat16):
    drawn = spread * jax.random.normal(own_key, dims, jnp.float32)
    if split:
        drawn = drawn * shard_levels(own_key, dims, split, -0.22, 0.18)
    return jnp.clip(drawn, -bound, bound).astype(held_as)


def setup_inputs(seed: int = 0) -> dict:
    keys = jax.random.split(jax.random.key(seed), 6)
    amplitudes = gaussian(keys[0], (NI, NJ, NT, TW), 1.0, 6.0, ((0, 4), (1, 8)))
    integrals = gaussian(keys[1], (NT, KMAX, AB, TW), TW ** -0.5, 0.09375, ((0, 8), (2, 4)))
    owner = jax.random.permutation(keys[2], NT).astype(jnp.int32)
    targets = distinct(keys[3], NT, NP, KMAX, 2048)
    counts = uneven(keys[4], NT, 3 * NT // 2, KMAX, 0).astype(jnp.int32)
    return dict(amplitudes=amplitudes, integrals=integrals, owner=owner, targets=targets, counts=counts)


def reference(amplitudes, integrals, owner, targets, counts):
    pair_count = NI * NJ

    def accumulate(running, tile_index):
        amp_tile = lax.dynamic_index_in_dim(amplitudes, tile_index, 2, keepdims=False)
        amp_tile = amp_tile.reshape(pair_count, TW).astype(jnp.float32)
        integral_block = lax.dynamic_index_in_dim(integrals, owner[tile_index], 0, keepdims=False).astype(jnp.float32)
        for slot_index in range(KMAX):
            product = jnp.dot(amp_tile, integral_block[slot_index].T, precision=lax.Precision.HIGHEST)
            rounded = lax.optimization_barrier(product.astype(jnp.bfloat16)).astype(jnp.float32)
            kept_flag = (slot_index < counts[tile_index]).astype(jnp.float32)
            running = running.at[targets[tile_index, slot_index]].add(rounded * kept_flag)
        return running, None

    start_sum = jnp.zeros((NP, pair_count, AB), jnp.float32)
    running, unused = lax.scan(accumulate, start_sum, jnp.arange(NT, dtype=jnp.int32))
    return running.reshape(NP, NI, NJ, AB).astype(jnp.bfloat16)
```

```python
import functools

import jax
import jax.numpy as jnp
from jax import lax
from jax.experimental import pallas as pl
from jax.experimental.pallas import tpu as pltpu
from jax.sharding import PartitionSpec as P

MIB = 1 << 20
SMEM = pl.BlockSpec(memory_space=pltpu.SMEM)


def find_tile(owner_ref, slot):
    def step(q, found):
        return jnp.where(owner_ref[q] == slot, q, found)

    return lax.fori_loop(0, owner_ref.shape[0], step, jnp.int32(0))


def select_kernel(rows, owner_ref, amp_ref, *rest):
    outs, pick_ref = rest[:-1], rest[-1]
    tiles = owner_ref.shape[0]

    @pl.when(pl.program_id(0) == 0)
    def _():
        me = lax.axis_index("wide")
        shape = pick_ref.shape
        out_row = lax.broadcasted_iota(jnp.int32, shape, 0)
        in_row = lax.broadcasted_iota(jnp.int32, shape, 1)
        slot = lax.bitwise_xor(out_row // rows, me)
        tile = in_row % tiles
        place = jnp.zeros(shape, jnp.int32)
        for q in range(tiles):
            place = jnp.where(tile == q, owner_ref[q], place)
        chosen = (place == slot) & (out_row % rows == in_row // tiles)
        pick_ref[...] = jnp.where(chosen, 1.0, 0.0).astype(pick_ref.dtype)

    moved = jnp.dot(pick_ref[...], amp_ref[...], preferred_element_type=jnp.float32)
    moved = moved.astype(amp_ref.dtype)
    for m, out in enumerate(outs):
        out[...] = moved[m * rows : (m + 1) * rows, :]


def select(amplitudes, owner, wide):
    i, j, tiles, width = amplitudes.shape
    rows = i * j
    block = min(width, 1024)
    return pl.pallas_call(
        functools.partial(select_kernel, rows),
        grid=(width // block,),
        in_specs=[SMEM, pl.BlockSpec((rows * tiles, block), lambda c: (0, c))],
        out_specs=[pl.BlockSpec((rows, block), lambda c: (0, c))] * wide,
        out_shape=[jax.ShapeDtypeStruct((rows, width), amplitudes.dtype)] * wide,
        scratch_shapes=[pltpu.VMEM((wide * rows, rows * tiles), amplitudes.dtype)],
        compiler_params=pltpu.CompilerParams(vmem_limit_bytes=32 * MIB),
        cost_estimate=pl.CostEstimate(
            flops=2 * wide * rows * rows * tiles * width,
            bytes_accessed=4 * rows * tiles * width,
            transcendentals=0,
        ),
        name="select_tiles",
    )(owner, amplitudes.reshape(rows * tiles, width))


def contract_kernel(count, rows, owner_ref, counts_ref, *rest):
    parts, integ_ref = rest[:count], rest[count]
    outs, all_ref = rest[count + 1 : -1], rest[-1]
    partner = pl.program_id(0)

    @pl.when((partner == 0) & (pl.program_id(1) == 0))
    def _():
        for n, part in enumerate(parts):
            all_ref[n * rows : (n + 1) * rows, :] = part[...]

    live = partner < counts_ref[find_tile(owner_ref, lax.axis_index("wide"))]

    @pl.when(live)
    def _():
        value = lax.dot_general(
            all_ref[...],
            integ_ref[0],
            (((1,), (1,)), ((), ())),
            preferred_element_type=jnp.float32,
        ).astype(jnp.bfloat16)
        for n, out in enumerate(outs):
            out[...] = value[n * rows : (n + 1) * rows, :]

    @pl.when(jnp.logical_not(live))
    def _():
        for out in outs:
            out[...] = jnp.zeros_like(out)


def contract(parts, integrals, owner, counts):
    rows, width = parts[0].shape
    partners, ab, _ = integrals.shape
    block = min(ab, 256)
    steps = ab // block
    count = len(parts)
    return pl.pallas_call(
        functools.partial(contract_kernel, count, rows),
        grid=(partners, steps),
        in_specs=[SMEM, SMEM]
        + [pl.BlockSpec((rows, width), lambda k, c: (0, 0))] * count
        + [pl.BlockSpec((1, block, width), lambda k, c: (k, c, 0))],
        out_specs=[pl.BlockSpec((rows, block), lambda k, c: (0, k * steps + c))] * count,
        out_shape=[jax.ShapeDtypeStruct((rows, partners * ab), jnp.bfloat16)] * count,
        scratch_shapes=[pltpu.VMEM((count * rows, width), parts[0].dtype)],
        compiler_params=pltpu.CompilerParams(vmem_limit_bytes=32 * MIB),
        cost_estimate=pl.CostEstimate(
            flops=2 * count * rows * width * partners * ab,
            bytes_accessed=2 * (partners * ab * width + count * rows * (width + partners * ab)),
            transcendentals=0,
        ),
        name="contract_rows",
    )(owner, counts, *parts, integrals)


def collect_kernel(wide, blk, partners, owner_ref, targets_ref, counts_ref, *rest):
    parts, out_ref, sum_ref = rest[:-2], rest[-2], rest[-1]
    me, mine = lax.axis_index("wide"), lax.axis_index("blk")
    ab = parts[0].shape[1] // partners
    sum_ref[...] = jnp.zeros_like(sum_ref)
    for m in range(wide):
        tile = find_tile(owner_ref, lax.bitwise_xor(me, m))
        live = counts_ref[tile]
        for k in range(partners):
            target = targets_ref[tile, k]

            @pl.when(k < live)
            def _():
                for n in range(blk):
                    begin = pl.multiple_of(lax.bitwise_xor(mine, n) * ab, 128)
                    value = parts[m * blk + n][:, k * ab : (k + 1) * ab]
                    sum_ref[target, :, pl.ds(begin, ab)] += value.astype(jnp.float32)

    out_ref[...] = sum_ref[...].astype(out_ref.dtype)


def collect(parts, owner, targets, counts, wide, blk, tiles_out):
    rows, columns = parts[0].shape
    partners = targets.shape[1]
    shape = (tiles_out, rows, blk * columns // partners)
    return pl.pallas_call(
        functools.partial(collect_kernel, wide, blk, partners),
        in_specs=[SMEM, SMEM, SMEM] + [pl.BlockSpec(memory_space=pltpu.VMEM)] * len(parts),
        out_specs=pl.BlockSpec(memory_space=pltpu.VMEM),
        out_shape=jax.ShapeDtypeStruct(shape, jnp.bfloat16),
        scratch_shapes=[pltpu.VMEM(shape, jnp.float32)],
        compiler_params=pltpu.CompilerParams(vmem_limit_bytes=32 * MIB),
        name="collect_targets",
    )(owner, targets, counts, *parts)


def body(amplitudes, integrals, owner, targets, counts):
    wide, blk = lax.axis_size("wide"), lax.axis_size("blk")
    i, j, tiles, width = amplitudes.shape
    rows = i * j

    def swap(value, axis, mask):
        return lax.ppermute(value, axis, [(s, s ^ mask) for s in range(lax.axis_size(axis))])

    def swap_both(value, m, n):
        pairs = [
            (w * blk + b, (w ^ m) * blk + (b ^ n)) for w in range(wide) for b in range(blk)
        ]
        return lax.ppermute(value, ("wide", "blk"), pairs)

    sent = select(amplitudes, owner, wide)
    gathered = []
    for m in range(wide):
        held = [sent[0] if m == 0 else swap(sent[m], "wide", m)]
        by_n = {0: held[0]}
        bit = blk // 2
        while bit:
            by_n.update({n | bit: swap(value, "blk", bit) for n, value in list(by_n.items())})
            bit //= 2
        gathered.append([by_n[n] for n in range(blk)])

    group = max(1, min(wide, 256 // (blk * rows)))
    returned = []
    for first in range(0, wide, group):
        masks = range(first, first + group)
        parts = [part for m in masks for part in gathered[m]]
        products = contract(parts, integrals[0], owner, counts)
        for at, product in enumerate(products):
            m, n = first + at // blk, at % blk
            returned.append(product if m == n == 0 else swap_both(product, m, n))

    tiles_out = wide
    ladder = collect(returned, owner, targets, counts, wide, blk, tiles_out)
    return ladder.reshape(tiles_out, i, j, -1)


def body_large(amplitudes, integrals, owner, targets, counts):
    wide_count = lax.axis_size("wide")
    my_index = lax.axis_index("wide")
    tile_ids = jnp.arange(owner.shape[0], dtype=jnp.int32)
    holder = jnp.sum(jnp.where(owner[None, :] == tile_ids[:, None], tile_ids[None, :], 0), axis=1)
    ordered = jnp.take(amplitudes, holder, axis=2)
    my_tile = lax.all_to_all(ordered, "wide", split_axis=2, concat_axis=1, tiled=True)
    my_holder = lax.dynamic_index_in_dim(holder, my_index, 0, keepdims=False)
    my_count = lax.dynamic_index_in_dim(counts, my_holder, 0, keepdims=False)
    slot_ids = jnp.arange(targets.shape[1], dtype=jnp.int32)
    live_slots = (slot_ids < my_count).astype(jnp.float32)
    my_integrals = integrals[0]
    width = my_tile.shape[3]
    portion = lax.all_gather(my_tile, "blk", axis=0, tiled=True)
    flat_rows = portion.reshape(-1, width)
    result = jnp.einsum("rc,kac->rka", flat_rows, my_integrals, preferred_element_type=jnp.float32)
    partial_value = result.reshape(
        portion.shape[0], portion.shape[1], my_integrals.shape[0], my_integrals.shape[1]
    )
    shaped = (partial_value * live_slots[None, None, :, None]).astype(jnp.bfloat16)
    received = lax.all_to_all(
        lax.all_to_all(shaped, "wide", split_axis=1, concat_axis=2, tiled=True),
        "blk",
        split_axis=0,
        concat_axis=3,
        tiled=True,
    )
    slot_targets = jnp.take(targets, holder, axis=0).reshape(-1)
    window_ids = jnp.arange(wide_count, dtype=jnp.int32)
    selector = (slot_targets[None, :] == window_ids[:, None]).astype(jnp.bfloat16)
    ladder = jnp.einsum("ps,ijsa->pija", selector, received, preferred_element_type=jnp.float32)
    return ladder.astype(jnp.bfloat16)


def solution(mesh):
    few = mesh.size <= 64
    placed = (P("blk", "wide", None, None), P("wide", None, "blk", None), P(), P(), P())
    return jax.shard_map(
        body if few else body_large,
        mesh=mesh,
        in_specs=placed,
        out_specs=P(None, "blk", "wide", None),
        check_vma=False,
    )
```

```python
import functools

import jax
import jax.numpy as jnp
from jax import lax
from jax.experimental import pallas as pl
from jax.experimental.pallas import tpu as pltpu
from jax.sharding import PartitionSpec as P

MIB = 1 << 20
SMEM = pl.BlockSpec(memory_space=pltpu.SMEM)


def find_tile(owner_ref, slot):
    def step(q, found):
        return jnp.where(owner_ref[q] == slot, q, found)

    return lax.fori_loop(0, owner_ref.shape[0], step, jnp.int32(0))


def select_kernel(rows, owner_ref, amp_ref, *rest):
    outs, pick_ref = rest[:-1], rest[-1]
    tiles = owner_ref.shape[0]

    @pl.when(pl.program_id(0) == 0)
    def _():
        me = lax.axis_index("wide")
        shape = pick_ref.shape
        out_row = lax.broadcasted_iota(jnp.int32, shape, 0)
        in_row = lax.broadcasted_iota(jnp.int32, shape, 1)
        slot = lax.bitwise_xor(out_row // rows, me)
        tile = in_row % tiles
        place = jnp.zeros(shape, jnp.int32)
        for q in range(tiles):
            place = jnp.where(tile == q, owner_ref[q], place)
        chosen = (place == slot) & (out_row % rows == in_row // tiles)
        pick_ref[...] = jnp.where(chosen, 1.0, 0.0).astype(pick_ref.dtype)

    moved = jnp.dot(pick_ref[...], amp_ref[...], preferred_element_type=jnp.float32)
    moved = moved.astype(amp_ref.dtype)
    for m, out in enumerate(outs):
        out[...] = moved[m * rows : (m + 1) * rows, :]


def select(amplitudes, owner, wide):
    i, j, tiles, width = amplitudes.shape
    rows = i * j
    block = min(width, 1024)
    return pl.pallas_call(
        functools.partial(select_kernel, rows),
        grid=(width // block,),
        in_specs=[SMEM, pl.BlockSpec((rows * tiles, block), lambda c: (0, c))],
        out_specs=[pl.BlockSpec((rows, block), lambda c: (0, c))] * wide,
        out_shape=[jax.ShapeDtypeStruct((rows, width), amplitudes.dtype)] * wide,
        scratch_shapes=[pltpu.VMEM((wide * rows, rows * tiles), amplitudes.dtype)],
        compiler_params=pltpu.CompilerParams(vmem_limit_bytes=32 * MIB),
        cost_estimate=pl.CostEstimate(
            flops=2 * wide * rows * rows * tiles * width,
            bytes_accessed=4 * rows * tiles * width,
            transcendentals=0,
        ),
        name="select_tiles",
    )(owner, amplitudes.reshape(rows * tiles, width))


def contract_kernel(owner_ref, counts_ref, rows_ref, integ_ref, out_ref):
    live = pl.program_id(0) < counts_ref[find_tile(owner_ref, lax.axis_index("wide"))]

    @pl.when(live)
    def _():
        out_ref[...] = lax.dot_general(
            rows_ref[...],
            integ_ref[0],
            (((1,), (1,)), ((), ())),
            preferred_element_type=jnp.float32,
        ).astype(out_ref.dtype)

    @pl.when(jnp.logical_not(live))
    def _():
        out_ref[...] = jnp.zeros_like(out_ref)


def contract(rows, integrals, owner, counts):
    count, width = rows.shape
    partners, ab, _ = integrals.shape
    block = min(ab, 256)
    steps = ab // block
    return pl.pallas_call(
        contract_kernel,
        grid=(partners, steps),
        in_specs=[
            SMEM,
            SMEM,
            pl.BlockSpec((count, width), lambda k, c: (0, 0)),
            pl.BlockSpec((1, block, width), lambda k, c: (k, c, 0)),
        ],
        out_specs=pl.BlockSpec((count, block), lambda k, c: (0, k * steps + c)),
        out_shape=jax.ShapeDtypeStruct((count, partners * ab), jnp.bfloat16),
        compiler_params=pltpu.CompilerParams(vmem_limit_bytes=32 * MIB),
        cost_estimate=pl.CostEstimate(
            flops=2 * count * width * partners * ab,
            bytes_accessed=2 * (partners * ab * width + count * (width + partners * ab)),
            transcendentals=0,
        ),
        name="contract_rows",
    )(owner, counts, rows, integrals)


def collect_kernel(partners, owner_ref, targets_ref, counts_ref, *rest):
    parts, out_ref, sum_ref = rest[:-2], rest[-2], rest[-1]
    me = lax.axis_index("wide")
    blk, _, columns = parts[0].shape
    ab = columns // partners
    sum_ref[...] = jnp.zeros_like(sum_ref)
    for m, part in enumerate(parts):
        tile = find_tile(owner_ref, lax.bitwise_xor(me, m))
        live = counts_ref[tile]
        for k in range(partners):
            target = targets_ref[tile, k]

            @pl.when(k < live)
            def _():
                for b in range(blk):
                    value = part[b, :, k * ab : (k + 1) * ab]
                    sum_ref[target, :, b * ab : (b + 1) * ab] += value.astype(jnp.float32)

    out_ref[...] = sum_ref[...].astype(out_ref.dtype)


def collect(parts, owner, targets, counts, tiles_out):
    blk, rows, columns = parts[0].shape
    partners = targets.shape[1]
    shape = (tiles_out, rows, blk * columns // partners)
    return pl.pallas_call(
        functools.partial(collect_kernel, partners),
        in_specs=[SMEM, SMEM, SMEM] + [pl.BlockSpec(memory_space=pltpu.VMEM)] * len(parts),
        out_specs=pl.BlockSpec(memory_space=pltpu.VMEM),
        out_shape=jax.ShapeDtypeStruct(shape, jnp.bfloat16),
        scratch_shapes=[pltpu.VMEM(shape, jnp.float32)],
        compiler_params=pltpu.CompilerParams(vmem_limit_bytes=32 * MIB),
        name="collect_targets",
    )(owner, targets, counts, *parts)


def after(value, earlier):
    return lax.optimization_barrier((value, earlier))[0]


def body(amplitudes, integrals, owner, targets, counts):
    wide, blk = lax.axis_size("wide"), lax.axis_size("blk")
    i, j, tiles, width = amplitudes.shape
    rows = i * j

    def swap(value, mask):
        return lax.ppermute(value, "wide", [(s, s ^ mask) for s in range(wide)])

    def exchange(value):
        return lax.all_to_all(value, "blk", split_axis=0, concat_axis=0, tiled=True)

    sent = select(amplitudes, owner, wide)
    held = [sent[0]]
    far = wide // 2
    crossing = {}
    for m in range(far, wide):
        value = sent[m] if m < far + 2 else after(sent[m], crossing[m - 2])
        crossing[m] = swap(value, m)
    held += [swap(sent[m], m) for m in range(1, far)] + [crossing[m] for m in range(far, wide)]

    returned = [None] * wide
    group = 2
    for first in range(0, wide, group):
        masks = range(first, first + group)
        rows_here = jnp.concatenate([held[m] for m in masks], axis=0)
        rows_all = lax.all_gather(rows_here, "blk", axis=0, tiled=True)
        product = contract(rows_all, integrals[0], owner, counts)
        product = product.reshape(blk, group, rows, -1)
        if first == far:
            moved = jnp.stack([swap(product[:, g], m) for g, m in enumerate(masks)], axis=1)
            moved = exchange(moved)
            for g, m in enumerate(masks):
                returned[m] = moved[:, g]
        else:
            moved = exchange(product)
            for g, m in enumerate(masks):
                returned[m] = moved[:, g] if m == 0 else swap(moved[:, g], m)

    tiles_out = wide
    ladder = collect(returned, owner, targets, counts, tiles_out)
    return ladder.reshape(tiles_out, i, j, -1)


def body_large(amplitudes, integrals, owner, targets, counts):
    wide_count = lax.axis_size("wide")
    my_index = lax.axis_index("wide")
    tile_ids = jnp.arange(owner.shape[0], dtype=jnp.int32)
    holder = jnp.sum(jnp.where(owner[None, :] == tile_ids[:, None], tile_ids[None, :], 0), axis=1)
    ordered = jnp.take(amplitudes, holder, axis=2)
    my_tile = lax.all_to_all(ordered, "wide", split_axis=2, concat_axis=1, tiled=True)
    my_holder = lax.dynamic_index_in_dim(holder, my_index, 0, keepdims=False)
    my_count = lax.dynamic_index_in_dim(counts, my_holder, 0, keepdims=False)
    slot_ids = jnp.arange(targets.shape[1], dtype=jnp.int32)
    live_slots = (slot_ids < my_count).astype(jnp.float32)
    my_integrals = integrals[0]
    width = my_tile.shape[3]
    portion = lax.all_gather(my_tile, "blk", axis=0, tiled=True)
    flat_rows = portion.reshape(-1, width)
    result = jnp.einsum("rc,kac->rka", flat_rows, my_integrals, preferred_element_type=jnp.float32)
    partial_value = result.reshape(
        portion.shape[0], portion.shape[1], my_integrals.shape[0], my_integrals.shape[1]
    )
    shaped = (partial_value * live_slots[None, None, :, None]).astype(jnp.bfloat16)
    received = lax.all_to_all(
        lax.all_to_all(shaped, "wide", split_axis=1, concat_axis=2, tiled=True),
        "blk",
        split_axis=0,
        concat_axis=3,
        tiled=True,
    )
    slot_targets = jnp.take(targets, holder, axis=0).reshape(-1)
    window_ids = jnp.arange(wide_count, dtype=jnp.int32)
    selector = (slot_targets[None, :] == window_ids[:, None]).astype(jnp.bfloat16)
    ladder = jnp.einsum("ps,ijsa->pija", selector, received, preferred_element_type=jnp.float32)
    return ladder.astype(jnp.bfloat16)


def solution(mesh):
    few = mesh.size <= 64
    placed = (P("blk", "wide", None, None), P("wide", None, "blk", None), P(), P(), P())
    return jax.shard_map(
        body if few else body_large,
        mesh=mesh,
        in_specs=placed,
        out_specs=P(None, "blk", "wide", None),
        check_vma=False,
    )
```

```python
import functools

import jax
import jax.numpy as jnp
from jax import lax
from jax.experimental import pallas as pl
from jax.experimental.pallas import tpu as pltpu
from jax.sharding import PartitionSpec as P

MIB = 1 << 20
KERNEL_VMEM = 48 * MIB
SMEM = pl.BlockSpec(memory_space=pltpu.SMEM)


def find_tile(owner_ref, slot):
    def step(q, found):
        return jnp.where(owner_ref[q] == slot, q, found)

    return lax.fori_loop(0, owner_ref.shape[0], step, jnp.int32(0))


def select_kernel(rows, owner_ref, amp_ref, *rest):
    outs, pick_ref = rest[:-1], rest[-1]
    tiles = owner_ref.shape[0]

    @pl.when(pl.program_id(0) == 0)
    def _():
        me = lax.axis_index("wide")
        shape = pick_ref.shape
        out_row = lax.broadcasted_iota(jnp.int32, shape, 0)
        in_row = lax.broadcasted_iota(jnp.int32, shape, 1)
        slot = lax.bitwise_xor(out_row // rows, me)
        tile = in_row % tiles
        place = jnp.zeros(shape, jnp.int32)
        for q in range(tiles):
            place = jnp.where(tile == q, owner_ref[q], place)
        chosen = (place == slot) & (out_row % rows == in_row // tiles)
        pick_ref[...] = jnp.where(chosen, 1.0, 0.0).astype(pick_ref.dtype)

    moved = jnp.dot(pick_ref[...], amp_ref[...], preferred_element_type=jnp.float32)
    moved = moved.astype(amp_ref.dtype)
    for m, out in enumerate(outs):
        out[...] = moved[m * rows : (m + 1) * rows, :]


def select(amplitudes, owner, wide):
    i, j, tiles, width = amplitudes.shape
    rows = i * j
    block = min(width, 1024)
    return pl.pallas_call(
        functools.partial(select_kernel, rows),
        grid=(width // block,),
        in_specs=[SMEM, pl.BlockSpec((rows * tiles, block), lambda c: (0, c))],
        out_specs=[pl.BlockSpec((rows, block), lambda c: (0, c))] * wide,
        out_shape=[jax.ShapeDtypeStruct((rows, width), amplitudes.dtype)] * wide,
        scratch_shapes=[pltpu.VMEM((wide * rows, rows * tiles), amplitudes.dtype)],
        compiler_params=pltpu.CompilerParams(vmem_limit_bytes=KERNEL_VMEM),
        cost_estimate=pl.CostEstimate(
            flops=2 * wide * rows * rows * tiles * width,
            bytes_accessed=4 * rows * tiles * width,
            transcendentals=0,
        ),
        name="select_tiles",
    )(owner, amplitudes.reshape(rows * tiles, width))


def contract_kernel(count, owner_ref, counts_ref, *rest):
    parts, integ_ref = rest[:count], rest[count]
    outs, rows_ref, sems = rest[count + 1 : -2], rest[-2], rest[-1]
    rows = parts[0].shape[0]
    copies = [
        pltpu.make_async_copy(part, rows_ref.at[pl.ds(n * rows, rows)], sems.at[n])
        for n, part in enumerate(parts)
    ]

    @pl.when((pl.program_id(0) == 0) & (pl.program_id(1) == 0))
    def _():
        for copy in copies:
            copy.start()
        for copy in copies:
            copy.wait()

    live = pl.program_id(0) < counts_ref[find_tile(owner_ref, lax.axis_index("wide"))]

    @pl.when(live)
    def _():
        value = lax.dot_general(
            rows_ref[...],
            integ_ref[0],
            (((1,), (1,)), ((), ())),
            preferred_element_type=jnp.float32,
        ).astype(jnp.bfloat16)
        each = outs[0].shape[0]
        for m, out in enumerate(outs):
            out[...] = value[m * each : (m + 1) * each]

    @pl.when(jnp.logical_not(live))
    def _():
        for out in outs:
            out[...] = jnp.zeros_like(out)


def contract(parts, integrals, owner, counts, outs):
    rows, width = parts[0].shape
    partners, ab, _ = integrals.shape
    block = min(ab, 256)
    steps = ab // block
    count = len(parts)
    each = count * rows // outs
    return pl.pallas_call(
        functools.partial(contract_kernel, count),
        grid=(partners, steps),
        in_specs=[SMEM, SMEM]
        + [pl.BlockSpec(memory_space=pl.ANY)] * count
        + [pl.BlockSpec((1, block, width), lambda k, c: (k, c, 0))],
        out_specs=[pl.BlockSpec((each, block), lambda k, c: (0, k * steps + c))] * outs,
        out_shape=[jax.ShapeDtypeStruct((each, partners * ab), jnp.bfloat16)] * outs,
        scratch_shapes=[
            pltpu.VMEM((count * rows, width), parts[0].dtype),
            pltpu.SemaphoreType.DMA((count,)),
        ],
        compiler_params=pltpu.CompilerParams(vmem_limit_bytes=KERNEL_VMEM),
        cost_estimate=pl.CostEstimate(
            flops=2 * count * rows * width * partners * ab,
            bytes_accessed=2 * (partners * ab * width + count * rows * (width + partners * ab)),
            transcendentals=0,
        ),
        name="contract_rows",
    )(owner, counts, *parts, integrals)


def collect_kernel(partners, owner_ref, targets_ref, counts_ref, *rest):
    wide = owner_ref.shape[0]
    parts, outs, sum_ref = rest[:wide], rest[wide:-1], rest[-1]
    me = lax.axis_index("wide")
    ab = parts[0].shape[1] // partners
    sum_ref[...] = jnp.zeros_like(sum_ref)
    for m, part in enumerate(parts):
        tile = find_tile(owner_ref, lax.bitwise_xor(me, m))
        live = counts_ref[tile]
        for k in range(partners):
            target = targets_ref[tile, k]

            @pl.when(k < live)
            def _():
                sum_ref[target] += part[:, k * ab : (k + 1) * ab].astype(jnp.float32)

    rows = outs[0].shape[1]
    for n, out in enumerate(outs):
        out[...] = sum_ref[:, n * rows : (n + 1) * rows, :].astype(out.dtype)


def collect(parts, owner, targets, counts, tiles_out, blk):
    rows, columns = parts[0].shape
    partners = targets.shape[1]
    ab = columns // partners
    return pl.pallas_call(
        functools.partial(collect_kernel, partners),
        in_specs=[SMEM, SMEM, SMEM] + [pl.BlockSpec(memory_space=pltpu.VMEM)] * len(parts),
        out_specs=[pl.BlockSpec(memory_space=pltpu.VMEM)] * blk,
        out_shape=[jax.ShapeDtypeStruct((tiles_out, rows // blk, ab), jnp.bfloat16)] * blk,
        scratch_shapes=[pltpu.VMEM((tiles_out, rows, ab), jnp.float32)],
        compiler_params=pltpu.CompilerParams(vmem_limit_bytes=KERNEL_VMEM),
        name="collect_targets",
    )(owner, targets, counts, *parts)


def place_kernel(*refs):
    parts, out_ref = refs[:-1], refs[-1]
    mine = lax.axis_index("blk")
    ab = parts[0].shape[2]
    for n, part in enumerate(parts):
        begin = pl.multiple_of(lax.bitwise_xor(mine, n) * ab, 128)
        out_ref[:, :, pl.ds(begin, ab)] = part[...]


def place(parts):
    tiles_out, rows, ab = parts[0].shape
    block = min(tiles_out, 2)
    return pl.pallas_call(
        place_kernel,
        grid=(tiles_out // block,),
        in_specs=[pl.BlockSpec((block, rows, ab), lambda p: (p, 0, 0))] * len(parts),
        out_specs=pl.BlockSpec((block, rows, len(parts) * ab), lambda p: (p, 0, 0)),
        out_shape=jax.ShapeDtypeStruct((tiles_out, rows, len(parts) * ab), parts[0].dtype),
        compiler_params=pltpu.CompilerParams(vmem_limit_bytes=KERNEL_VMEM),
        name="place_columns",
    )(*parts)


def after(value, earlier):
    return lax.optimization_barrier((value, *earlier))[0] if earlier else value


def body(amplitudes, integrals, owner, targets, counts):
    wide, blk = lax.axis_size("wide"), lax.axis_size("blk")
    i, j, tiles, width = amplitudes.shape

    def swap(value, axis, mask, earlier=()):
        pairs = [(s, s ^ mask) for s in range(lax.axis_size(axis))]
        return lax.ppermute(after(value, earlier), axis, pairs)

    sent = select(amplitudes, owner, wide)
    got = {(0, 0): sent[0]}

    def wide_step(m, *earlier):
        got[m, 0] = swap(sent[m], "wide", m, [got[e] for e in earlier])

    def chip_step(m, *earlier):
        got[m, 2] = swap(got[m, 0], "blk", 2, [got[e] for e in earlier])

    def core_step(m):
        for n in (0, 2):
            got[m, n + 1] = swap(got[m, n], "blk", 1)

    returned = [None] * wide

    def product(*masks):
        parts = [got[m, n] for m in masks for n in range(blk)]
        for m, made in zip(masks, contract(parts, integrals[0], owner, counts, len(masks))):
            returned[m] = made if m == 0 else swap(made, "wide", m)

    wide_step(1)
    wide_step(2)
    wide_step(6)
    chip_step(0)
    wide_step(4, (1, 0))
    wide_step(5, (2, 0))
    chip_step(1, (0, 2))
    chip_step(2, (0, 2))
    core_step(0)
    wide_step(3, (4, 0), (1, 2))
    wide_step(7, (4, 0), (1, 2))
    chip_step(6, (1, 2))
    core_step(1)
    product(0, 1)
    chip_step(4, (2, 2))
    chip_step(5, (6, 2))
    core_step(2)
    core_step(6)
    product(2, 6)
    chip_step(3, (4, 2))
    chip_step(7, (5, 2))
    core_step(4)
    core_step(5)
    product(4, 5)
    core_step(3)
    core_step(7)
    product(3, 7)

    sums = collect(returned, owner, targets, counts, wide, blk)
    sums = [sums[0]] + [swap(sums[n], "blk", n) for n in range(1, blk)]
    return place(sums).reshape(wide, i, j, -1)


def body_large(amplitudes, integrals, owner, targets, counts):
    wide_count = lax.axis_size("wide")
    my_index = lax.axis_index("wide")
    tile_ids = jnp.arange(owner.shape[0], dtype=jnp.int32)
    holder = jnp.sum(jnp.where(owner[None, :] == tile_ids[:, None], tile_ids[None, :], 0), axis=1)
    ordered = jnp.take(amplitudes, holder, axis=2)
    my_tile = lax.all_to_all(ordered, "wide", split_axis=2, concat_axis=1, tiled=True)
    my_holder = lax.dynamic_index_in_dim(holder, my_index, 0, keepdims=False)
    my_count = lax.dynamic_index_in_dim(counts, my_holder, 0, keepdims=False)
    slot_ids = jnp.arange(targets.shape[1], dtype=jnp.int32)
    live_slots = (slot_ids < my_count).astype(jnp.float32)
    my_integrals = integrals[0]
    width = my_tile.shape[3]
    portion = lax.all_gather(my_tile, "blk", axis=0, tiled=True)
    flat_rows = portion.reshape(-1, width)
    result = jnp.einsum("rc,kac->rka", flat_rows, my_integrals, preferred_element_type=jnp.float32)
    partial_value = result.reshape(
        portion.shape[0], portion.shape[1], my_integrals.shape[0], my_integrals.shape[1]
    )
    shaped = (partial_value * live_slots[None, None, :, None]).astype(jnp.bfloat16)
    received = lax.all_to_all(
        lax.all_to_all(shaped, "wide", split_axis=1, concat_axis=2, tiled=True),
        "blk",
        split_axis=0,
        concat_axis=3,
        tiled=True,
    )
    slot_targets = jnp.take(targets, holder, axis=0).reshape(-1)
    window_ids = jnp.arange(wide_count, dtype=jnp.int32)
    selector = (slot_targets[None, :] == window_ids[:, None]).astype(jnp.bfloat16)
    ladder = jnp.einsum("ps,ijsa->pija", selector, received, preferred_element_type=jnp.float32)
    return ladder.astype(jnp.bfloat16)


def solution(mesh):
    few = mesh.shape["wide"] == 8 and mesh.shape["blk"] == 4
    placed = (P("blk", "wide", None, None), P("wide", None, "blk", None), P(), P(), P())
    return jax.shard_map(
        body if few else body_large,
        mesh=mesh,
        in_specs=placed,
        out_specs=P(None, "blk", "wide", None),
        check_vma=False,
    )
```

```python
import functools

import jax
import jax.numpy as jnp
from jax import lax
from jax.experimental import pallas as pl
from jax.experimental.pallas import tpu as pltpu
from jax.sharding import PartitionSpec as P

MIB = 1 << 20
KERNEL_VMEM = 16 * MIB
SMEM = pl.BlockSpec(memory_space=pltpu.SMEM)


def find_tile(owner_ref, slot):
    def step(q, found):
        return jnp.where(owner_ref[q] == slot, q, found)

    return lax.fori_loop(0, owner_ref.shape[0], step, jnp.int32(0))


def select_kernel(rows, owner_ref, amp_ref, *rest):
    outs, pick_ref = rest[:-1], rest[-1]
    tiles = owner_ref.shape[0]

    @pl.when(pl.program_id(0) == 0)
    def _():
        me = lax.axis_index("wide")
        shape = pick_ref.shape
        out_row = lax.broadcasted_iota(jnp.int32, shape, 0)
        in_row = lax.broadcasted_iota(jnp.int32, shape, 1)
        slot = lax.bitwise_xor(out_row // rows, me)
        tile = in_row % tiles
        place = jnp.zeros(shape, jnp.int32)
        for q in range(tiles):
            place = jnp.where(tile == q, owner_ref[q], place)
        chosen = (place == slot) & (out_row % rows == in_row // tiles)
        pick_ref[...] = jnp.where(chosen, 1.0, 0.0).astype(pick_ref.dtype)

    moved = jnp.dot(pick_ref[...], amp_ref[...], preferred_element_type=jnp.float32)
    moved = moved.astype(amp_ref.dtype)
    for m, out in enumerate(outs):
        out[...] = moved[m * rows : (m + 1) * rows, :]


def select(amplitudes, owner, wide):
    i, j, tiles, width = amplitudes.shape
    rows = i * j
    block = min(width, 1024)
    return pl.pallas_call(
        functools.partial(select_kernel, rows),
        grid=(width // block,),
        in_specs=[SMEM, pl.BlockSpec((rows * tiles, block), lambda c: (0, c))],
        out_specs=[pl.BlockSpec((rows, block), lambda c: (0, c))] * wide,
        out_shape=[jax.ShapeDtypeStruct((rows, width), amplitudes.dtype)] * wide,
        scratch_shapes=[pltpu.VMEM((wide * rows, rows * tiles), amplitudes.dtype)],
        compiler_params=pltpu.CompilerParams(vmem_limit_bytes=KERNEL_VMEM),
        cost_estimate=pl.CostEstimate(
            flops=2 * wide * rows * rows * tiles * width,
            bytes_accessed=4 * rows * tiles * width,
            transcendentals=0,
        ),
        name="select_tiles",
    )(owner, amplitudes.reshape(rows * tiles, width))


def contract_kernel(count, owner_ref, counts_ref, *rest):
    parts, own_ref, other_ref = rest[:count], rest[count], rest[count + 1]
    outs, rows_ref, sems = rest[count + 2 : -2], rest[-2], rest[-1]
    rows = parts[0].shape[0]
    partner, source, block = (pl.program_id(axis) for axis in range(3))
    copies = [
        pltpu.make_async_copy(part, rows_ref.at[pl.ds(n * rows, rows)], sems.at[n])
        for n, part in enumerate(parts)
    ]

    @pl.when((partner == 0) & (source == 0) & (block == 0))
    def _():
        for copy in copies:
            copy.start()
        for copy in copies:
            copy.wait()

    live = partner < counts_ref[find_tile(owner_ref, lax.axis_index("wide"))]

    def multiply(integ_ref):
        value = lax.dot_general(
            rows_ref[...],
            integ_ref[0],
            (((1,), (1,)), ((), ())),
            preferred_element_type=jnp.float32,
        ).astype(jnp.bfloat16)
        each = outs[0].shape[0]
        for m, out in enumerate(outs):
            out[...] = value[m * each : (m + 1) * each]

    @pl.when(live & (source == 0))
    def _():
        multiply(own_ref)

    @pl.when(live & (source == 1))
    def _():
        multiply(other_ref)

    @pl.when(jnp.logical_not(live))
    def _():
        for out in outs:
            out[...] = jnp.zeros_like(out)


def contract(parts, own, other, owner, counts, outs):
    rows, width = parts[0].shape
    partners, ab, _ = own.shape
    block = min(ab, 256)
    steps = ab // block
    count = len(parts)
    each = count * rows // outs
    return pl.pallas_call(
        functools.partial(contract_kernel, count),
        grid=(partners, 2, steps),
        in_specs=[SMEM, SMEM]
        + [pl.BlockSpec(memory_space=pl.ANY)] * count
        + [
            pl.BlockSpec((1, block, width), lambda k, s, c: (k, jnp.where(s == 0, c, steps - 1), 0)),
            pl.BlockSpec((1, block, width), lambda k, s, c: (k, jnp.where(s == 0, 0, c), 0)),
        ],
        out_specs=[
            pl.BlockSpec((each, block), lambda k, s, c: (0, (k * 2 + s) * steps + c)),
        ]
        * outs,
        out_shape=[jax.ShapeDtypeStruct((each, partners * 2 * ab), jnp.bfloat16)] * outs,
        scratch_shapes=[
            pltpu.VMEM((count * rows, width), parts[0].dtype),
            pltpu.SemaphoreType.DMA((count,)),
        ],
        compiler_params=pltpu.CompilerParams(vmem_limit_bytes=KERNEL_VMEM),
        cost_estimate=pl.CostEstimate(
            flops=4 * count * rows * width * partners * ab,
            bytes_accessed=4 * partners * ab * width,
            transcendentals=0,
        ),
        name="contract_rows",
    )(owner, counts, *parts, own, other)


def collect_kernel(partners, owner_ref, targets_ref, counts_ref, *rest):
    wide = owner_ref.shape[0]
    parts, outs, sum_ref = rest[:wide], rest[wide:-1], rest[-1]
    me = lax.axis_index("wide")
    ab = parts[0].shape[1] // partners
    sum_ref[...] = jnp.zeros_like(sum_ref)
    for m, part in enumerate(parts):
        tile = find_tile(owner_ref, lax.bitwise_xor(me, m))
        live = counts_ref[tile]
        for k in range(partners):
            target = targets_ref[tile, k]

            @pl.when(k < live)
            def _():
                sum_ref[target] += part[:, k * ab : (k + 1) * ab].astype(jnp.float32)

    rows = outs[0].shape[1]
    for n, out in enumerate(outs):
        out[...] = sum_ref[:, n * rows : (n + 1) * rows, :].astype(out.dtype)


def collect(parts, owner, targets, counts, tiles_out):
    rows, columns = parts[0].shape
    partners = targets.shape[1]
    ab = columns // partners
    return pl.pallas_call(
        functools.partial(collect_kernel, partners),
        in_specs=[SMEM, SMEM, SMEM] + [pl.BlockSpec(memory_space=pltpu.VMEM)] * len(parts),
        out_specs=[pl.BlockSpec(memory_space=pltpu.VMEM)] * 2,
        out_shape=[jax.ShapeDtypeStruct((tiles_out, rows // 2, ab), jnp.bfloat16)] * 2,
        scratch_shapes=[pltpu.VMEM((tiles_out, rows, ab), jnp.float32)],
        compiler_params=pltpu.CompilerParams(vmem_limit_bytes=KERNEL_VMEM),
        name="collect_targets",
    )(owner, targets, counts, *parts)


def place_kernel(*refs):
    parts, out_ref = refs[:-1], refs[-1]
    mine = lax.axis_index("blk")
    ab = parts[0].shape[2] // 2
    for chip, part in enumerate(parts):
        for core in range(2):
            begin = pl.multiple_of(lax.bitwise_xor(mine, chip * 2 + core) * ab, 128)
            out_ref[:, :, pl.ds(begin, ab)] = part[:, :, core * ab : (core + 1) * ab]


def place(parts):
    tiles_out, rows, columns = parts[0].shape
    block = min(tiles_out, 2)
    return pl.pallas_call(
        place_kernel,
        grid=(tiles_out // block,),
        in_specs=[pl.BlockSpec((block, rows, columns), lambda p: (p, 0, 0))] * len(parts),
        out_specs=pl.BlockSpec((block, rows, len(parts) * columns), lambda p: (p, 0, 0)),
        out_shape=jax.ShapeDtypeStruct((tiles_out, rows, len(parts) * columns), parts[0].dtype),
        compiler_params=pltpu.CompilerParams(vmem_limit_bytes=KERNEL_VMEM),
        name="place_columns",
    )(*parts)


def after(value, earlier):
    return lax.optimization_barrier((value, *earlier))[0] if earlier else value


def body(amplitudes, integrals, owner, targets, counts):
    wide = lax.axis_size("wide")
    i, j, tiles, width = amplitudes.shape

    def swap(value, axis, mask, earlier=()):
        pairs = [(s, s ^ mask) for s in range(lax.axis_size(axis))]
        return lax.ppermute(after(value, earlier), axis, pairs)

    own = integrals[0]
    other = swap(own, "blk", 1)
    sent = select(amplitudes, owner, wide)
    got = {(0, 0): sent[0]}

    def wide_step(m, *earlier):
        got[m, 0] = swap(sent[m], "wide", m, [got[e] for e in earlier])

    def chip_step(m, *earlier):
        got[m, 1] = swap(got[m, 0], "blk", 2, [got[e] for e in earlier])

    returned = [None] * wide

    def product(*masks, earlier=()):
        parts = [got[m, n] for m in masks for n in range(2)]
        first = after(owner, [got[m, 2] for m in earlier])
        made = contract(parts, own, other, first, counts, len(masks))
        for m, value in zip(masks, made):
            returned[m] = value if m == 0 else swap(value, "wide", m)
            got[m, 2] = value

    chip_step(0)
    wide_step(2)
    wide_step(1)
    chip_step(2)
    wide_step(6, (2, 0))
    chip_step(1)
    wide_step(4, (0, 1), (1, 0))
    chip_step(6)
    wide_step(3, (6, 0), (2, 1))
    wide_step(5, (1, 1))
    wide_step(7, (6, 1))
    chip_step(4)
    product(0, 2, 1, 6)
    chip_step(5)
    chip_step(3, (0, 2))
    product(4, 5, earlier=(0,))
    chip_step(7, (0, 2))
    product(3, 7, earlier=(4,))

    sums = collect(returned, owner, targets, counts, wide)
    return place([sums[0], swap(sums[1], "blk", 2)]).reshape(wide, i, j, -1)


def body_large(amplitudes, integrals, owner, targets, counts):
    wide_count = lax.axis_size("wide")
    my_index = lax.axis_index("wide")
    tile_ids = jnp.arange(owner.shape[0], dtype=jnp.int32)
    holder = jnp.sum(jnp.where(owner[None, :] == tile_ids[:, None], tile_ids[None, :], 0), axis=1)
    ordered = jnp.take(amplitudes, holder, axis=2)
    my_tile = lax.all_to_all(ordered, "wide", split_axis=2, concat_axis=1, tiled=True)
    my_holder = lax.dynamic_index_in_dim(holder, my_index, 0, keepdims=False)
    my_count = lax.dynamic_index_in_dim(counts, my_holder, 0, keepdims=False)
    slot_ids = jnp.arange(targets.shape[1], dtype=jnp.int32)
    live_slots = (slot_ids < my_count).astype(jnp.float32)
    my_integrals = integrals[0]
    width = my_tile.shape[3]
    portion = lax.all_gather(my_tile, "blk", axis=0, tiled=True)
    flat_rows = portion.reshape(-1, width)
    result = jnp.einsum("rc,kac->rka", flat_rows, my_integrals, preferred_element_type=jnp.float32)
    partial_value = result.reshape(
        portion.shape[0], portion.shape[1], my_integrals.shape[0], my_integrals.shape[1]
    )
    shaped = (partial_value * live_slots[None, None, :, None]).astype(jnp.bfloat16)
    received = lax.all_to_all(
        lax.all_to_all(shaped, "wide", split_axis=1, concat_axis=2, tiled=True),
        "blk",
        split_axis=0,
        concat_axis=3,
        tiled=True,
    )
    slot_targets = jnp.take(targets, holder, axis=0).reshape(-1)
    window_ids = jnp.arange(wide_count, dtype=jnp.int32)
    selector = (slot_targets[None, :] == window_ids[:, None]).astype(jnp.bfloat16)
    ladder = jnp.einsum("ps,ijsa->pija", selector, received, preferred_element_type=jnp.float32)
    return ladder.astype(jnp.bfloat16)


def solution(mesh):
    few = mesh.shape["wide"] == 8 and mesh.shape["blk"] == 4
    placed = (P("blk", "wide", None, None), P("wide", None, "blk", None), P(), P(), P())
    return jax.shard_map(
        body if few else body_large,
        mesh=mesh,
        in_specs=placed,
        out_specs=P(None, "blk", "wide", None),
        check_vma=False,
    )
```

```python
import functools

import jax
import jax.numpy as jnp
from jax import lax
from jax.experimental import pallas as pl
from jax.experimental.pallas import tpu as pltpu
from jax.sharding import PartitionSpec as P

MIB = 1 << 20
KERNEL_VMEM = 16 * MIB
SMEM = pl.BlockSpec(memory_space=pltpu.SMEM)


def find_tile(owner_ref, slot):
    def step(q, found):
        return jnp.where(owner_ref[q] == slot, q, found)

    return lax.fori_loop(0, owner_ref.shape[0], step, jnp.int32(0))


def select_kernel(rows, groups, owner_ref, amp_ref, *rest):
    outs, pick_ref = rest[:-1], rest[-1]
    tiles = owner_ref.shape[0]

    @pl.when(pl.program_id(0) == 0)
    def _():
        me = lax.axis_index("wide")
        shape = pick_ref.shape
        out_row = lax.broadcasted_iota(jnp.int32, shape, 0)
        in_row = lax.broadcasted_iota(jnp.int32, shape, 1)
        slot = lax.bitwise_xor(out_row // rows, me)
        tile = in_row % tiles
        place = jnp.zeros(shape, jnp.int32)
        for q in range(tiles):
            place = jnp.where(tile == q, owner_ref[q], place)
        chosen = (place == slot) & (out_row % rows == in_row // tiles)
        pick_ref[...] = jnp.where(chosen, 1.0, 0.0).astype(pick_ref.dtype)

    moved = jnp.dot(pick_ref[...], amp_ref[...], preferred_element_type=jnp.float32)
    moved = moved.astype(amp_ref.dtype)
    for group, out in zip(groups, outs):
        for at, m in enumerate(group):
            out[at * rows : (at + 1) * rows] = moved[m * rows : (m + 1) * rows]


def select(amplitudes, owner, groups):
    i, j, tiles, width = amplitudes.shape
    rows = i * j
    wide = sum(map(len, groups))
    block = min(width, 1024)
    return pl.pallas_call(
        functools.partial(select_kernel, rows, groups),
        grid=(width // block,),
        in_specs=[SMEM, pl.BlockSpec((rows * tiles, block), lambda c: (0, c))],
        out_specs=[pl.BlockSpec((len(g) * rows, block), lambda c: (0, c)) for g in groups],
        out_shape=[jax.ShapeDtypeStruct((len(g) * rows, width), amplitudes.dtype) for g in groups],
        scratch_shapes=[pltpu.VMEM((wide * rows, rows * tiles), amplitudes.dtype)],
        compiler_params=pltpu.CompilerParams(vmem_limit_bytes=KERNEL_VMEM),
        cost_estimate=pl.CostEstimate(
            flops=2 * wide * rows * rows * tiles * width,
            bytes_accessed=4 * rows * tiles * width,
            transcendentals=0,
        ),
        name="select_tiles",
    )(owner, amplitudes.reshape(rows * tiles, width))


def contract_kernel(count, owner_ref, counts_ref, *rest):
    parts, own_ref, other_ref = rest[:count], rest[count], rest[count + 1]
    outs, rows_ref, sems = rest[count + 2 : -2], rest[-2], rest[-1]
    rows = rows_ref.shape[0] // count
    partner, source, block = (pl.program_id(axis) for axis in range(3))
    copies = [
        pltpu.make_async_copy(part.at[pl.ds(0, rows)], rows_ref.at[pl.ds(n * rows, rows)], sems.at[n])
        for n, part in enumerate(parts)
    ]

    @pl.when((partner == 0) & (source == 0) & (block == 0))
    def _():
        for copy in copies:
            copy.start()
        for copy in copies:
            copy.wait()

    live = partner < counts_ref[find_tile(owner_ref, lax.axis_index("wide"))]

    def multiply(integ_ref):
        value = lax.dot_general(
            rows_ref[...],
            integ_ref[0],
            (((1,), (1,)), ((), ())),
            preferred_element_type=jnp.float32,
        ).astype(jnp.bfloat16)
        each = outs[0].shape[0]
        for m, out in enumerate(outs):
            out[...] = value[m * each : (m + 1) * each]

    @pl.when(live & (source == 0))
    def _():
        multiply(own_ref)

    @pl.when(live & (source == 1))
    def _():
        multiply(other_ref)

    @pl.when(jnp.logical_not(live))
    def _():
        for out in outs:
            out[...] = jnp.zeros_like(out)


def contract(parts, rows, own, other, owner, counts, outs):
    width = parts[0].shape[1]
    partners, ab, _ = own.shape
    block = min(ab, 256)
    steps = ab // block
    count = len(parts)
    each = count * rows // outs
    return pl.pallas_call(
        functools.partial(contract_kernel, count),
        grid=(partners, 2, steps),
        in_specs=[SMEM, SMEM]
        + [pl.BlockSpec(memory_space=pl.ANY)] * count
        + [
            pl.BlockSpec((1, block, width), lambda k, s, c: (k, jnp.where(s == 0, c, steps - 1), 0)),
            pl.BlockSpec((1, block, width), lambda k, s, c: (k, jnp.where(s == 0, 0, c), 0)),
        ],
        out_specs=[
            pl.BlockSpec((each, block), lambda k, s, c: (0, (k * 2 + s) * steps + c)),
        ]
        * outs,
        out_shape=[jax.ShapeDtypeStruct((each, partners * 2 * ab), jnp.bfloat16)] * outs,
        scratch_shapes=[
            pltpu.VMEM((count * rows, width), parts[0].dtype),
            pltpu.SemaphoreType.DMA((count,)),
        ],
        compiler_params=pltpu.CompilerParams(vmem_limit_bytes=KERNEL_VMEM),
        cost_estimate=pl.CostEstimate(
            flops=4 * count * rows * width * partners * ab,
            bytes_accessed=4 * partners * ab * width,
            transcendentals=0,
        ),
        name="contract_rows",
    )(owner, counts, *parts, own, other)


def collect_kernel(partners, owner_ref, targets_ref, counts_ref, *rest):
    wide = owner_ref.shape[0]
    parts, outs, sum_ref = rest[:wide], rest[wide:-1], rest[-1]
    me = lax.axis_index("wide")
    ab = parts[0].shape[1] // partners
    sum_ref[...] = jnp.zeros_like(sum_ref)
    for m, part in enumerate(parts):
        tile = find_tile(owner_ref, lax.bitwise_xor(me, m))
        live = counts_ref[tile]
        for k in range(partners):
            target = targets_ref[tile, k]

            @pl.when(k < live)
            def _():
                sum_ref[target] += part[:, k * ab : (k + 1) * ab].astype(jnp.float32)

    rows = outs[0].shape[1]
    for n, out in enumerate(outs):
        out[...] = sum_ref[:, n * rows : (n + 1) * rows, :].astype(out.dtype)


def collect(parts, owner, targets, counts, tiles_out):
    rows, columns = parts[0].shape
    partners = targets.shape[1]
    ab = columns // partners
    return pl.pallas_call(
        functools.partial(collect_kernel, partners),
        in_specs=[SMEM, SMEM, SMEM] + [pl.BlockSpec(memory_space=pltpu.VMEM)] * len(parts),
        out_specs=[pl.BlockSpec(memory_space=pltpu.VMEM)] * 2,
        out_shape=[jax.ShapeDtypeStruct((tiles_out, rows // 2, ab), jnp.bfloat16)] * 2,
        scratch_shapes=[pltpu.VMEM((tiles_out, rows, ab), jnp.float32)],
        compiler_params=pltpu.CompilerParams(vmem_limit_bytes=KERNEL_VMEM),
        name="collect_targets",
    )(owner, targets, counts, *parts)


def place_kernel(*refs):
    parts, out_ref = refs[:-1], refs[-1]
    mine = lax.axis_index("blk")
    ab = parts[0].shape[2] // 2
    for chip, part in enumerate(parts):
        for core in range(2):
            begin = pl.multiple_of(lax.bitwise_xor(mine, chip * 2 + core) * ab, 128)
            out_ref[:, :, pl.ds(begin, ab)] = part[:, :, core * ab : (core + 1) * ab]


def place(parts):
    tiles_out, rows, columns = parts[0].shape
    block = min(tiles_out, 2)
    return pl.pallas_call(
        place_kernel,
        grid=(tiles_out // block,),
        in_specs=[pl.BlockSpec((block, rows, columns), lambda p: (p, 0, 0))] * len(parts),
        out_specs=pl.BlockSpec((block, rows, len(parts) * columns), lambda p: (p, 0, 0)),
        out_shape=jax.ShapeDtypeStruct((tiles_out, rows, len(parts) * columns), parts[0].dtype),
        compiler_params=pltpu.CompilerParams(vmem_limit_bytes=KERNEL_VMEM),
        name="place_columns",
    )(*parts)


def after(value, earlier):
    return lax.optimization_barrier((value, *earlier))[0] if earlier else value


def body(amplitudes, integrals, owner, targets, counts):
    wide = lax.axis_size("wide")
    i, j, tiles, width = amplitudes.shape
    rows = i * j

    def swap(value, axis, mask, earlier=()):
        pairs = [(s, s ^ mask) for s in range(lax.axis_size(axis))]
        return lax.ppermute(after(value, earlier), axis, pairs)

    own = integrals[0]
    done = {}
    past = []

    def run(**steps):
        now = {name: swap(value, axis, mask, past) for name, (value, axis, mask) in steps.items()}
        done.update(now)
        past[:] = now.values()

    def chip(m):
        return done[f"to{m}"], "blk", 2

    def product(*masks):
        parts = [done[f"{at}{m}"] for m in masks for at in ("to", "chip")]
        out = contract(parts, rows, own, done["other"], owner, counts, len(masks))
        done.update(zip([f"made{m}" for m in masks], out))

    groups = tuple((m,) for m in range(wide))
    sent = select(amplitudes, owner, groups)
    done["to0"] = sent[0]
    run(
        chip0=(sent[0], "blk", 2),
        to2=(sent[2], "wide", 2),
        to6=(sent[6], "wide", 6),
        to1=(sent[1], "wide", 1),
    )
    done["other"] = swap(own, "blk", 1, past)
    run(
        chip2=chip(2),
        chip6=chip(6),
        via2=(sent[4], "wide", 2),
        via7=(sent[5], "wide", 7),
        to7=(sent[7], "wide", 7),
    )
    run(
        chip1=chip(1),
        chip7=chip(7),
        to4=(done["via2"], "wide", 6),
        to5=(done["via7"], "wide", 2),
    )
    product(0, 1, 2, 6)
    run(chip4=chip(4), chip5=chip(5), to3=(sent[3], "wide", 3))
    product(4, 5, 7)
    run(
        chip3=chip(3),
        back1=(done["made1"], "wide", 1),
        back2=(done["made2"], "wide", 2),
        back6=(done["made6"], "wide", 6),
    )
    product(3)
    run(
        half2=(done["made4"], "wide", 2),
        half7=(done["made5"], "wide", 7),
        back7=(done["made7"], "wide", 7),
    )
    run(
        back4=(done["half2"], "wide", 6),
        back5=(done["half7"], "wide", 2),
        back3=(done["made3"], "wide", 3),
    )

    sums = collect([done["made0"]] + [done[f"back{m}"] for m in range(1, wide)], owner, targets, counts, wide)
    return place([sums[0], swap(sums[1], "blk", 2)]).reshape(wide, i, j, -1)


def body_large(amplitudes, integrals, owner, targets, counts):
    wide_count = lax.axis_size("wide")
    my_index = lax.axis_index("wide")
    tile_ids = jnp.arange(owner.shape[0], dtype=jnp.int32)
    holder = jnp.sum(jnp.where(owner[None, :] == tile_ids[:, None], tile_ids[None, :], 0), axis=1)
    ordered = jnp.take(amplitudes, holder, axis=2)
    my_tile = lax.all_to_all(ordered, "wide", split_axis=2, concat_axis=1, tiled=True)
    my_holder = lax.dynamic_index_in_dim(holder, my_index, 0, keepdims=False)
    my_count = lax.dynamic_index_in_dim(counts, my_holder, 0, keepdims=False)
    slot_ids = jnp.arange(targets.shape[1], dtype=jnp.int32)
    live_slots = (slot_ids < my_count).astype(jnp.float32)
    my_integrals = integrals[0]
    width = my_tile.shape[3]
    portion = lax.all_gather(my_tile, "blk", axis=0, tiled=True)
    flat_rows = portion.reshape(-1, width)
    result = jnp.einsum("rc,kac->rka", flat_rows, my_integrals, preferred_element_type=jnp.float32)
    partial_value = result.reshape(
        portion.shape[0], portion.shape[1], my_integrals.shape[0], my_integrals.shape[1]
    )
    shaped = (partial_value * live_slots[None, None, :, None]).astype(jnp.bfloat16)
    received = lax.all_to_all(
        lax.all_to_all(shaped, "wide", split_axis=1, concat_axis=2, tiled=True),
        "blk",
        split_axis=0,
        concat_axis=3,
        tiled=True,
    )
    slot_targets = jnp.take(targets, holder, axis=0).reshape(-1)
    window_ids = jnp.arange(wide_count, dtype=jnp.int32)
    selector = (slot_targets[None, :] == window_ids[:, None]).astype(jnp.bfloat16)
    ladder = jnp.einsum("ps,ijsa->pija", selector, received, preferred_element_type=jnp.float32)
    return ladder.astype(jnp.bfloat16)


def solution(mesh):
    few = mesh.shape["wide"] == 8 and mesh.shape["blk"] == 4
    placed = (P("blk", "wide", None, None), P("wide", None, "blk", None), P(), P(), P())
    return jax.shard_map(
        body if few else body_large,
        mesh=mesh,
        in_specs=placed,
        out_specs=P(None, "blk", "wide", None),
        check_vma=False,
    )
```

```python
import functools

import jax
import jax.numpy as jnp
from jax import lax
from jax.experimental import pallas as pl
from jax.experimental.pallas import tpu as pltpu
from jax.sharding import PartitionSpec as P

MIB = 1 << 20
KERNEL_VMEM = 16 * MIB
CONTRACT_VMEM = 40 * MIB
SMEM = pl.BlockSpec(memory_space=pltpu.SMEM)


def find_tile(owner_ref, slot):
    def step(q, found):
        return jnp.where(owner_ref[q] == slot, q, found)

    return lax.fori_loop(0, owner_ref.shape[0], step, jnp.int32(0))


def select_kernel(rows, groups, owner_ref, amp_ref, *rest):
    outs, pick_ref = rest[:-1], rest[-1]
    tiles = owner_ref.shape[0]

    @pl.when(pl.program_id(0) == 0)
    def _():
        me = lax.axis_index("wide")
        shape = pick_ref.shape
        out_row = lax.broadcasted_iota(jnp.int32, shape, 0)
        in_row = lax.broadcasted_iota(jnp.int32, shape, 1)
        slot = lax.bitwise_xor(out_row // rows, me)
        tile = in_row % tiles
        place = jnp.zeros(shape, jnp.int32)
        for q in range(tiles):
            place = jnp.where(tile == q, owner_ref[q], place)
        chosen = (place == slot) & (out_row % rows == in_row // tiles)
        pick_ref[...] = jnp.where(chosen, 1.0, 0.0).astype(pick_ref.dtype)

    moved = jnp.dot(pick_ref[...], amp_ref[...], preferred_element_type=jnp.float32)
    moved = moved.astype(amp_ref.dtype)
    for group, out in zip(groups, outs):
        for at, m in enumerate(group):
            out[at * rows : (at + 1) * rows] = moved[m * rows : (m + 1) * rows]


def select(amplitudes, owner, groups):
    i, j, tiles, width = amplitudes.shape
    rows = i * j
    wide = sum(map(len, groups))
    block = min(width, 1024)
    return pl.pallas_call(
        functools.partial(select_kernel, rows, groups),
        grid=(width // block,),
        in_specs=[SMEM, pl.BlockSpec((rows * tiles, block), lambda c: (0, c))],
        out_specs=[pl.BlockSpec((len(g) * rows, block), lambda c: (0, c)) for g in groups],
        out_shape=[jax.ShapeDtypeStruct((len(g) * rows, width), amplitudes.dtype) for g in groups],
        scratch_shapes=[pltpu.VMEM((wide * rows, rows * tiles), amplitudes.dtype)],
        compiler_params=pltpu.CompilerParams(vmem_limit_bytes=KERNEL_VMEM),
        cost_estimate=pl.CostEstimate(
            flops=2 * wide * rows * rows * tiles * width,
            bytes_accessed=4 * rows * tiles * width,
            transcendentals=0,
        ),
        name="select_tiles",
    )(owner, amplitudes.reshape(rows * tiles, width))


def contract_kernel(count, block, owner_ref, counts_ref, *rest):
    parts, integrals = rest[:count], rest[count : count + 2]
    outs, rows_ref, sems = rest[count + 2 : -2], rest[-2], rest[-1]
    rows = rows_ref.shape[0] // count
    copies = [
        pltpu.make_async_copy(part.at[pl.ds(0, rows)], rows_ref.at[pl.ds(n * rows, rows)], sems.at[n])
        for n, part in enumerate(parts)
    ]
    for copy in copies:
        copy.start()
    for copy in copies:
        copy.wait()

    partners, ab, _ = integrals[0].shape
    live = counts_ref[find_tile(owner_ref, lax.axis_index("wide"))]
    for k in range(partners):

        @pl.when(k < live)
        def _():
            for source, integ_ref in enumerate(integrals):

                @pl.loop(0, ab // block)
                def _(c):
                    begin = pl.multiple_of(c * block, block)
                    value = lax.dot_general(
                        rows_ref[...],
                        integ_ref[k, pl.ds(begin, block), :],
                        (((1,), (1,)), ((), ())),
                        preferred_element_type=jnp.float32,
                    ).astype(jnp.bfloat16)
                    column = pl.multiple_of((2 * k + source) * ab + begin, block)
                    first = 0
                    for out in outs:
                        out[:, pl.ds(column, block)] = value[first : first + out.shape[0]]
                        first += out.shape[0]

        @pl.when(k >= live)
        def _():
            for out in outs:
                shape = (out.shape[0], 2 * ab)
                out[:, 2 * k * ab : 2 * (k + 1) * ab] = jnp.zeros(shape, out.dtype)


def contract(parts, rows, out_rows, own, other, owner, counts):
    width = parts[0].shape[1]
    partners, ab, _ = own.shape
    count = len(parts)
    vmem = pl.BlockSpec(memory_space=pltpu.VMEM)
    return pl.pallas_call(
        functools.partial(contract_kernel, count, min(ab, 256)),
        in_specs=[SMEM, SMEM] + [pl.BlockSpec(memory_space=pl.ANY)] * count + [vmem, vmem],
        out_specs=[vmem] * len(out_rows),
        out_shape=[
            jax.ShapeDtypeStruct((each, partners * 2 * ab), jnp.bfloat16) for each in out_rows
        ],
        scratch_shapes=[
            pltpu.VMEM((count * rows, width), parts[0].dtype),
            pltpu.SemaphoreType.DMA((count,)),
        ],
        compiler_params=pltpu.CompilerParams(vmem_limit_bytes=CONTRACT_VMEM),
        cost_estimate=pl.CostEstimate(
            flops=4 * count * rows * width * partners * ab,
            bytes_accessed=4 * partners * ab * width,
            transcendentals=0,
        ),
        name="contract_rows",
    )(owner, counts, *parts, own, other)


def collect_kernel(partners, owner_ref, targets_ref, counts_ref, *rest):
    parts, out_ref, sum_ref = rest[:-2], rest[-2], rest[-1]
    me, mine = lax.axis_index("wide"), lax.axis_index("blk")
    ab = parts[0].shape[1] // (2 * partners)
    sum_ref[...] = jnp.zeros_like(sum_ref)
    for m in range(len(parts) // 2):
        tile = find_tile(owner_ref, lax.bitwise_xor(me, m))
        live = counts_ref[tile]
        for k in range(partners):
            target = targets_ref[tile, k]

            @pl.when(k < live)
            def _():
                for n in range(4):
                    begin = pl.multiple_of(lax.bitwise_xor(mine, n) * ab, 128)
                    column = (2 * k + n % 2) * ab
                    value = parts[2 * m + n // 2][:, column : column + ab]
                    sum_ref[target, :, pl.ds(begin, ab)] += value.astype(jnp.float32)

    outer, inner = out_ref.shape[1:3]
    for i in range(outer):
        out_ref[:, i] = sum_ref[:, i * inner : (i + 1) * inner, :].astype(out_ref.dtype)


def collect(parts, owner, targets, counts, shape):
    partners = targets.shape[1]
    return pl.pallas_call(
        functools.partial(collect_kernel, partners),
        in_specs=[SMEM, SMEM, SMEM] + [pl.BlockSpec(memory_space=pltpu.VMEM)] * len(parts),
        out_specs=pl.BlockSpec(memory_space=pltpu.VMEM),
        out_shape=jax.ShapeDtypeStruct(shape, jnp.bfloat16),
        scratch_shapes=[pltpu.VMEM((shape[0], shape[1] * shape[2], shape[3]), jnp.float32)],
        compiler_params=pltpu.CompilerParams(vmem_limit_bytes=KERNEL_VMEM),
        name="collect_targets",
    )(owner, targets, counts, *parts)


def after(value, earlier):
    return lax.optimization_barrier((value, *earlier))[0] if earlier else value


def body(amplitudes, integrals, owner, targets, counts):
    wide, blk = lax.axis_size("wide"), lax.axis_size("blk")
    i, j, tiles, width = amplitudes.shape
    rows = i * j
    own = integrals[0]
    done = {}

    def step(name, value, axis, mask, *earlier):
        pairs = [(s, s ^ mask) for s in range(lax.axis_size(axis))]
        value = done[value] if isinstance(value, str) else value
        done[name] = lax.ppermute(after(value, [done[e] for e in earlier]), axis, pairs)

    def chip(m, *earlier):
        step(f"chip{m}", done[f"to{m}"][:rows], "blk", 2, *earlier)

    def product(*masks, earlier=()):
        parts = [done[f"{at}{m}"] for at in ("to", "chip") for m in masks]
        out_rows = [rows] * len(masks) + [rows * len(masks)]
        first = after(owner, [done[e] for e in earlier])
        out = contract(parts, rows, out_rows, own, done["other"], first, counts)
        done.update(zip([f"near{m}" for m in masks], out))
        return out[-1]

    def give(name, value, masks, *earlier):
        step(name, value, "blk", 2, *earlier)
        for at, m in enumerate(masks):
            done[f"far{m}"] = done[name][at * rows : (at + 1) * rows]

    groups = ((0,), (1,), (2,), (3,), (4, 5), (6, 7))
    done["to0"], s1, s2, s3, s45, s67 = select(amplitudes, owner, groups)
    step("other", own, "blk", 1)
    step("to4", s45, "wide", 4)
    chip(0)
    step("to1", s1, "wide", 1)
    step("to2", s2, "wide", 2)

    chip(1, "chip0", "to1", "to2")
    chip(2, "chip0", "to1", "to2")
    step("to3", s3, "wide", 3, "chip0", "to1", "to2")

    step("to6", s67, "wide", 6, "to4")
    step("to5", done["to4"][rows:], "wide", 1)
    chip(4, "chip1", "chip2", "to3")
    far = product(0, 1, 2)

    chip(5, "to5", "chip4", "near0")
    step("back1", "near1", "wide", 1)
    step("back2", "near2", "wide", 2)

    chip(3, "chip5")
    far45 = product(4, 5, earlier=("near0",))

    step("back4", "near4", "wide", 4)
    step("back5", "near5", "wide", 5)
    chip(6, "chip3")
    step("to7", done["to6"][rows:], "wide", 1)
    give("far45", far45, (4, 5), "chip3")

    chip(7, "chip6", "to7")
    step("beyond4", "far4", "wide", 4)
    step("beyond5", "far5", "wide", 5)
    give("far012", far, (0, 1, 2), "chip6")
    step("beyond1", "far1", "wide", 1)
    step("beyond2", "far2", "wide", 2)

    far = product(6, 7, 3, earlier=("near4",))
    give("far673", far, (6, 7, 3))
    step("back6", "near6", "wide", 6)
    step("back7", "near7", "wide", 7)
    step("back3", "near3", "wide", 3)
    step("beyond6", "far6", "wide", 6)
    step("beyond7", "far7", "wide", 7)
    step("beyond3", "far3", "wide", 3)
    done["back0"], done["beyond0"] = done["near0"], done["far0"]
    parts = [done[f"{at}{m}"] for m in range(wide) for at in ("back", "beyond")]
    return collect(parts, owner, targets, counts, (wide, i, j, blk * own.shape[1]))


def body_large(amplitudes, integrals, owner, targets, counts):
    wide_count = lax.axis_size("wide")
    my_index = lax.axis_index("wide")
    tile_ids = jnp.arange(owner.shape[0], dtype=jnp.int32)
    holder = jnp.sum(jnp.where(owner[None, :] == tile_ids[:, None], tile_ids[None, :], 0), axis=1)
    ordered = jnp.take(amplitudes, holder, axis=2)
    my_tile = lax.all_to_all(ordered, "wide", split_axis=2, concat_axis=1, tiled=True)
    my_holder = lax.dynamic_index_in_dim(holder, my_index, 0, keepdims=False)
    my_count = lax.dynamic_index_in_dim(counts, my_holder, 0, keepdims=False)
    slot_ids = jnp.arange(targets.shape[1], dtype=jnp.int32)
    live_slots = (slot_ids < my_count).astype(jnp.float32)
    my_integrals = integrals[0]
    width = my_tile.shape[3]
    portion = lax.all_gather(my_tile, "blk", axis=0, tiled=True)
    flat_rows = portion.reshape(-1, width)
    result = jnp.einsum("rc,kac->rka", flat_rows, my_integrals, preferred_element_type=jnp.float32)
    partial_value = result.reshape(
        portion.shape[0], portion.shape[1], my_integrals.shape[0], my_integrals.shape[1]
    )
    shaped = (partial_value * live_slots[None, None, :, None]).astype(jnp.bfloat16)
    received = lax.all_to_all(
        lax.all_to_all(shaped, "wide", split_axis=1, concat_axis=2, tiled=True),
        "blk",
        split_axis=0,
        concat_axis=3,
        tiled=True,
    )
    slot_targets = jnp.take(targets, holder, axis=0).reshape(-1)
    window_ids = jnp.arange(wide_count, dtype=jnp.int32)
    selector = (slot_targets[None, :] == window_ids[:, None]).astype(jnp.bfloat16)
    ladder = jnp.einsum("ps,ijsa->pija", selector, received, preferred_element_type=jnp.float32)
    return ladder.astype(jnp.bfloat16)


def solution(mesh):
    few = mesh.shape["wide"] == 8 and mesh.shape["blk"] == 4
    placed = (P("blk", "wide", None, None), P("wide", None, "blk", None), P(), P(), P())
    return jax.shard_map(
        body if few else body_large,
        mesh=mesh,
        in_specs=placed,
        out_specs=P(None, "blk", "wide", None),
        check_vma=False,
    )
```

```python
import functools

import jax
import jax.numpy as jnp
from jax import lax
from jax.experimental import pallas as pl
from jax.experimental.pallas import tpu as pltpu
from jax.sharding import PartitionSpec as P

MIB = 1 << 20
KERNEL_VMEM = 16 * MIB
CONTRACT_VMEM = 48 * MIB
SMEM = pl.BlockSpec(memory_space=pltpu.SMEM)


def find_tile(owner_ref, slot):
    def step(q, found):
        return jnp.where(owner_ref[q] == slot, q, found)

    return lax.fori_loop(0, owner_ref.shape[0], step, jnp.int32(0))


def select_kernel(rows, groups, owner_ref, amp_ref, *rest):
    outs, pick_ref = rest[:-1], rest[-1]
    tiles = owner_ref.shape[0]

    @pl.when(pl.program_id(0) == 0)
    def _():
        me = lax.axis_index("wide")
        shape = pick_ref.shape
        out_row = lax.broadcasted_iota(jnp.int32, shape, 0)
        in_row = lax.broadcasted_iota(jnp.int32, shape, 1)
        slot = lax.bitwise_xor(out_row // rows, me)
        tile = in_row % tiles
        place = jnp.zeros(shape, jnp.int32)
        for q in range(tiles):
            place = jnp.where(tile == q, owner_ref[q], place)
        chosen = (place == slot) & (out_row % rows == in_row // tiles)
        pick_ref[...] = jnp.where(chosen, 1.0, 0.0).astype(pick_ref.dtype)

    moved = jnp.dot(pick_ref[...], amp_ref[...], preferred_element_type=jnp.float32)
    moved = moved.astype(amp_ref.dtype)
    for group, out in zip(groups, outs):
        for at, m in enumerate(group):
            out[at * rows : (at + 1) * rows] = moved[m * rows : (m + 1) * rows]


def select(amplitudes, owner, groups):
    i, j, tiles, width = amplitudes.shape
    rows = i * j
    wide = sum(map(len, groups))
    block = min(width, 1024)
    return pl.pallas_call(
        functools.partial(select_kernel, rows, groups),
        grid=(width // block,),
        in_specs=[SMEM, pl.BlockSpec((rows * tiles, block), lambda c: (0, c))],
        out_specs=[pl.BlockSpec((len(g) * rows, block), lambda c: (0, c)) for g in groups],
        out_shape=[jax.ShapeDtypeStruct((len(g) * rows, width), amplitudes.dtype) for g in groups],
        scratch_shapes=[pltpu.VMEM((wide * rows, rows * tiles), amplitudes.dtype)],
        compiler_params=pltpu.CompilerParams(vmem_limit_bytes=KERNEL_VMEM),
        cost_estimate=pl.CostEstimate(
            flops=2 * wide * rows * rows * tiles * width,
            bytes_accessed=4 * rows * tiles * width,
            transcendentals=0,
        ),
        name="select_tiles",
    )(owner, amplitudes.reshape(rows * tiles, width))


def contract_kernel(count, owner_ref, counts_ref, *rest):
    parts, integrals = rest[:count], rest[count : count + 2]
    outs, rows_ref, sems = rest[count + 2 : -2], rest[-2], rest[-1]
    rows = rows_ref.shape[0] // count
    partner, source, block = (pl.program_id(axis) for axis in range(3))
    copies = [
        pltpu.make_async_copy(part.at[pl.ds(0, rows)], rows_ref.at[pl.ds(n * rows, rows)], sems.at[n])
        for n, part in enumerate(parts)
    ]

    @pl.when((partner == 0) & (source == 0) & (block == 0))
    def _():
        for copy in copies:
            copy.start()
        for copy in copies:
            copy.wait()

    live = partner < counts_ref[find_tile(owner_ref, lax.axis_index("wide"))]
    for at, integ_ref in enumerate(integrals):

        @pl.when(live & (source == at))
        def _():
            value = lax.dot_general(
                rows_ref[...],
                integ_ref[0],
                (((1,), (1,)), ((), ())),
                preferred_element_type=jnp.float32,
            ).astype(jnp.bfloat16)
            first = 0
            for out in outs:
                out[...] = value[first : first + out.shape[0]]
                first += out.shape[0]

    @pl.when(jnp.logical_not(live))
    def _():
        for out in outs:
            out[...] = jnp.zeros_like(out)


def contract(parts, rows, out_rows, own, other, owner, counts):
    width = parts[0].shape[1]
    partners, ab, _ = own.shape
    count = len(parts)
    block = min(ab, 256)
    steps = ab // block
    return pl.pallas_call(
        functools.partial(contract_kernel, count),
        grid=(partners, 2, steps),
        in_specs=[SMEM, SMEM]
        + [pl.BlockSpec(memory_space=pl.ANY)] * count
        + [
            pl.BlockSpec((1, block, width), lambda k, s, c: (k, jnp.where(s == 0, c, steps - 1), 0)),
            pl.BlockSpec((1, block, width), lambda k, s, c: (k, jnp.where(s == 0, 0, c), 0)),
        ],
        out_specs=[
            pl.BlockSpec((each, block), lambda k, s, c: (0, (k * 2 + s) * steps + c))
            for each in out_rows
        ],
        out_shape=[
            jax.ShapeDtypeStruct((each, partners * 2 * ab), jnp.bfloat16) for each in out_rows
        ],
        scratch_shapes=[
            pltpu.VMEM((count * rows, width), parts[0].dtype),
            pltpu.SemaphoreType.DMA((count,)),
        ],
        compiler_params=pltpu.CompilerParams(vmem_limit_bytes=CONTRACT_VMEM),
        cost_estimate=pl.CostEstimate(
            flops=4 * count * rows * width * partners * ab,
            bytes_accessed=4 * partners * ab * width,
            transcendentals=0,
        ),
        name="contract_rows",
    )(owner, counts, *parts, own, other)


def collect_kernel(partners, owner_ref, targets_ref, counts_ref, *rest):
    parts, out_ref, sum_ref = rest[:-2], rest[-2], rest[-1]
    me, mine = lax.axis_index("wide"), lax.axis_index("blk")
    ab = parts[0].shape[1] // (2 * partners)
    sum_ref[...] = jnp.zeros_like(sum_ref)
    for m in range(len(parts) // 2):
        tile = find_tile(owner_ref, lax.bitwise_xor(me, m))
        live = counts_ref[tile]
        for k in range(partners):
            target = targets_ref[tile, k]

            @pl.when(k < live)
            def _():
                for n in range(4):
                    begin = pl.multiple_of(lax.bitwise_xor(mine, n) * ab, 128)
                    column = (2 * k + n % 2) * ab
                    value = parts[2 * m + n // 2][:, column : column + ab]
                    sum_ref[target, :, pl.ds(begin, ab)] += value.astype(jnp.float32)

    outer, inner = out_ref.shape[1:3]
    for i in range(outer):
        out_ref[:, i] = sum_ref[:, i * inner : (i + 1) * inner, :].astype(out_ref.dtype)


def collect(parts, owner, targets, counts, shape):
    partners = targets.shape[1]
    return pl.pallas_call(
        functools.partial(collect_kernel, partners),
        in_specs=[SMEM, SMEM, SMEM] + [pl.BlockSpec(memory_space=pltpu.VMEM)] * len(parts),
        out_specs=pl.BlockSpec(memory_space=pltpu.VMEM),
        out_shape=jax.ShapeDtypeStruct(shape, jnp.bfloat16),
        scratch_shapes=[pltpu.VMEM((shape[0], shape[1] * shape[2], shape[3]), jnp.float32)],
        compiler_params=pltpu.CompilerParams(vmem_limit_bytes=KERNEL_VMEM),
        name="collect_targets",
    )(owner, targets, counts, *parts)


def after(value, earlier):
    return lax.optimization_barrier((value, *earlier))[0] if earlier else value


def body(amplitudes, integrals, owner, targets, counts):
    wide, blk = lax.axis_size("wide"), lax.axis_size("blk")
    i, j, tiles, width = amplitudes.shape
    rows = i * j
    own = integrals[0]
    done = {}

    def step(name, value, axis, mask, *earlier):
        pairs = [(s, s ^ mask) for s in range(lax.axis_size(axis))]
        value = done[value] if isinstance(value, str) else value
        done[name] = lax.ppermute(after(value, [done[e] for e in earlier]), axis, pairs)

    def chip(m, *earlier):
        step(f"chip{m}", done[f"to{m}"][:rows], "blk", 2, *earlier)

    def product(*masks, earlier=()):
        parts = [done[f"{at}{m}"] for at in ("to", "chip") for m in masks]
        out_rows = [rows] * len(masks) + [rows * len(masks)]
        first = after(owner, [done[e] for e in earlier])
        out = contract(parts, rows, out_rows, own, done["other"], first, counts)
        done.update(zip([f"near{m}" for m in masks], out))
        return out[-1]

    def give(name, value, masks, *earlier):
        step(name, value, "blk", 2, *earlier)
        for at, m in enumerate(masks):
            done[f"far{m}"] = done[name][at * rows : (at + 1) * rows]

    def back(m, *earlier):
        both = jnp.concatenate([done[f"near{m}"], done[f"far{m}"]])
        step(f"both{m}", both, "wide", m, *earlier)
        done[f"back{m}"], done[f"beyond{m}"] = done[f"both{m}"][:rows], done[f"both{m}"][rows:]

    groups = ((0,), (1,), (2,), (3,), (4, 5), (6,), (7,))
    done["to0"], s1, s2, s3, s45, s6, s7 = select(amplitudes, owner, groups)
    step("other", own, "blk", 1)
    step("to4", s45, "wide", 4)
    chip(0)
    step("to1", s1, "wide", 1)
    chip(1)
    step("to2", s2, "wide", 2, "to1")
    step("to3", s3, "wide", 3, "chip0")
    chip(2)
    step("to6", s6, "wide", 6, "to4", "chip1")
    step("to5", done["to4"][rows:], "wide", 1, "other")
    chip(4)
    chip(5)
    step("to7", s7, "wide", 7, "chip4", "to5")
    chip(3, "chip5")
    far45 = product(4, 5)

    step("back4", "near4", "wide", 4)
    step("back5", "near5", "wide", 5)
    chip(6)
    give("far45", far45, (4, 5))
    chip(7, "near4")
    far = product(0, 1, 2, 3, earlier=("near4", "chip6"))
    step("beyond4", "far4", "wide", 4)
    step("beyond5", "far5", "wide", 5)

    far67 = product(6, 7, earlier=("near0",))
    step("back6", "near6", "wide", 6)
    step("back7", "near7", "wide", 7)
    give("far67", far67, (6, 7))
    give("far0123", far, (0, 1, 2, 3), "chip7")
    back(1)
    back(2)
    back(3)
    step("beyond6", "far6", "wide", 6)
    step("beyond7", "far7", "wide", 7)
    done["back0"], done["beyond0"] = done["near0"], done["far0"]
    parts = [done[f"{at}{m}"] for m in range(wide) for at in ("back", "beyond")]
    return collect(parts, owner, targets, counts, (wide, i, j, blk * own.shape[1]))


def body_large(amplitudes, integrals, owner, targets, counts):
    wide_count = lax.axis_size("wide")
    my_index = lax.axis_index("wide")
    tile_ids = jnp.arange(owner.shape[0], dtype=jnp.int32)
    holder = jnp.sum(jnp.where(owner[None, :] == tile_ids[:, None], tile_ids[None, :], 0), axis=1)
    ordered = jnp.take(amplitudes, holder, axis=2)
    my_tile = lax.all_to_all(ordered, "wide", split_axis=2, concat_axis=1, tiled=True)
    my_holder = lax.dynamic_index_in_dim(holder, my_index, 0, keepdims=False)
    my_count = lax.dynamic_index_in_dim(counts, my_holder, 0, keepdims=False)
    slot_ids = jnp.arange(targets.shape[1], dtype=jnp.int32)
    live_slots = (slot_ids < my_count).astype(jnp.float32)
    my_integrals = integrals[0]
    width = my_tile.shape[3]
    portion = lax.all_gather(my_tile, "blk", axis=0, tiled=True)
    flat_rows = portion.reshape(-1, width)
    result = jnp.einsum("rc,kac->rka", flat_rows, my_integrals, preferred_element_type=jnp.float32)
    partial_value = result.reshape(
        portion.shape[0], portion.shape[1], my_integrals.shape[0], my_integrals.shape[1]
    )
    shaped = (partial_value * live_slots[None, None, :, None]).astype(jnp.bfloat16)
    received = lax.all_to_all(
        lax.all_to_all(shaped, "wide", split_axis=1, concat_axis=2, tiled=True),
        "blk",
        split_axis=0,
        concat_axis=3,
        tiled=True,
    )
    slot_targets = jnp.take(targets, holder, axis=0).reshape(-1)
    window_ids = jnp.arange(wide_count, dtype=jnp.int32)
    selector = (slot_targets[None, :] == window_ids[:, None]).astype(jnp.bfloat16)
    ladder = jnp.einsum("ps,ijsa->pija", selector, received, preferred_element_type=jnp.float32)
    return ladder.astype(jnp.bfloat16)


def solution(mesh):
    few = mesh.shape["wide"] == 8 and mesh.shape["blk"] == 4
    placed = (P("blk", "wide", None, None), P("wide", None, "blk", None), P(), P(), P())
    return jax.shard_map(
        body if few else body_large,
        mesh=mesh,
        in_specs=placed,
        out_specs=P(None, "blk", "wide", None),
        check_vma=False,
    )
```

```python
import functools

import jax
import jax.numpy as jnp
from jax import lax
from jax.experimental import pallas as pl
from jax.experimental.pallas import tpu as pltpu
from jax.sharding import PartitionSpec as P

MIB = 1 << 20
KERNEL_VMEM = 16 * MIB
CONTRACT_VMEM = 20 * MIB
HOLD_VMEM = 44 * MIB
SMEM = pl.BlockSpec(memory_space=pltpu.SMEM)


def find_tile(owner_ref, slot):
    def step(q, found):
        return jnp.where(owner_ref[q] == slot, q, found)

    return lax.fori_loop(0, owner_ref.shape[0], step, jnp.int32(0))


def select_kernel(rows, groups, owner_ref, amp_ref, *rest):
    outs, pick_ref = rest[:-1], rest[-1]
    tiles = owner_ref.shape[0]

    @pl.when(pl.program_id(0) == 0)
    def _():
        me = lax.axis_index("wide")
        shape = pick_ref.shape
        out_row = lax.broadcasted_iota(jnp.int32, shape, 0)
        in_row = lax.broadcasted_iota(jnp.int32, shape, 1)
        slot = lax.bitwise_xor(out_row // rows, me)
        tile = in_row % tiles
        place = jnp.zeros(shape, jnp.int32)
        for q in range(tiles):
            place = jnp.where(tile == q, owner_ref[q], place)
        chosen = (place == slot) & (out_row % rows == in_row // tiles)
        pick_ref[...] = jnp.where(chosen, 1.0, 0.0).astype(pick_ref.dtype)

    moved = jnp.dot(pick_ref[...], amp_ref[...], preferred_element_type=jnp.float32)
    moved = moved.astype(amp_ref.dtype)
    for group, out in zip(groups, outs):
        for at, m in enumerate(group):
            out[at * rows : (at + 1) * rows] = moved[m * rows : (m + 1) * rows]


def select(amplitudes, owner, groups):
    i, j, tiles, width = amplitudes.shape
    rows = i * j
    wide = sum(map(len, groups))
    block = min(width, 1024)
    return pl.pallas_call(
        functools.partial(select_kernel, rows, groups),
        grid=(width // block,),
        in_specs=[SMEM, pl.BlockSpec((rows * tiles, block), lambda c: (0, c))],
        out_specs=[pl.BlockSpec((len(g) * rows, block), lambda c: (0, c)) for g in groups],
        out_shape=[jax.ShapeDtypeStruct((len(g) * rows, width), amplitudes.dtype) for g in groups],
        scratch_shapes=[pltpu.VMEM((wide * rows, rows * tiles), amplitudes.dtype)],
        compiler_params=pltpu.CompilerParams(vmem_limit_bytes=KERNEL_VMEM),
        cost_estimate=pl.CostEstimate(
            flops=2 * wide * rows * rows * tiles * width,
            bytes_accessed=4 * rows * tiles * width,
            transcendentals=0,
        ),
        name="select_tiles",
    )(owner, amplitudes.reshape(rows * tiles, width))


def hold_kernel(value_ref, held_ref, sem):
    copy = pltpu.make_async_copy(value_ref, held_ref, sem)
    copy.start()
    copy.wait()


def hold(value):
    return pl.pallas_call(
        hold_kernel,
        in_specs=[pl.BlockSpec(memory_space=pl.ANY)],
        out_specs=pl.BlockSpec(memory_space=pltpu.VMEM),
        out_shape=jax.ShapeDtypeStruct(value.shape, value.dtype),
        scratch_shapes=[pltpu.SemaphoreType.DMA],
        compiler_params=pltpu.CompilerParams(vmem_limit_bytes=HOLD_VMEM),
        name="hold_integrals",
    )(value)


def contract_kernel(count, block, *refs):
    parts, integrals = refs[:count], refs[count : count + 2]
    outs, rows_ref, sems = refs[count + 2 : -2], refs[-2], refs[-1]
    rows = rows_ref.shape[0] // count
    partners, ab, _ = integrals[0].shape
    copies = [
        pltpu.make_async_copy(part.at[pl.ds(0, rows)], rows_ref.at[pl.ds(n * rows, rows)], sems.at[n])
        for n, part in enumerate(parts)
    ]
    for copy in copies:
        copy.start()
    for copy in copies:
        copy.wait()
    for source, integ_ref in enumerate(integrals):

        @pl.loop(0, partners * ab // block)
        def _(at):
            k, begin = at // (ab // block), pl.multiple_of(at % (ab // block) * block, block)
            value = lax.dot_general(
                integ_ref[k, pl.ds(begin, block), :],
                rows_ref[...],
                (((1,), (1,)), ((), ())),
                preferred_element_type=jnp.float32,
            ).T.astype(jnp.bfloat16)
            column = pl.multiple_of((2 * k + source) * ab + begin, block)
            first = 0
            for out in outs:
                out[:, pl.ds(column, block)] = value[first : first + out.shape[0]]
                first += out.shape[0]


def contract(parts, rows, out_rows, own, other):
    width = parts[0].shape[1]
    partners, ab, _ = own.shape
    count = len(parts)
    vmem = pl.BlockSpec(memory_space=pltpu.VMEM)
    return pl.pallas_call(
        functools.partial(contract_kernel, count, min(ab, 512)),
        in_specs=[pl.BlockSpec(memory_space=pl.ANY)] * count + [vmem, vmem],
        out_specs=[vmem] * len(out_rows),
        out_shape=[
            jax.ShapeDtypeStruct((each, partners * 2 * ab), jnp.bfloat16) for each in out_rows
        ],
        scratch_shapes=[
            pltpu.VMEM((count * rows, width), parts[0].dtype),
            pltpu.SemaphoreType.DMA((count,)),
        ],
        compiler_params=pltpu.CompilerParams(vmem_limit_bytes=CONTRACT_VMEM),
        cost_estimate=pl.CostEstimate(
            flops=4 * count * rows * width * partners * ab,
            bytes_accessed=4 * partners * ab * width,
            transcendentals=0,
        ),
        name="contract_rows",
    )(*parts, own, other)


def collect_kernel(partners, owner_ref, targets_ref, counts_ref, *rest):
    wide = owner_ref.shape[0]
    parts, outs, sum_ref = rest[:wide], rest[wide:-1], rest[-1]
    me = lax.axis_index("wide")
    ab = parts[0].shape[1] // partners
    sum_ref[...] = jnp.zeros_like(sum_ref)
    for m, part in enumerate(parts):
        tile = find_tile(owner_ref, lax.bitwise_xor(me, m))
        live = counts_ref[tile]
        for k in range(partners):
            target = targets_ref[tile, k]

            @pl.when(k < live)
            def _():
                sum_ref[target] += part[:, k * ab : (k + 1) * ab].astype(jnp.float32)

    rows = outs[0].shape[1]
    for n, out in enumerate(outs):
        out[...] = sum_ref[:, n * rows : (n + 1) * rows, :].astype(out.dtype)


def collect(parts, owner, targets, counts, tiles_out):
    rows, columns = parts[0].shape
    partners = targets.shape[1]
    ab = columns // partners
    return pl.pallas_call(
        functools.partial(collect_kernel, partners),
        in_specs=[SMEM, SMEM, SMEM] + [pl.BlockSpec(memory_space=pltpu.VMEM)] * len(parts),
        out_specs=[pl.BlockSpec(memory_space=pltpu.VMEM)] * 2,
        out_shape=[jax.ShapeDtypeStruct((tiles_out, rows // 2, ab), jnp.bfloat16)] * 2,
        scratch_shapes=[pltpu.VMEM((tiles_out, rows, ab), jnp.float32)],
        compiler_params=pltpu.CompilerParams(vmem_limit_bytes=KERNEL_VMEM),
        name="collect_targets",
    )(owner, targets, counts, *parts)


def place_kernel(*refs):
    parts, out_ref = refs[:-1], refs[-1]
    mine = lax.axis_index("blk")
    ab = parts[0].shape[2] // 2
    for chip, part in enumerate(parts):
        for core in range(2):
            begin = pl.multiple_of(lax.bitwise_xor(mine, chip * 2 + core) * ab, 128)
            out_ref[:, :, pl.ds(begin, ab)] = part[:, :, core * ab : (core + 1) * ab]


def place(parts):
    tiles_out, rows, columns = parts[0].shape
    block = min(tiles_out, 2)
    return pl.pallas_call(
        place_kernel,
        grid=(tiles_out // block,),
        in_specs=[pl.BlockSpec((block, rows, columns), lambda p: (p, 0, 0))] * len(parts),
        out_specs=pl.BlockSpec((block, rows, len(parts) * columns), lambda p: (p, 0, 0)),
        out_shape=jax.ShapeDtypeStruct((tiles_out, rows, len(parts) * columns), parts[0].dtype),
        compiler_params=pltpu.CompilerParams(vmem_limit_bytes=KERNEL_VMEM),
        name="place_columns",
    )(*parts)


def after(value, earlier):
    return lax.optimization_barrier((value, *earlier))[0] if earlier else value


def body(amplitudes, integrals, owner, targets, counts):
    wide = lax.axis_size("wide")
    i, j, tiles, width = amplitudes.shape
    rows = i * j
    own = integrals[0]
    done = {}

    def step(name, value, axis, mask, *earlier):
        pairs = [(s, s ^ mask) for s in range(lax.axis_size(axis))]
        value = done[value] if isinstance(value, str) else value
        done[name] = lax.ppermute(after(value, [done[e] for e in earlier]), axis, pairs)

    def chip(m, *earlier):
        step(f"chip{m}", done[f"to{m}"][:rows], "blk", 2, *earlier)

    def product(*masks, earlier=()):
        parts = [done[f"{at}{m}"] for m in masks for at in ("to", "chip")]
        parts[0] = after(parts[0], [done[e] for e in earlier])
        out = contract(parts, rows, [2 * rows] * len(masks), done["own"], done["other"])
        done.update(zip([f"made{m}" for m in masks], out))

    def back(m, *earlier):
        step(f"back{m}", f"made{m}", "wide", m, *earlier)

    groups = ((0,), (1,), (2,), (3,), (4, 5), (6,), (7,))
    done["to0"], s1, s2, s3, s45, s6, s7 = select(amplitudes, owner, groups)
    step("other", own, "blk", 1)
    step("to4", s45, "wide", 4)
    chip(0)
    step("to1", s1, "wide", 1)
    done["own"] = hold(after(own, [done["to1"], done["chip0"]]))
    chip(1, "own")
    step("to2", s2, "wide", 2, "to1")
    step("to3", s3, "wide", 3, "to1")
    step("to6", s6, "wide", 6, "to4", "chip1", "to2")
    step("to5", done["to4"][rows:], "wide", 1, "other")
    chip(4, "chip1")
    chip(5, "to6", "to3")
    step("to7", s7, "wide", 7, "chip4", "to5")
    product(4, 5)

    back(4)
    back(5)
    chip(6, "chip5")
    chip(7, "made4")
    chip(2, "chip7")
    chip(3, "chip7")
    product(6, 7, earlier=("back4", "chip6"))
    back(6)
    back(7)
    product(0, 1, 2, 3, earlier=("made6",))
    back(1)
    back(2)
    back(3)
    parts = [done["made0"]] + [done[f"back{m}"] for m in range(1, wide)]
    sums = list(collect(parts, owner, targets, counts, wide))
    done["sums"] = sums[1]
    step("swapped", "sums", "blk", 2)
    return place([sums[0], done["swapped"]]).reshape(wide, i, j, -1)


def body_large(amplitudes, integrals, owner, targets, counts):
    wide_count = lax.axis_size("wide")
    my_index = lax.axis_index("wide")
    tile_ids = jnp.arange(owner.shape[0], dtype=jnp.int32)
    holder = jnp.sum(jnp.where(owner[None, :] == tile_ids[:, None], tile_ids[None, :], 0), axis=1)
    ordered = jnp.take(amplitudes, holder, axis=2)
    my_tile = lax.all_to_all(ordered, "wide", split_axis=2, concat_axis=1, tiled=True)
    my_holder = lax.dynamic_index_in_dim(holder, my_index, 0, keepdims=False)
    my_count = lax.dynamic_index_in_dim(counts, my_holder, 0, keepdims=False)
    slot_ids = jnp.arange(targets.shape[1], dtype=jnp.int32)
    live_slots = (slot_ids < my_count).astype(jnp.float32)
    my_integrals = integrals[0]
    width = my_tile.shape[3]
    portion = lax.all_gather(my_tile, "blk", axis=0, tiled=True)
    flat_rows = portion.reshape(-1, width)
    result = jnp.einsum("rc,kac->rka", flat_rows, my_integrals, preferred_element_type=jnp.float32)
    partial_value = result.reshape(
        portion.shape[0], portion.shape[1], my_integrals.shape[0], my_integrals.shape[1]
    )
    shaped = (partial_value * live_slots[None, None, :, None]).astype(jnp.bfloat16)
    received = lax.all_to_all(
        lax.all_to_all(shaped, "wide", split_axis=1, concat_axis=2, tiled=True),
        "blk",
        split_axis=0,
        concat_axis=3,
        tiled=True,
    )
    slot_targets = jnp.take(targets, holder, axis=0).reshape(-1)
    window_ids = jnp.arange(wide_count, dtype=jnp.int32)
    selector = (slot_targets[None, :] == window_ids[:, None]).astype(jnp.bfloat16)
    ladder = jnp.einsum("ps,ijsa->pija", selector, received, preferred_element_type=jnp.float32)
    return ladder.astype(jnp.bfloat16)


def solution(mesh):
    few = mesh.shape["wide"] == 8 and mesh.shape["blk"] == 4
    placed = (P("blk", "wide", None, None), P("wide", None, "blk", None), P(), P(), P())
    return jax.shard_map(
        body if few else body_large,
        mesh=mesh,
        in_specs=placed,
        out_specs=P(None, "blk", "wide", None),
        check_vma=False,
    )
```

```python
import functools

import jax
import jax.numpy as jnp
from jax import lax
from jax.experimental import pallas as pl
from jax.experimental.pallas import tpu as pltpu
from jax.sharding import PartitionSpec as P

MIB = 1 << 20
KERNEL_VMEM = 16 * MIB
CONTRACT_VMEM = 20 * MIB
HOLD_VMEM = 44 * MIB
SMEM = pl.BlockSpec(memory_space=pltpu.SMEM)


def find_tile(owner_ref, slot):
    def step(q, found):
        return jnp.where(owner_ref[q] == slot, q, found)

    return lax.fori_loop(0, owner_ref.shape[0], step, jnp.int32(0))


def select_kernel(rows, groups, owner_ref, amp_ref, *rest):
    outs, pick_ref = rest[:-1], rest[-1]
    tiles = owner_ref.shape[0]

    @pl.when(pl.program_id(0) == 0)
    def _():
        me = lax.axis_index("wide")
        shape = pick_ref.shape
        out_row = lax.broadcasted_iota(jnp.int32, shape, 0)
        in_row = lax.broadcasted_iota(jnp.int32, shape, 1)
        slot = lax.bitwise_xor(out_row // rows, me)
        tile = in_row % tiles
        place = jnp.zeros(shape, jnp.int32)
        for q in range(tiles):
            place = jnp.where(tile == q, owner_ref[q], place)
        chosen = (place == slot) & (out_row % rows == in_row // tiles)
        pick_ref[...] = jnp.where(chosen, 1.0, 0.0).astype(pick_ref.dtype)

    moved = jnp.dot(pick_ref[...], amp_ref[...], preferred_element_type=jnp.float32)
    moved = moved.astype(amp_ref.dtype)
    for group, out in zip(groups, outs):
        for at, m in enumerate(group):
            out[at * rows : (at + 1) * rows] = moved[m * rows : (m + 1) * rows]


def select(amplitudes, owner, groups):
    i, j, tiles, width = amplitudes.shape
    rows = i * j
    wide = sum(map(len, groups))
    block = min(width, 1024)
    return pl.pallas_call(
        functools.partial(select_kernel, rows, groups),
        grid=(width // block,),
        in_specs=[SMEM, pl.BlockSpec((rows * tiles, block), lambda c: (0, c))],
        out_specs=[pl.BlockSpec((len(g) * rows, block), lambda c: (0, c)) for g in groups],
        out_shape=[jax.ShapeDtypeStruct((len(g) * rows, width), amplitudes.dtype) for g in groups],
        scratch_shapes=[pltpu.VMEM((wide * rows, rows * tiles), amplitudes.dtype)],
        compiler_params=pltpu.CompilerParams(vmem_limit_bytes=KERNEL_VMEM),
        cost_estimate=pl.CostEstimate(
            flops=2 * wide * rows * rows * tiles * width,
            bytes_accessed=4 * rows * tiles * width,
            transcendentals=0,
        ),
        name="select_tiles",
    )(owner, amplitudes.reshape(rows * tiles, width))


def hold_kernel(value_ref, held_ref, sem):
    copy = pltpu.make_async_copy(value_ref, held_ref, sem)
    copy.start()
    copy.wait()


def hold(value):
    return pl.pallas_call(
        hold_kernel,
        in_specs=[pl.BlockSpec(memory_space=pl.ANY)],
        out_specs=pl.BlockSpec(memory_space=pltpu.VMEM),
        out_shape=jax.ShapeDtypeStruct(value.shape, value.dtype),
        scratch_shapes=[pltpu.SemaphoreType.DMA],
        compiler_params=pltpu.CompilerParams(vmem_limit_bytes=HOLD_VMEM),
        name="hold_integrals",
    )(value)


def contract_kernel(count, block, *refs):
    parts, integrals = refs[:count], refs[count : count + 2]
    outs, rows_ref, sems = refs[count + 2 : -2], refs[-2], refs[-1]
    rows = rows_ref.shape[0] // count
    partners, ab, _ = integrals[0].shape
    copies = [
        pltpu.make_async_copy(part.at[pl.ds(0, rows)], rows_ref.at[pl.ds(n * rows, rows)], sems.at[n])
        for n, part in enumerate(parts)
    ]
    for copy in copies:
        copy.start()
    for copy in copies:
        copy.wait()
    for source, integ_ref in enumerate(integrals):

        @pl.loop(0, partners * ab // block)
        def _(at):
            k, begin = at // (ab // block), pl.multiple_of(at % (ab // block) * block, block)
            value = lax.dot_general(
                integ_ref[k, pl.ds(begin, block), :],
                rows_ref[...],
                (((1,), (1,)), ((), ())),
                preferred_element_type=jnp.float32,
            ).T.astype(jnp.bfloat16)
            column = pl.multiple_of((2 * k + source) * ab + begin, block)
            first = 0
            for out in outs:
                out[:, pl.ds(column, block)] = value[first : first + out.shape[0]]
                first += out.shape[0]


def contract(parts, rows, out_rows, own, other):
    width = parts[0].shape[1]
    partners, ab, _ = own.shape
    count = len(parts)
    vmem = pl.BlockSpec(memory_space=pltpu.VMEM)
    return pl.pallas_call(
        functools.partial(contract_kernel, count, min(ab, 512)),
        in_specs=[pl.BlockSpec(memory_space=pl.ANY)] * count + [vmem, vmem],
        out_specs=[vmem] * len(out_rows),
        out_shape=[
            jax.ShapeDtypeStruct((each, partners * 2 * ab), jnp.bfloat16) for each in out_rows
        ],
        scratch_shapes=[
            pltpu.VMEM((count * rows, width), parts[0].dtype),
            pltpu.SemaphoreType.DMA((count,)),
        ],
        compiler_params=pltpu.CompilerParams(vmem_limit_bytes=CONTRACT_VMEM),
        cost_estimate=pl.CostEstimate(
            flops=4 * count * rows * width * partners * ab,
            bytes_accessed=4 * partners * ab * width,
            transcendentals=0,
        ),
        name="contract_rows",
    )(*parts, own, other)


def collect_kernel(partners, owner_ref, targets_ref, counts_ref, *rest):
    wide = owner_ref.shape[0]
    parts, outs, sum_ref = rest[:wide], rest[wide:-1], rest[-1]
    me = lax.axis_index("wide")
    ab = parts[0].shape[1] // partners
    sum_ref[...] = jnp.zeros_like(sum_ref)
    for m, part in enumerate(parts):
        tile = find_tile(owner_ref, lax.bitwise_xor(me, m))
        live = counts_ref[tile]
        for k in range(partners):
            target = targets_ref[tile, k]

            @pl.when(k < live)
            def _():
                sum_ref[target] += part[:, k * ab : (k + 1) * ab].astype(jnp.float32)

    rows = outs[0].shape[1]
    for n, out in enumerate(outs):
        out[...] = sum_ref[:, n * rows : (n + 1) * rows, :].astype(out.dtype)


def collect(parts, owner, targets, counts, tiles_out):
    rows, columns = parts[0].shape
    partners = targets.shape[1]
    ab = columns // partners
    return pl.pallas_call(
        functools.partial(collect_kernel, partners),
        in_specs=[SMEM, SMEM, SMEM] + [pl.BlockSpec(memory_space=pltpu.VMEM)] * len(parts),
        out_specs=[pl.BlockSpec(memory_space=pltpu.VMEM)] * 2,
        out_shape=[jax.ShapeDtypeStruct((tiles_out, rows // 2, ab), jnp.bfloat16)] * 2,
        scratch_shapes=[pltpu.VMEM((tiles_out, rows, ab), jnp.float32)],
        compiler_params=pltpu.CompilerParams(vmem_limit_bytes=KERNEL_VMEM),
        name="collect_targets",
    )(owner, targets, counts, *parts)


def place_kernel(*refs):
    parts, out_ref = refs[:-1], refs[-1]
    mine = lax.axis_index("blk")
    ab = parts[0].shape[2] // 2
    for chip, part in enumerate(parts):
        for core in range(2):
            begin = pl.multiple_of(lax.bitwise_xor(mine, chip * 2 + core) * ab, 128)
            out_ref[:, :, pl.ds(begin, ab)] = part[:, :, core * ab : (core + 1) * ab]


def place(parts):
    tiles_out, rows, columns = parts[0].shape
    block = min(tiles_out, 2)
    return pl.pallas_call(
        place_kernel,
        grid=(tiles_out // block,),
        in_specs=[pl.BlockSpec((block, rows, columns), lambda p: (p, 0, 0))] * len(parts),
        out_specs=pl.BlockSpec((block, rows, len(parts) * columns), lambda p: (p, 0, 0)),
        out_shape=jax.ShapeDtypeStruct((tiles_out, rows, len(parts) * columns), parts[0].dtype),
        compiler_params=pltpu.CompilerParams(vmem_limit_bytes=KERNEL_VMEM),
        name="place_columns",
    )(*parts)


def after(value, earlier):
    return lax.optimization_barrier((value, *earlier))[0] if earlier else value


def body(amplitudes, integrals, owner, targets, counts):
    wide = lax.axis_size("wide")
    i, j, tiles, width = amplitudes.shape
    rows = i * j
    own = integrals[0]
    done = {}

    def step(name, value, axis, mask, *earlier):
        pairs = [(s, s ^ mask) for s in range(lax.axis_size(axis))]
        value = done[value] if isinstance(value, str) else value
        done[name] = lax.ppermute(after(value, [done[e] for e in earlier]), axis, pairs)

    def chip(m, *earlier):
        step(f"chip{m}", done[f"to{m}"][:rows], "blk", 2, *earlier)

    def product(*masks, cut=1, earlier=()):
        parts = [done[f"{at}{m}"] for m in masks for at in ("to", "chip")]
        parts[0] = after(parts[0], [done[e] for e in earlier])
        out_rows = [2 * rows * cut] * (len(masks) // cut)
        out = contract(parts, rows, out_rows, done["own"], done["other"])
        done.update(zip([f"made{m}" for m in masks[::cut]], out))

    def back(m, *earlier):
        step(f"back{m}", f"made{m}", "wide", m, *earlier)

    groups = ((0,), (1,), (2,), (3,), (4, 5), (6,), (7,))
    done["to0"], s1, s2, s3, s45, s6, s7 = select(amplitudes, owner, groups)
    step("other", own, "blk", 1)
    step("to4", s45, "wide", 4)
    chip(0)
    step("to1", s1, "wide", 1)
    done["own"] = hold(after(own, [done["to1"], done["chip0"]]))
    chip(1, "own")
    step("to2", s2, "wide", 2, "to1")
    step("to3", s3, "wide", 3, "to1")
    step("to6", s6, "wide", 6, "chip1", "own")
    step("to5", done["to4"][rows:], "wide", 1, "other")
    chip(4, "chip1")
    chip(5, "to6", "to2")
    step("to7", s7, "wide", 7, "to4", "to5", "to3")
    chip(2, "chip5")
    chip(3, "chip5")
    product(4, 5, cut=2)

    back(4)
    chip(6, "chip5")
    chip(7, "made4")
    product(0, 1, 2, 3, earlier=("made4",))
    step("back5", done["back4"][2 * rows :], "wide", 1)
    done["back4"] = done["back4"][: 2 * rows]
    product(6, 7, earlier=("made0",))
    back(6)
    back(7)
    back(1)
    back(2)
    back(3)
    parts = [done["made0"]] + [done[f"back{m}"] for m in range(1, wide)]
    sums = list(collect(parts, owner, targets, counts, wide))
    done["sums"] = sums[1]
    step("swapped", "sums", "blk", 2)
    return place([sums[0], done["swapped"]]).reshape(wide, i, j, -1)


def body_large(amplitudes, integrals, owner, targets, counts):
    wide_count = lax.axis_size("wide")
    my_index = lax.axis_index("wide")
    tile_ids = jnp.arange(owner.shape[0], dtype=jnp.int32)
    holder = jnp.sum(jnp.where(owner[None, :] == tile_ids[:, None], tile_ids[None, :], 0), axis=1)
    ordered = jnp.take(amplitudes, holder, axis=2)
    my_tile = lax.all_to_all(ordered, "wide", split_axis=2, concat_axis=1, tiled=True)
    my_holder = lax.dynamic_index_in_dim(holder, my_index, 0, keepdims=False)
    my_count = lax.dynamic_index_in_dim(counts, my_holder, 0, keepdims=False)
    slot_ids = jnp.arange(targets.shape[1], dtype=jnp.int32)
    live_slots = (slot_ids < my_count).astype(jnp.float32)
    my_integrals = integrals[0]
    width = my_tile.shape[3]
    portion = lax.all_gather(my_tile, "blk", axis=0, tiled=True)
    flat_rows = portion.reshape(-1, width)
    result = jnp.einsum("rc,kac->rka", flat_rows, my_integrals, preferred_element_type=jnp.float32)
    partial_value = result.reshape(
        portion.shape[0], portion.shape[1], my_integrals.shape[0], my_integrals.shape[1]
    )
    shaped = (partial_value * live_slots[None, None, :, None]).astype(jnp.bfloat16)
    received = lax.all_to_all(
        lax.all_to_all(shaped, "wide", split_axis=1, concat_axis=2, tiled=True),
        "blk",
        split_axis=0,
        concat_axis=3,
        tiled=True,
    )
    slot_targets = jnp.take(targets, holder, axis=0).reshape(-1)
    window_ids = jnp.arange(wide_count, dtype=jnp.int32)
    selector = (slot_targets[None, :] == window_ids[:, None]).astype(jnp.bfloat16)
    ladder = jnp.einsum("ps,ijsa->pija", selector, received, preferred_element_type=jnp.float32)
    return ladder.astype(jnp.bfloat16)


def solution(mesh):
    few = mesh.shape["wide"] == 8 and mesh.shape["blk"] == 4
    placed = (P("blk", "wide", None, None), P("wide", None, "blk", None), P(), P(), P())
    return jax.shard_map(
        body if few else body_large,
        mesh=mesh,
        in_specs=placed,
        out_specs=P(None, "blk", "wide", None),
        check_vma=False,
    )
```

```python
import functools

import jax
import jax.numpy as jnp
from jax import lax
from jax.experimental import pallas as pl
from jax.experimental.pallas import tpu as pltpu
from jax.sharding import PartitionSpec as P

MIB = 1 << 20
KERNEL_VMEM = 16 * MIB
CONTRACT_VMEM = 20 * MIB
HOLD_VMEM = 44 * MIB
SMEM = pl.BlockSpec(memory_space=pltpu.SMEM)


def find_tile(owner_ref, slot):
    def step(q, found):
        return jnp.where(owner_ref[q] == slot, q, found)

    return lax.fori_loop(0, owner_ref.shape[0], step, jnp.int32(0))


def select_kernel(rows, groups, owner_ref, amp_ref, *rest):
    outs, pick_ref = rest[:-1], rest[-1]
    tiles = owner_ref.shape[0]

    @pl.when(pl.program_id(0) == 0)
    def _():
        me = lax.axis_index("wide")
        shape = pick_ref.shape
        out_row = lax.broadcasted_iota(jnp.int32, shape, 0)
        in_row = lax.broadcasted_iota(jnp.int32, shape, 1)
        slot = lax.bitwise_xor(out_row // rows, me)
        tile = in_row % tiles
        place = jnp.zeros(shape, jnp.int32)
        for q in range(tiles):
            place = jnp.where(tile == q, owner_ref[q], place)
        chosen = (place == slot) & (out_row % rows == in_row // tiles)
        pick_ref[...] = jnp.where(chosen, 1.0, 0.0).astype(pick_ref.dtype)

    moved = jnp.dot(pick_ref[...], amp_ref[...], preferred_element_type=jnp.float32)
    moved = moved.astype(amp_ref.dtype)
    for group, out in zip(groups, outs):
        for at, m in enumerate(group):
            out[at * rows : (at + 1) * rows] = moved[m * rows : (m + 1) * rows]


def select(amplitudes, owner, groups):
    i, j, tiles, width = amplitudes.shape
    rows = i * j
    wide = sum(map(len, groups))
    block = min(width, 1024)
    return pl.pallas_call(
        functools.partial(select_kernel, rows, groups),
        grid=(width // block,),
        in_specs=[SMEM, pl.BlockSpec((rows * tiles, block), lambda c: (0, c))],
        out_specs=[pl.BlockSpec((len(g) * rows, block), lambda c: (0, c)) for g in groups],
        out_shape=[jax.ShapeDtypeStruct((len(g) * rows, width), amplitudes.dtype) for g in groups],
        scratch_shapes=[pltpu.VMEM((wide * rows, rows * tiles), amplitudes.dtype)],
        compiler_params=pltpu.CompilerParams(vmem_limit_bytes=KERNEL_VMEM),
        cost_estimate=pl.CostEstimate(
            flops=2 * wide * rows * rows * tiles * width,
            bytes_accessed=4 * rows * tiles * width,
            transcendentals=0,
        ),
        name="select_tiles",
    )(owner, amplitudes.reshape(rows * tiles, width))


def hold_kernel(value_ref, held_ref, sem):
    copy = pltpu.make_async_copy(value_ref, held_ref, sem)
    copy.start()
    copy.wait()


def hold(value):
    return pl.pallas_call(
        hold_kernel,
        in_specs=[pl.BlockSpec(memory_space=pl.ANY)],
        out_specs=pl.BlockSpec(memory_space=pltpu.VMEM),
        out_shape=jax.ShapeDtypeStruct(value.shape, value.dtype),
        scratch_shapes=[pltpu.SemaphoreType.DMA],
        compiler_params=pltpu.CompilerParams(vmem_limit_bytes=HOLD_VMEM),
        name="hold_integrals",
    )(value)


def contract_kernel(count, block, *refs):
    parts, integrals = refs[:count], refs[count : count + 2]
    outs, rows_ref, sems = refs[count + 2 : -2], refs[-2], refs[-1]
    rows = rows_ref.shape[0] // count
    partners, ab, _ = integrals[0].shape
    copies = [
        pltpu.make_async_copy(part.at[pl.ds(0, rows)], rows_ref.at[pl.ds(n * rows, rows)], sems.at[n])
        for n, part in enumerate(parts)
    ]
    for copy in copies:
        copy.start()
    for copy in copies:
        copy.wait()
    for source, integ_ref in enumerate(integrals):

        @pl.loop(0, partners * ab // block)
        def _(at):
            k, begin = at // (ab // block), pl.multiple_of(at % (ab // block) * block, block)
            value = lax.dot_general(
                integ_ref[k, pl.ds(begin, block), :],
                rows_ref[...],
                (((1,), (1,)), ((), ())),
                preferred_element_type=jnp.float32,
            ).T.astype(jnp.bfloat16)
            column = pl.multiple_of((2 * k + source) * ab + begin, block)
            first = 0
            for out in outs:
                out[:, pl.ds(column, block)] = value[first : first + out.shape[0]]
                first += out.shape[0]


def contract(parts, rows, out_rows, own, other):
    width = parts[0].shape[1]
    partners, ab, _ = own.shape
    count = len(parts)
    vmem = pl.BlockSpec(memory_space=pltpu.VMEM)
    return pl.pallas_call(
        functools.partial(contract_kernel, count, min(ab, 512)),
        in_specs=[pl.BlockSpec(memory_space=pl.ANY)] * count + [vmem, vmem],
        out_specs=[vmem] * len(out_rows),
        out_shape=[
            jax.ShapeDtypeStruct((each, partners * 2 * ab), jnp.bfloat16) for each in out_rows
        ],
        scratch_shapes=[
            pltpu.VMEM((count * rows, width), parts[0].dtype),
            pltpu.SemaphoreType.DMA((count,)),
        ],
        compiler_params=pltpu.CompilerParams(vmem_limit_bytes=CONTRACT_VMEM),
        name="contract_rows",
    )(*parts, own, other)


def collect_kernel(partners, rows, places, owner_ref, targets_ref, counts_ref, *rest):
    parts, out_ref, sum_ref = rest[:-2], rest[-2], rest[-1]
    me, mine = lax.axis_index("wide"), lax.axis_index("blk")
    ab = parts[0].shape[1] // (2 * partners)
    sum_ref[...] = jnp.zeros_like(sum_ref)
    for m in range(len(places) // 2):
        tile = find_tile(owner_ref, lax.bitwise_xor(me, m))
        live = counts_ref[tile]
        for k in range(partners):
            target = targets_ref[tile, k]

            @pl.when(k < live)
            def _():
                for n in range(4):
                    part, first = places[2 * m + n // 2]
                    begin = pl.multiple_of(lax.bitwise_xor(mine, n) * ab, 128)
                    column = (2 * k + n % 2) * ab
                    value = parts[part][first : first + rows, column : column + ab]
                    sum_ref[target, :, pl.ds(begin, ab)] += value.astype(jnp.float32)

    outer, inner = out_ref.shape[1:3]
    for i in range(outer):
        out_ref[:, i] = sum_ref[:, i * inner : (i + 1) * inner, :].astype(out_ref.dtype)


def collect(parts, places, owner, targets, counts, shape):
    partners, rows = targets.shape[1], shape[1] * shape[2]
    return pl.pallas_call(
        functools.partial(collect_kernel, partners, rows, places),
        in_specs=[SMEM, SMEM, SMEM] + [pl.BlockSpec(memory_space=pltpu.VMEM)] * len(parts),
        out_specs=pl.BlockSpec(memory_space=pltpu.VMEM),
        out_shape=jax.ShapeDtypeStruct(shape, jnp.bfloat16),
        scratch_shapes=[pltpu.VMEM((shape[0], rows, shape[3]), jnp.float32)],
        compiler_params=pltpu.CompilerParams(vmem_limit_bytes=KERNEL_VMEM),
        name="collect_targets",
    )(owner, targets, counts, *parts)


def after(value, earlier):
    return lax.optimization_barrier((value, *earlier))[0] if earlier else value


def body(amplitudes, integrals, owner, targets, counts):
    wide = lax.axis_size("wide")
    i, j, tiles, width = amplitudes.shape
    rows = i * j
    own = integrals[0]
    done = {}

    def step(name, value, axis, mask, *earlier):
        pairs = [(s, s ^ mask) for s in range(lax.axis_size(axis))]
        value = done[value] if isinstance(value, str) else value
        done[name] = lax.ppermute(after(value, [done[e] for e in earlier]), axis, pairs)

    def chip(m, *earlier):
        step(f"chip{m}", done[f"to{m}"][:rows], "blk", 2, *earlier)

    def product(parts, out_rows, *earlier):
        parts = [done[name] for name in parts]
        parts[0] = after(parts[0], [done[e] for e in earlier])
        return contract(parts, rows, out_rows, done["own"], done["other"])

    def near_far(masks, *earlier):
        parts = [f"{at}{m}" for at in ("to", "chip") for m in masks]
        made = product(parts, [rows] * len(masks) + [rows * len(masks)], *earlier)
        done.update(zip([f"near{m}" for m in masks], made))
        return made[-1]

    def swap_far(name, value, masks, *earlier):
        step(name, value, "blk", 2, *earlier)
        for at, m in enumerate(masks):
            done[f"far{m}"] = done[name][at * rows : (at + 1) * rows]

    def back(m, *earlier):
        both = jnp.concatenate([done[f"near{m}"], done[f"far{m}"]])
        step(f"from{m}", both, "wide", m, *earlier)

    groups = ((0,), (1,), (2,), (3,), (4, 5), (6,), (7,))
    done["to0"], s1, s2, s3, s45, s6, s7 = select(amplitudes, owner, groups)
    step("other", own, "blk", 1)
    step("to4", s45, "wide", 4)
    chip(0, "other")
    step("to1", s1, "wide", 1, "other")
    done["own"] = hold(after(own, [done["other"]]))
    chip(1, "own")
    step("to2", s2, "wide", 2, "to1")
    step("to6", s6, "wide", 6, "to4", "chip1")
    step("to5", done["to4"][rows:], "wide", 1, "chip1", "chip0")
    chip(4, "chip1")
    chip(5, "to6", "to2")
    step("to7", s7, "wide", 7, "to5")
    (done["made45"],) = product(("to4", "chip4", "to5", "chip5"), [4 * rows])

    step("from4", "made45", "wide", 4)
    step("to3", s3, "wide", 3, "chip4")
    chip(6, "chip5")
    chip(7, "made45")
    far = near_far((6, 7), "chip6")
    swap_far("swap67", far, (6, 7))
    chip(2, "chip5")
    chip(3, "chip7")
    far = near_far((0, 1, 2, 3), "near6")
    swap_far("swap0123", far, (0, 1, 2, 3))
    step("from5", done["from4"][2 * rows :], "wide", 1)
    back(6)
    back(7)
    back(1)
    back(2)
    back(3)
    far45 = jnp.concatenate([done["from4"][rows : 2 * rows], done["from5"][rows:]])
    step("swap45", far45, "blk", 2)
    parts = [done["near0"], done["swap0123"]] + [done[f"from{m}"] for m in range(1, wide)]
    parts += [done["swap45"]]
    places = [(0, 0), (1, 0)]
    for m in range(1, wide):
        places += [(m + 1, 0), (m + 1, rows) if m not in (4, 5) else (wide + 1, (m - 4) * rows)]
    shape = (wide, i, j, lax.axis_size("blk") * own.shape[1])
    return collect(parts, places, owner, targets, counts, shape)


def body_large(amplitudes, integrals, owner, targets, counts):
    wide_count = lax.axis_size("wide")
    my_index = lax.axis_index("wide")
    tile_ids = jnp.arange(owner.shape[0], dtype=jnp.int32)
    holder = jnp.sum(jnp.where(owner[None, :] == tile_ids[:, None], tile_ids[None, :], 0), axis=1)
    ordered = jnp.take(amplitudes, holder, axis=2)
    my_tile = lax.all_to_all(ordered, "wide", split_axis=2, concat_axis=1, tiled=True)
    my_holder = lax.dynamic_index_in_dim(holder, my_index, 0, keepdims=False)
    my_count = lax.dynamic_index_in_dim(counts, my_holder, 0, keepdims=False)
    slot_ids = jnp.arange(targets.shape[1], dtype=jnp.int32)
    live_slots = (slot_ids < my_count).astype(jnp.float32)
    my_integrals = integrals[0]
    width = my_tile.shape[3]
    portion = lax.all_gather(my_tile, "blk", axis=0, tiled=True)
    flat_rows = portion.reshape(-1, width)
    result = jnp.einsum("rc,kac->rka", flat_rows, my_integrals, preferred_element_type=jnp.float32)
    partial_value = result.reshape(
        portion.shape[0], portion.shape[1], my_integrals.shape[0], my_integrals.shape[1]
    )
    shaped = (partial_value * live_slots[None, None, :, None]).astype(jnp.bfloat16)
    received = lax.all_to_all(
        lax.all_to_all(shaped, "wide", split_axis=1, concat_axis=2, tiled=True),
        "blk",
        split_axis=0,
        concat_axis=3,
        tiled=True,
    )
    slot_targets = jnp.take(targets, holder, axis=0).reshape(-1)
    window_ids = jnp.arange(wide_count, dtype=jnp.int32)
    selector = (slot_targets[None, :] == window_ids[:, None]).astype(jnp.bfloat16)
    ladder = jnp.einsum("ps,ijsa->pija", selector, received, preferred_element_type=jnp.float32)
    return ladder.astype(jnp.bfloat16)


def solution(mesh):
    few = mesh.shape["wide"] == 8 and mesh.shape["blk"] == 4
    placed = (P("blk", "wide", None, None), P("wide", None, "blk", None), P(), P(), P())
    return jax.shard_map(
        body if few else body_large,
        mesh=mesh,
        in_specs=placed,
        out_specs=P(None, "blk", "wide", None),
        check_vma=False,
    )
```

```python
import functools

import jax
import jax.numpy as jnp
from jax import lax
from jax.experimental import pallas as pl
from jax.experimental.pallas import tpu as pltpu
from jax.sharding import PartitionSpec as P

MIB = 1 << 20
KERNEL_VMEM = 16 * MIB
CONTRACT_VMEM = 20 * MIB
HOLD_VMEM = 44 * MIB
SMEM = pl.BlockSpec(memory_space=pltpu.SMEM)


def find_tile(owner_ref, slot):
    def step(q, found):
        return jnp.where(owner_ref[q] == slot, q, found)

    return lax.fori_loop(0, owner_ref.shape[0], step, jnp.int32(0))


def select_kernel(rows, groups, owner_ref, amp_ref, *rest):
    outs, pick_ref = rest[:-1], rest[-1]
    tiles = owner_ref.shape[0]

    @pl.when(pl.program_id(0) == 0)
    def _():
        me = lax.axis_index("wide")
        shape = pick_ref.shape
        out_row = lax.broadcasted_iota(jnp.int32, shape, 0)
        in_row = lax.broadcasted_iota(jnp.int32, shape, 1)
        slot = lax.bitwise_xor(out_row // rows, me)
        tile = in_row % tiles
        place = jnp.zeros(shape, jnp.int32)
        for q in range(tiles):
            place = jnp.where(tile == q, owner_ref[q], place)
        chosen = (place == slot) & (out_row % rows == in_row // tiles)
        pick_ref[...] = jnp.where(chosen, 1.0, 0.0).astype(pick_ref.dtype)

    moved = jnp.dot(pick_ref[...], amp_ref[...], preferred_element_type=jnp.float32)
    moved = moved.astype(amp_ref.dtype)
    for group, out in zip(groups, outs):
        for at, m in enumerate(group):
            out[at * rows : (at + 1) * rows] = moved[m * rows : (m + 1) * rows]


def select(amplitudes, owner, groups):
    i, j, tiles, width = amplitudes.shape
    rows = i * j
    wide = sum(map(len, groups))
    block = min(width, 1024)
    return pl.pallas_call(
        functools.partial(select_kernel, rows, groups),
        grid=(width // block,),
        in_specs=[SMEM, pl.BlockSpec((rows * tiles, block), lambda c: (0, c))],
        out_specs=[pl.BlockSpec((len(g) * rows, block), lambda c: (0, c)) for g in groups],
        out_shape=[jax.ShapeDtypeStruct((len(g) * rows, width), amplitudes.dtype) for g in groups],
        scratch_shapes=[pltpu.VMEM((wide * rows, rows * tiles), amplitudes.dtype)],
        compiler_params=pltpu.CompilerParams(vmem_limit_bytes=KERNEL_VMEM),
        cost_estimate=pl.CostEstimate(
            flops=2 * wide * rows * rows * tiles * width,
            bytes_accessed=4 * rows * tiles * width,
            transcendentals=0,
        ),
        name="select_tiles",
    )(owner, amplitudes.reshape(rows * tiles, width))


def hold_kernel(value_ref, held_ref, sem):
    copy = pltpu.make_async_copy(value_ref, held_ref, sem)
    copy.start()
    copy.wait()


def hold(value):
    return pl.pallas_call(
        hold_kernel,
        in_specs=[pl.BlockSpec(memory_space=pl.ANY)],
        out_specs=pl.BlockSpec(memory_space=pltpu.VMEM),
        out_shape=jax.ShapeDtypeStruct(value.shape, value.dtype),
        scratch_shapes=[pltpu.SemaphoreType.DMA],
        compiler_params=pltpu.CompilerParams(vmem_limit_bytes=HOLD_VMEM),
        name="hold_integrals",
    )(value)


def contract_kernel(count, block, *refs):
    parts, integrals = refs[:count], refs[count : count + 2]
    outs, rows_ref, sems = refs[count + 2 : -2], refs[-2], refs[-1]
    rows = rows_ref.shape[0] // count
    partners, ab, _ = integrals[0].shape
    copies = [
        pltpu.make_async_copy(part.at[pl.ds(0, rows)], rows_ref.at[pl.ds(n * rows, rows)], sems.at[n])
        for n, part in enumerate(parts)
    ]
    for copy in copies:
        copy.start()
    for copy in copies:
        copy.wait()
    for source, integ_ref in enumerate(integrals):

        @pl.loop(0, partners * ab // block)
        def _(at):
            k, begin = at // (ab // block), pl.multiple_of(at % (ab // block) * block, block)
            value = lax.dot_general(
                integ_ref[k, pl.ds(begin, block), :],
                rows_ref[...],
                (((1,), (1,)), ((), ())),
                preferred_element_type=jnp.float32,
            ).T.astype(jnp.bfloat16)
            column = pl.multiple_of((2 * k + source) * ab + begin, block)
            first = 0
            for out in outs:
                out[:, pl.ds(column, block)] = value[first : first + out.shape[0]]
                first += out.shape[0]


def contract(parts, rows, out_rows, own, other):
    width = parts[0].shape[1]
    partners, ab, _ = own.shape
    count = len(parts)
    vmem = pl.BlockSpec(memory_space=pltpu.VMEM)
    return pl.pallas_call(
        functools.partial(contract_kernel, count, min(ab, 512)),
        in_specs=[pl.BlockSpec(memory_space=pl.ANY)] * count + [vmem, vmem],
        out_specs=[vmem] * len(out_rows),
        out_shape=[
            jax.ShapeDtypeStruct((each, partners * 2 * ab), jnp.bfloat16) for each in out_rows
        ],
        scratch_shapes=[
            pltpu.VMEM((count * rows, width), parts[0].dtype),
            pltpu.SemaphoreType.DMA((count,)),
        ],
        compiler_params=pltpu.CompilerParams(vmem_limit_bytes=CONTRACT_VMEM),
        name="contract_rows",
    )(*parts, own, other)


def collect_kernel(partners, rows, places, owner_ref, targets_ref, counts_ref, *rest):
    parts, out_ref, sum_ref = rest[:-2], rest[-2], rest[-1]
    me, mine = lax.axis_index("wide"), lax.axis_index("blk")
    ab = parts[0].shape[1] // (2 * partners)
    sum_ref[...] = jnp.zeros_like(sum_ref)
    for m in range(len(places) // 2):
        tile = find_tile(owner_ref, lax.bitwise_xor(me, m))
        live = counts_ref[tile]
        for k in range(partners):
            target = targets_ref[tile, k]

            @pl.when(k < live)
            def _():
                for n in range(4):
                    part, first = places[2 * m + n // 2]
                    begin = pl.multiple_of(lax.bitwise_xor(mine, n) * ab, 128)
                    column = (2 * k + n % 2) * ab
                    value = parts[part][first : first + rows, column : column + ab]
                    sum_ref[target, :, pl.ds(begin, ab)] += value.astype(jnp.float32)

    outer, inner = out_ref.shape[1:3]
    for i in range(outer):
        out_ref[:, i] = sum_ref[:, i * inner : (i + 1) * inner, :].astype(out_ref.dtype)


def collect(parts, places, owner, targets, counts, shape):
    partners, rows = targets.shape[1], shape[1] * shape[2]
    return pl.pallas_call(
        functools.partial(collect_kernel, partners, rows, places),
        in_specs=[SMEM, SMEM, SMEM] + [pl.BlockSpec(memory_space=pltpu.VMEM)] * len(parts),
        out_specs=pl.BlockSpec(memory_space=pltpu.VMEM),
        out_shape=jax.ShapeDtypeStruct(shape, jnp.bfloat16),
        scratch_shapes=[pltpu.VMEM((shape[0], rows, shape[3]), jnp.float32)],
        compiler_params=pltpu.CompilerParams(vmem_limit_bytes=KERNEL_VMEM),
        name="collect_targets",
    )(owner, targets, counts, *parts)


def after(value, earlier):
    return lax.optimization_barrier((value, *earlier))[0] if earlier else value


def body(amplitudes, integrals, owner, targets, counts):
    wide = lax.axis_size("wide")
    i, j, tiles, width = amplitudes.shape
    rows = i * j
    own = integrals[0]
    done = {}

    def step(name, value, axis, mask, *earlier):
        pairs = [(s, s ^ mask) for s in range(lax.axis_size(axis))]
        value = done[value] if isinstance(value, str) else value
        done[name] = lax.ppermute(after(value, [done[e] for e in earlier]), axis, pairs)

    def chip(m, *earlier):
        step(f"chip{m}", done[f"to{m}"][:rows], "blk", 2, *earlier)

    def product(parts, out_rows, *earlier):
        parts = [done[name] for name in parts]
        parts[0] = after(parts[0], [done[e] for e in earlier])
        return contract(parts, rows, out_rows, done["own"], done["other"])

    def near_far(masks, *earlier):
        parts = [f"{at}{m}" for at in ("to", "chip") for m in masks]
        made = product(parts, [rows] * len(masks) + [rows * len(masks)], *earlier)
        done.update(zip([f"near{m}" for m in masks], made))
        return made[-1]

    def swap_far(name, value, masks, *earlier):
        step(name, value, "blk", 2, *earlier)
        for at, m in enumerate(masks):
            done[f"far{m}"] = done[name][at * rows : (at + 1) * rows]

    def back(m, *earlier):
        both = jnp.concatenate([done[f"near{m}"], done[f"far{m}"]])
        step(f"from{m}", both, "wide", m, *earlier)

    groups = ((0,), (1,), (2,), (3,), (4, 5), (6,), (7,))
    done["to0"], s1, s2, s3, s45, s6, s7 = select(amplitudes, owner, groups)
    step("other", own, "blk", 1)
    step("to4", s45, "wide", 4)
    chip(0, "other")
    step("to1", s1, "wide", 1, "other")
    done["own"] = hold(after(own, [done["other"]]))
    chip(1, "own")
    step("to2", s2, "wide", 2, "to1")
    step("to6", s6, "wide", 6, "to4", "chip1")
    step("to5", done["to4"][rows:], "wide", 1, "chip1", "chip0")
    chip(4, "chip1")
    far01 = near_far((0, 1), "chip0")
    chip(5, "to6", "to2", "near0")
    step("to7", s7, "wide", 7, "chip4")
    (done["made45"],) = product(("to4", "chip4", "to5", "chip5"), [4 * rows])

    step("from4", "made45", "wide", 4)
    step("to3", s3, "wide", 3, "to5")
    chip(6, "chip5")
    chip(7, "made45")
    far = near_far((6, 7), "chip6", "to3")
    swap_far("swap67", far, (6, 7))
    swap_far("swap01", far01, (0, 1), "near6")
    chip(2, "chip6")
    chip(3, "chip7")
    far = near_far((2, 3), "near6")
    swap_far("swap23", far, (2, 3))
    step("from5", done["from4"][2 * rows :], "wide", 1)
    back(6)
    back(7)
    back(1)
    back(2)
    back(3)
    far45 = jnp.concatenate([done["from4"][rows : 2 * rows], done["from5"][rows:]])
    step("swap45", far45, "blk", 2)
    parts = [done["near0"], done["swap01"]] + [done[f"from{m}"] for m in range(1, wide)]
    parts += [done["swap45"]]
    places = [(0, 0), (1, 0)]
    for m in range(1, wide):
        places += [(m + 1, 0), (m + 1, rows) if m not in (4, 5) else (wide + 1, (m - 4) * rows)]
    shape = (wide, i, j, lax.axis_size("blk") * own.shape[1])
    return collect(parts, places, owner, targets, counts, shape)


def body_large(amplitudes, integrals, owner, targets, counts):
    wide_count = lax.axis_size("wide")
    my_index = lax.axis_index("wide")
    tile_ids = jnp.arange(owner.shape[0], dtype=jnp.int32)
    holder = jnp.sum(jnp.where(owner[None, :] == tile_ids[:, None], tile_ids[None, :], 0), axis=1)
    ordered = jnp.take(amplitudes, holder, axis=2)
    my_tile = lax.all_to_all(ordered, "wide", split_axis=2, concat_axis=1, tiled=True)
    my_holder = lax.dynamic_index_in_dim(holder, my_index, 0, keepdims=False)
    my_count = lax.dynamic_index_in_dim(counts, my_holder, 0, keepdims=False)
    slot_ids = jnp.arange(targets.shape[1], dtype=jnp.int32)
    live_slots = (slot_ids < my_count).astype(jnp.float32)
    my_integrals = integrals[0]
    width = my_tile.shape[3]
    portion = lax.all_gather(my_tile, "blk", axis=0, tiled=True)
    flat_rows = portion.reshape(-1, width)
    result = jnp.einsum("rc,kac->rka", flat_rows, my_integrals, preferred_element_type=jnp.float32)
    partial_value = result.reshape(
        portion.shape[0], portion.shape[1], my_integrals.shape[0], my_integrals.shape[1]
    )
    shaped = (partial_value * live_slots[None, None, :, None]).astype(jnp.bfloat16)
    received = lax.all_to_all(
        lax.all_to_all(shaped, "wide", split_axis=1, concat_axis=2, tiled=True),
        "blk",
        split_axis=0,
        concat_axis=3,
        tiled=True,
    )
    slot_targets = jnp.take(targets, holder, axis=0).reshape(-1)
    window_ids = jnp.arange(wide_count, dtype=jnp.int32)
    selector = (slot_targets[None, :] == window_ids[:, None]).astype(jnp.bfloat16)
    ladder = jnp.einsum("ps,ijsa->pija", selector, received, preferred_element_type=jnp.float32)
    return ladder.astype(jnp.bfloat16)


def solution(mesh):
    few = mesh.shape["wide"] == 8 and mesh.shape["blk"] == 4
    placed = (P("blk", "wide", None, None), P("wide", None, "blk", None), P(), P(), P())
    return jax.shard_map(
        body if few else body_large,
        mesh=mesh,
        in_specs=placed,
        out_specs=P(None, "blk", "wide", None),
        check_vma=False,
    )
```

```python
import functools

import jax
import jax.numpy as jnp
from jax import lax
from jax.experimental import pallas as pl
from jax.experimental.pallas import tpu as pltpu
from jax.sharding import PartitionSpec as P

MIB = 1 << 20
KERNEL_VMEM = 16 * MIB
CONTRACT_VMEM = 20 * MIB
HOLD_VMEM = 44 * MIB
SMEM = pl.BlockSpec(memory_space=pltpu.SMEM)


def find_tile(owner_ref, slot):
    def step(q, found):
        return jnp.where(owner_ref[q] == slot, q, found)

    return lax.fori_loop(0, owner_ref.shape[0], step, jnp.int32(0))


def select_kernel(rows, groups, owner_ref, amp_ref, *rest):
    outs, pick_ref = rest[:-1], rest[-1]
    tiles = owner_ref.shape[0]

    @pl.when(pl.program_id(0) == 0)
    def _():
        me = lax.axis_index("wide")
        shape = pick_ref.shape
        out_row = lax.broadcasted_iota(jnp.int32, shape, 0)
        in_row = lax.broadcasted_iota(jnp.int32, shape, 1)
        slot = lax.bitwise_xor(out_row // rows, me)
        tile = in_row % tiles
        place = jnp.zeros(shape, jnp.int32)
        for q in range(tiles):
            place = jnp.where(tile == q, owner_ref[q], place)
        chosen = (place == slot) & (out_row % rows == in_row // tiles)
        pick_ref[...] = jnp.where(chosen, 1.0, 0.0).astype(pick_ref.dtype)

    moved = jnp.dot(pick_ref[...], amp_ref[...], preferred_element_type=jnp.float32)
    moved = moved.astype(amp_ref.dtype)
    for group, out in zip(groups, outs):
        for at, m in enumerate(group):
            out[at * rows : (at + 1) * rows] = moved[m * rows : (m + 1) * rows]


def select(amplitudes, owner, groups):
    i, j, tiles, width = amplitudes.shape
    rows = i * j
    wide = sum(map(len, groups))
    block = min(width, 1024)
    return pl.pallas_call(
        functools.partial(select_kernel, rows, groups),
        grid=(width // block,),
        in_specs=[SMEM, pl.BlockSpec((rows * tiles, block), lambda c: (0, c))],
        out_specs=[pl.BlockSpec((len(g) * rows, block), lambda c: (0, c)) for g in groups],
        out_shape=[jax.ShapeDtypeStruct((len(g) * rows, width), amplitudes.dtype) for g in groups],
        scratch_shapes=[pltpu.VMEM((wide * rows, rows * tiles), amplitudes.dtype)],
        compiler_params=pltpu.CompilerParams(vmem_limit_bytes=KERNEL_VMEM),
        cost_estimate=pl.CostEstimate(
            flops=2 * wide * rows * rows * tiles * width,
            bytes_accessed=4 * rows * tiles * width,
            transcendentals=0,
        ),
        name="select_tiles",
    )(owner, amplitudes.reshape(rows * tiles, width))


def hold_kernel(value_ref, held_ref, sem):
    copy = pltpu.make_async_copy(value_ref, held_ref, sem)
    copy.start()
    copy.wait()


def hold(value):
    return pl.pallas_call(
        hold_kernel,
        in_specs=[pl.BlockSpec(memory_space=pl.ANY)],
        out_specs=pl.BlockSpec(memory_space=pltpu.VMEM),
        out_shape=jax.ShapeDtypeStruct(value.shape, value.dtype),
        scratch_shapes=[pltpu.SemaphoreType.DMA],
        compiler_params=pltpu.CompilerParams(vmem_limit_bytes=HOLD_VMEM),
        name="hold_integrals",
    )(value)


def contract_kernel(count, block, *refs):
    parts, integrals = refs[:count], refs[count : count + 2]
    outs, rows_ref, sems = refs[count + 2 : -2], refs[-2], refs[-1]
    rows = rows_ref.shape[0] // count
    partners, ab, _ = integrals[0].shape
    copies = [
        pltpu.make_async_copy(part.at[pl.ds(0, rows)], rows_ref.at[pl.ds(n * rows, rows)], sems.at[n])
        for n, part in enumerate(parts)
    ]
    for copy in copies:
        copy.start()
    for copy in copies:
        copy.wait()
    for source, integ_ref in enumerate(integrals):

        @pl.loop(0, partners * ab // block)
        def _(at):
            k, begin = at // (ab // block), pl.multiple_of(at % (ab // block) * block, block)
            value = lax.dot_general(
                integ_ref[k, pl.ds(begin, block), :],
                rows_ref[...],
                (((1,), (1,)), ((), ())),
                preferred_element_type=jnp.float32,
            ).T.astype(jnp.bfloat16)
            column = pl.multiple_of((2 * k + source) * ab + begin, block)
            first = 0
            for out in outs:
                out[:, pl.ds(column, block)] = value[first : first + out.shape[0]]
                first += out.shape[0]


def contract(parts, rows, out_rows, own, other):
    width = parts[0].shape[1]
    partners, ab, _ = own.shape
    count = len(parts)
    vmem = pl.BlockSpec(memory_space=pltpu.VMEM)
    return pl.pallas_call(
        functools.partial(contract_kernel, count, min(ab, 512)),
        in_specs=[pl.BlockSpec(memory_space=pl.ANY)] * count + [vmem, vmem],
        out_specs=[vmem] * len(out_rows),
        out_shape=[
            jax.ShapeDtypeStruct((each, partners * 2 * ab), jnp.bfloat16) for each in out_rows
        ],
        scratch_shapes=[
            pltpu.VMEM((count * rows, width), parts[0].dtype),
            pltpu.SemaphoreType.DMA((count,)),
        ],
        compiler_params=pltpu.CompilerParams(vmem_limit_bytes=CONTRACT_VMEM),
        name="contract_rows",
    )(*parts, own, other)


def collect_kernel(partners, rows, places, owner_ref, targets_ref, counts_ref, *rest):
    parts, out_ref, sum_ref = rest[:-2], rest[-2], rest[-1]
    me, mine = lax.axis_index("wide"), lax.axis_index("blk")
    ab = parts[0].shape[1] // (2 * partners)
    sum_ref[...] = jnp.zeros_like(sum_ref)
    for m in range(len(places) // 2):
        tile = find_tile(owner_ref, lax.bitwise_xor(me, m))
        live = counts_ref[tile]
        for k in range(partners):
            target = targets_ref[tile, k]

            @pl.when(k < live)
            def _():
                for n in range(4):
                    part, first = places[2 * m + n // 2]
                    begin = pl.multiple_of(lax.bitwise_xor(mine, n) * ab, 128)
                    column = (2 * k + n % 2) * ab
                    value = parts[part][first : first + rows, column : column + ab]
                    sum_ref[target, :, pl.ds(begin, ab)] += value.astype(jnp.float32)

    outer, inner = out_ref.shape[1:3]
    for i in range(outer):
        out_ref[:, i] = sum_ref[:, i * inner : (i + 1) * inner, :].astype(out_ref.dtype)


def collect(parts, places, owner, targets, counts, shape):
    partners, rows = targets.shape[1], shape[1] * shape[2]
    return pl.pallas_call(
        functools.partial(collect_kernel, partners, rows, places),
        in_specs=[SMEM, SMEM, SMEM] + [pl.BlockSpec(memory_space=pltpu.VMEM)] * len(parts),
        out_specs=pl.BlockSpec(memory_space=pltpu.VMEM),
        out_shape=jax.ShapeDtypeStruct(shape, jnp.bfloat16),
        scratch_shapes=[pltpu.VMEM((shape[0], rows, shape[3]), jnp.float32)],
        compiler_params=pltpu.CompilerParams(vmem_limit_bytes=KERNEL_VMEM),
        name="collect_targets",
    )(owner, targets, counts, *parts)


def after(value, earlier):
    return lax.optimization_barrier((value, *earlier))[0] if earlier else value


def body(amplitudes, integrals, owner, targets, counts):
    wide = lax.axis_size("wide")
    i, j, tiles, width = amplitudes.shape
    rows = i * j
    own = integrals[0]
    done = {}

    def step(name, value, axis, mask, *earlier):
        pairs = [(s, s ^ mask) for s in range(lax.axis_size(axis))]
        value = done[value] if isinstance(value, str) else value
        done[name] = lax.ppermute(after(value, [done[e] for e in earlier]), axis, pairs)

    def chip(m, *earlier):
        step(f"chip{m}", done[f"to{m}"][:rows], "blk", 2, *earlier)

    def product(parts, out_rows, *earlier):
        parts = [done[name] for name in parts]
        parts[0] = after(parts[0], [done[e] for e in earlier])
        return contract(parts, rows, out_rows, done["own"], done["other"])

    def near_far(masks, *earlier):
        parts = [f"{at}{m}" for at in ("to", "chip") for m in masks]
        made = product(parts, [rows] * len(masks) + [rows * len(masks)], *earlier)
        done.update(zip([f"near{m}" for m in masks], made))
        return made[-1]

    def swap_far(name, value, masks, *earlier):
        step(name, value, "blk", 2, *earlier)
        for at, m in enumerate(masks):
            done[f"far{m}"] = done[name][at * rows : (at + 1) * rows]

    def back(m, *earlier):
        both = jnp.concatenate([done[f"near{m}"], done[f"far{m}"]])
        step(f"from{m}", both, "wide", m, *earlier)

    groups = ((0,), (1,), (2,), (3,), (4, 5), (6,), (7,))
    done["to0"], s1, s2, s3, s45, s6, s7 = select(amplitudes, owner, groups)
    step("other", own, "blk", 1)
    step("to2", s2, "wide", 2)
    step("to3", s3, "wide", 3)
    step("to4", s45, "wide", 4)
    chip(0, "other")
    step("to1", s1, "wide", 1, "other")
    done["own"] = hold(after(own, [done["other"]]))
    chip(2, "other")
    chip(1, "other")
    chip(3, "other")
    step("to6", s6, "wide", 6, "to4", "chip0")
    step("to5", done["to4"][rows:], "wide", 1, "chip2")
    chip(4, "chip2")
    far = near_far((0, 1, 2, 3), "chip0")
    chip(5, "to6", "near0")
    step("to7", s7, "wide", 7, "chip4")
    (done["made45"],) = product(("to4", "chip4", "to5", "chip5"), [4 * rows])

    step("from4", "made45", "wide", 4)
    swap_far("swap0123", far, (0, 1, 2, 3), "chip5")
    chip(6, "chip5")
    chip(7, "made45")
    back(1)
    back(2)
    back(3)
    far = near_far((6, 7), "chip6")
    swap_far("swap67", far, (6, 7))
    step("from5", done["from4"][2 * rows :], "wide", 1)
    back(6)
    back(7)
    far45 = jnp.concatenate([done["from4"][rows : 2 * rows], done["from5"][rows:]])
    step("swap45", far45, "blk", 2)
    parts = [done["near0"], done["swap0123"]] + [done[f"from{m}"] for m in range(1, wide)]
    parts += [done["swap45"]]
    places = [(0, 0), (1, 0)]
    for m in range(1, wide):
        places += [(m + 1, 0), (m + 1, rows) if m not in (4, 5) else (wide + 1, (m - 4) * rows)]
    shape = (wide, i, j, lax.axis_size("blk") * own.shape[1])
    return collect(parts, places, owner, targets, counts, shape)


def body_large(amplitudes, integrals, owner, targets, counts):
    wide_count = lax.axis_size("wide")
    my_index = lax.axis_index("wide")
    tile_ids = jnp.arange(owner.shape[0], dtype=jnp.int32)
    holder = jnp.sum(jnp.where(owner[None, :] == tile_ids[:, None], tile_ids[None, :], 0), axis=1)
    ordered = jnp.take(amplitudes, holder, axis=2)
    my_tile = lax.all_to_all(ordered, "wide", split_axis=2, concat_axis=1, tiled=True)
    my_holder = lax.dynamic_index_in_dim(holder, my_index, 0, keepdims=False)
    my_count = lax.dynamic_index_in_dim(counts, my_holder, 0, keepdims=False)
    slot_ids = jnp.arange(targets.shape[1], dtype=jnp.int32)
    live_slots = (slot_ids < my_count).astype(jnp.float32)
    my_integrals = integrals[0]
    width = my_tile.shape[3]
    portion = lax.all_gather(my_tile, "blk", axis=0, tiled=True)
    flat_rows = portion.reshape(-1, width)
    result = jnp.einsum("rc,kac->rka", flat_rows, my_integrals, preferred_element_type=jnp.float32)
    partial_value = result.reshape(
        portion.shape[0], portion.shape[1], my_integrals.shape[0], my_integrals.shape[1]
    )
    shaped = (partial_value * live_slots[None, None, :, None]).astype(jnp.bfloat16)
    received = lax.all_to_all(
        lax.all_to_all(shaped, "wide", split_axis=1, concat_axis=2, tiled=True),
        "blk",
        split_axis=0,
        concat_axis=3,
        tiled=True,
    )
    slot_targets = jnp.take(targets, holder, axis=0).reshape(-1)
    window_ids = jnp.arange(wide_count, dtype=jnp.int32)
    selector = (slot_targets[None, :] == window_ids[:, None]).astype(jnp.bfloat16)
    ladder = jnp.einsum("ps,ijsa->pija", selector, received, preferred_element_type=jnp.float32)
    return ladder.astype(jnp.bfloat16)


def solution(mesh):
    few = mesh.shape["wide"] == 8 and mesh.shape["blk"] == 4
    placed = (P("blk", "wide", None, None), P("wide", None, "blk", None), P(), P(), P())
    return jax.shard_map(
        body if few else body_large,
        mesh=mesh,
        in_specs=placed,
        out_specs=P(None, "blk", "wide", None),
        check_vma=False,
    )
```

```python
import functools

import jax
import jax.numpy as jnp
from jax import lax
from jax.experimental import pallas as pl
from jax.experimental.pallas import tpu as pltpu
from jax.sharding import PartitionSpec as P

MIB = 1 << 20
KERNEL_VMEM = 16 * MIB
CONTRACT_VMEM = 20 * MIB
HOLD_VMEM = 44 * MIB
SMEM = pl.BlockSpec(memory_space=pltpu.SMEM)


def find_tile(owner_ref, slot):
    def step(q, found):
        return jnp.where(owner_ref[q] == slot, q, found)

    return lax.fori_loop(0, owner_ref.shape[0], step, jnp.int32(0))


def select_kernel(rows, groups, owner_ref, amp_ref, *rest):
    outs, pick_ref = rest[:-1], rest[-1]
    tiles = owner_ref.shape[0]

    @pl.when(pl.program_id(0) == 0)
    def _():
        me = lax.axis_index("wide")
        shape = pick_ref.shape
        out_row = lax.broadcasted_iota(jnp.int32, shape, 0)
        in_row = lax.broadcasted_iota(jnp.int32, shape, 1)
        slot = lax.bitwise_xor(out_row // rows, me)
        tile = in_row % tiles
        place = jnp.zeros(shape, jnp.int32)
        for q in range(tiles):
            place = jnp.where(tile == q, owner_ref[q], place)
        chosen = (place == slot) & (out_row % rows == in_row // tiles)
        pick_ref[...] = jnp.where(chosen, 1.0, 0.0).astype(pick_ref.dtype)

    moved = jnp.dot(pick_ref[...], amp_ref[...], preferred_element_type=jnp.float32)
    moved = moved.astype(amp_ref.dtype)
    for group, out in zip(groups, outs):
        for at, m in enumerate(group):
            out[at * rows : (at + 1) * rows] = moved[m * rows : (m + 1) * rows]


def select(amplitudes, owner, groups):
    i, j, tiles, width = amplitudes.shape
    rows = i * j
    wide = sum(map(len, groups))
    block = min(width, 1024)
    return pl.pallas_call(
        functools.partial(select_kernel, rows, groups),
        grid=(width // block,),
        in_specs=[SMEM, pl.BlockSpec((rows * tiles, block), lambda c: (0, c))],
        out_specs=[pl.BlockSpec((len(g) * rows, block), lambda c: (0, c)) for g in groups],
        out_shape=[jax.ShapeDtypeStruct((len(g) * rows, width), amplitudes.dtype) for g in groups],
        scratch_shapes=[pltpu.VMEM((wide * rows, rows * tiles), amplitudes.dtype)],
        compiler_params=pltpu.CompilerParams(vmem_limit_bytes=KERNEL_VMEM),
        cost_estimate=pl.CostEstimate(
            flops=2 * wide * rows * rows * tiles * width,
            bytes_accessed=4 * rows * tiles * width,
            transcendentals=0,
        ),
        name="select_tiles",
    )(owner, amplitudes.reshape(rows * tiles, width))


def hold_kernel(value_ref, held_ref, sem):
    copy = pltpu.make_async_copy(value_ref, held_ref, sem)
    copy.start()
    copy.wait()


def hold(value):
    return pl.pallas_call(
        hold_kernel,
        in_specs=[pl.BlockSpec(memory_space=pl.ANY)],
        out_specs=pl.BlockSpec(memory_space=pltpu.VMEM),
        out_shape=jax.ShapeDtypeStruct(value.shape, value.dtype),
        scratch_shapes=[pltpu.SemaphoreType.DMA],
        compiler_params=pltpu.CompilerParams(vmem_limit_bytes=HOLD_VMEM),
        name="hold_integrals",
    )(value)


def contract_kernel(count, block, *refs):
    parts, integrals = refs[:count], refs[count : count + 2]
    outs, rows_ref, sems = refs[count + 2 : -2], refs[-2], refs[-1]
    rows = rows_ref.shape[0] // count
    partners, ab, _ = integrals[0].shape
    copies = [
        pltpu.make_async_copy(part.at[pl.ds(0, rows)], rows_ref.at[pl.ds(n * rows, rows)], sems.at[n])
        for n, part in enumerate(parts)
    ]
    for copy in copies:
        copy.start()
    for copy in copies:
        copy.wait()
    for source, integ_ref in enumerate(integrals):

        @pl.loop(0, partners * ab // block)
        def _(at):
            k, begin = at // (ab // block), pl.multiple_of(at % (ab // block) * block, block)
            value = lax.dot_general(
                integ_ref[k, pl.ds(begin, block), :],
                rows_ref[...],
                (((1,), (1,)), ((), ())),
                preferred_element_type=jnp.float32,
            ).T.astype(jnp.bfloat16)
            column = pl.multiple_of((2 * k + source) * ab + begin, block)
            first = 0
            for out in outs:
                out[:, pl.ds(column, block)] = value[first : first + out.shape[0]]
                first += out.shape[0]


def contract(parts, rows, out_rows, own, other):
    width = parts[0].shape[1]
    partners, ab, _ = own.shape
    count = len(parts)
    vmem = pl.BlockSpec(memory_space=pltpu.VMEM)
    return pl.pallas_call(
        functools.partial(contract_kernel, count, min(ab, 512)),
        in_specs=[pl.BlockSpec(memory_space=pl.ANY)] * count + [vmem, vmem],
        out_specs=[vmem] * len(out_rows),
        out_shape=[
            jax.ShapeDtypeStruct((each, partners * 2 * ab), jnp.bfloat16) for each in out_rows
        ],
        scratch_shapes=[
            pltpu.VMEM((count * rows, width), parts[0].dtype),
            pltpu.SemaphoreType.DMA((count,)),
        ],
        compiler_params=pltpu.CompilerParams(vmem_limit_bytes=CONTRACT_VMEM),
        name="contract_rows",
    )(*parts, own, other)


def collect_kernel(partners, rows, places, owner_ref, targets_ref, counts_ref, *rest):
    parts, out_ref, sum_ref = rest[:-2], rest[-2], rest[-1]
    me, mine = lax.axis_index("wide"), lax.axis_index("blk")
    ab = parts[0].shape[1] // (2 * partners)
    sum_ref[...] = jnp.zeros_like(sum_ref)
    for m in range(len(places) // 2):
        tile = find_tile(owner_ref, lax.bitwise_xor(me, m))
        live = counts_ref[tile]
        for k in range(partners):
            target = targets_ref[tile, k]

            @pl.when(k < live)
            def _():
                for n in range(4):
                    part, first = places[2 * m + n // 2]
                    begin = pl.multiple_of(lax.bitwise_xor(mine, n) * ab, 128)
                    column = (2 * k + n % 2) * ab
                    value = parts[part][first : first + rows, column : column + ab]
                    sum_ref[target, :, pl.ds(begin, ab)] += value.astype(jnp.float32)

    outer, inner = out_ref.shape[1:3]
    for i in range(outer):
        out_ref[:, i] = sum_ref[:, i * inner : (i + 1) * inner, :].astype(out_ref.dtype)


def collect(parts, places, owner, targets, counts, shape):
    partners, rows = targets.shape[1], shape[1] * shape[2]
    return pl.pallas_call(
        functools.partial(collect_kernel, partners, rows, places),
        in_specs=[SMEM, SMEM, SMEM] + [pl.BlockSpec(memory_space=pltpu.VMEM)] * len(parts),
        out_specs=pl.BlockSpec(memory_space=pltpu.VMEM),
        out_shape=jax.ShapeDtypeStruct(shape, jnp.bfloat16),
        scratch_shapes=[pltpu.VMEM((shape[0], rows, shape[3]), jnp.float32)],
        compiler_params=pltpu.CompilerParams(vmem_limit_bytes=KERNEL_VMEM),
        name="collect_targets",
    )(owner, targets, counts, *parts)


def after(value, earlier):
    return lax.optimization_barrier((value, *earlier))[0] if earlier else value


def body(amplitudes, integrals, owner, targets, counts):
    wide = lax.axis_size("wide")
    i, j, tiles, width = amplitudes.shape
    rows = i * j
    own = integrals[0]
    done = {}

    def step(name, value, axis, mask, *earlier):
        pairs = [(s, s ^ mask) for s in range(lax.axis_size(axis))]
        value = done[value] if isinstance(value, str) else value
        done[name] = lax.ppermute(after(value, [done[e] for e in earlier]), axis, pairs)

    def chip(m, *earlier):
        step(f"chip{m}", done[f"to{m}"][:rows], "blk", 2, *earlier)

    def product(parts, out_rows, *earlier):
        parts = [done[name] for name in parts]
        parts[0] = after(parts[0], [done[e] for e in earlier])
        return contract(parts, rows, out_rows, done["own"], done["other"])

    def near_far(masks, *earlier):
        parts = [f"{at}{m}" for at in ("to", "chip") for m in masks]
        made = product(parts, [rows] * len(masks) + [rows * len(masks)], *earlier)
        done.update(zip([f"near{m}" for m in masks], made))
        return made[-1]

    def swap_far(name, value, masks, *earlier):
        step(name, value, "blk", 2, *earlier)
        for at, m in enumerate(masks):
            done[f"far{m}"] = done[name][at * rows : (at + 1) * rows]

    def back(m, *earlier):
        both = jnp.concatenate([done[f"near{m}"], done[f"far{m}"]])
        step(f"from{m}", both, "wide", m, *earlier)

    groups = ((0,), (1,), (2,), (3,), (4, 5), (6,), (7,))
    done["to0"], s1, s2, s3, s45, s6, s7 = select(amplitudes, owner, groups)
    step("other", own, "blk", 1)
    step("to2", s2, "wide", 2)
    step("to3", s3, "wide", 3)
    step("to4", s45, "wide", 4)
    chip(0, "other")
    step("to1", s1, "wide", 1, "other")
    done["own"] = hold(after(own, [done["other"]]))
    chip(1, "other")
    chip(2, "other", "chip0", "to1")
    chip(3, "other")
    step("to6", s6, "wide", 6, "to4", "chip1")
    step("to5", done["to4"][rows:], "wide", 1, "chip1")
    chip(4, "chip2")
    chip(5, "to6", "chip0", "chip1", "chip3", "own")
    step("to7", s7, "wide", 7, "chip4")
    (done["made45"],) = product(("to4", "chip4", "to5", "chip5"), [4 * rows])

    step("from4", "made45", "wide", 4)
    chip(6, "chip5")
    chip(7, "made45")
    near = [f"{at}{m}" for m in range(4) for at in ("to", "chip")]
    made = product(near, [2 * rows] * 4, "made45")
    done.update(zip([f"near{m}" for m in range(4)], made))
    step("from1", "near1", "wide", 1)
    step("from2", "near2", "wide", 2)
    step("from3", "near3", "wide", 3)
    far = near_far((6, 7), "chip6", "near0")
    swap_far("swap67", far, (6, 7))
    step("from5", done["from4"][2 * rows :], "wide", 1)
    back(6)
    back(7)
    far = [done["near0"]] + [done[f"from{m}"] for m in (1, 2, 3)]
    step("swap0123", jnp.concatenate([value[rows:] for value in far]), "blk", 2)
    far = [done["from4"][: 2 * rows], done["from5"]]
    step("swap45", jnp.concatenate([value[rows:] for value in far]), "blk", 2)
    parts = [done["near0"]] + [done[f"from{m}"] for m in range(1, wide)]
    parts += [done["swap0123"], done["swap45"]]
    places = []
    for m in range(wide):
        places += [(m, 0), (wide, m * rows) if m < 4 else (wide + 1, (m - 4) * rows)]
        if m > 5:
            places[-1] = (m, rows)
    shape = (wide, i, j, lax.axis_size("blk") * own.shape[1])
    return collect(parts, places, owner, targets, counts, shape)


def body_large(amplitudes, integrals, owner, targets, counts):
    wide_count = lax.axis_size("wide")
    my_index = lax.axis_index("wide")
    tile_ids = jnp.arange(owner.shape[0], dtype=jnp.int32)
    holder = jnp.sum(jnp.where(owner[None, :] == tile_ids[:, None], tile_ids[None, :], 0), axis=1)
    ordered = jnp.take(amplitudes, holder, axis=2)
    my_tile = lax.all_to_all(ordered, "wide", split_axis=2, concat_axis=1, tiled=True)
    my_holder = lax.dynamic_index_in_dim(holder, my_index, 0, keepdims=False)
    my_count = lax.dynamic_index_in_dim(counts, my_holder, 0, keepdims=False)
    slot_ids = jnp.arange(targets.shape[1], dtype=jnp.int32)
    live_slots = (slot_ids < my_count).astype(jnp.float32)
    my_integrals = integrals[0]
    width = my_tile.shape[3]
    portion = lax.all_gather(my_tile, "blk", axis=0, tiled=True)
    flat_rows = portion.reshape(-1, width)
    result = jnp.einsum("rc,kac->rka", flat_rows, my_integrals, preferred_element_type=jnp.float32)
    partial_value = result.reshape(
        portion.shape[0], portion.shape[1], my_integrals.shape[0], my_integrals.shape[1]
    )
    shaped = (partial_value * live_slots[None, None, :, None]).astype(jnp.bfloat16)
    received = lax.all_to_all(
        lax.all_to_all(shaped, "wide", split_axis=1, concat_axis=2, tiled=True),
        "blk",
        split_axis=0,
        concat_axis=3,
        tiled=True,
    )
    slot_targets = jnp.take(targets, holder, axis=0).reshape(-1)
    window_ids = jnp.arange(wide_count, dtype=jnp.int32)
    selector = (slot_targets[None, :] == window_ids[:, None]).astype(jnp.bfloat16)
    ladder = jnp.einsum("ps,ijsa->pija", selector, received, preferred_element_type=jnp.float32)
    return ladder.astype(jnp.bfloat16)


def solution(mesh):
    few = mesh.shape["wide"] == 8 and mesh.shape["blk"] == 4
    placed = (P("blk", "wide", None, None), P("wide", None, "blk", None), P(), P(), P())
    return jax.shard_map(
        body if few else body_large,
        mesh=mesh,
        in_specs=placed,
        out_specs=P(None, "blk", "wide", None),
        check_vma=False,
    )
```

```python
import functools

import jax
import jax.numpy as jnp
from jax import lax
from jax.experimental import pallas as pl
from jax.experimental.pallas import tpu as pltpu
from jax.sharding import PartitionSpec as P

MIB = 1 << 20
KERNEL_VMEM = 16 * MIB
CONTRACT_VMEM = 20 * MIB
HOLD_VMEM = 44 * MIB
SMEM = pl.BlockSpec(memory_space=pltpu.SMEM)


def find_tile(owner_ref, slot):
    def step(q, found):
        return jnp.where(owner_ref[q] == slot, q, found)

    return lax.fori_loop(0, owner_ref.shape[0], step, jnp.int32(0))


def select_kernel(rows, groups, owner_ref, amp_ref, *rest):
    outs, pick_ref = rest[:-1], rest[-1]
    tiles = owner_ref.shape[0]

    @pl.when(pl.program_id(0) == 0)
    def _():
        me = lax.axis_index("wide")
        shape = pick_ref.shape
        out_row = lax.broadcasted_iota(jnp.int32, shape, 0)
        in_row = lax.broadcasted_iota(jnp.int32, shape, 1)
        slot = lax.bitwise_xor(out_row // rows, me)
        tile = in_row % tiles
        place = jnp.zeros(shape, jnp.int32)
        for q in range(tiles):
            place = jnp.where(tile == q, owner_ref[q], place)
        chosen = (place == slot) & (out_row % rows == in_row // tiles)
        pick_ref[...] = jnp.where(chosen, 1.0, 0.0).astype(pick_ref.dtype)

    moved = jnp.dot(pick_ref[...], amp_ref[...], preferred_element_type=jnp.float32)
    moved = moved.astype(amp_ref.dtype)
    for group, out in zip(groups, outs):
        for at, m in enumerate(group):
            out[at * rows : (at + 1) * rows] = moved[m * rows : (m + 1) * rows]


def select(amplitudes, owner, groups):
    i, j, tiles, width = amplitudes.shape
    rows = i * j
    wide = sum(map(len, groups))
    block = min(width, 1024)
    return pl.pallas_call(
        functools.partial(select_kernel, rows, groups),
        grid=(width // block,),
        in_specs=[SMEM, pl.BlockSpec((rows * tiles, block), lambda c: (0, c))],
        out_specs=[pl.BlockSpec((len(g) * rows, block), lambda c: (0, c)) for g in groups],
        out_shape=[jax.ShapeDtypeStruct((len(g) * rows, width), amplitudes.dtype) for g in groups],
        scratch_shapes=[pltpu.VMEM((wide * rows, rows * tiles), amplitudes.dtype)],
        compiler_params=pltpu.CompilerParams(vmem_limit_bytes=KERNEL_VMEM),
        cost_estimate=pl.CostEstimate(
            flops=2 * wide * rows * rows * tiles * width,
            bytes_accessed=4 * rows * tiles * width,
            transcendentals=0,
        ),
        name="select_tiles",
    )(owner, amplitudes.reshape(rows * tiles, width))


def hold_kernel(value_ref, held_ref, sem):
    copy = pltpu.make_async_copy(value_ref, held_ref, sem)
    copy.start()
    copy.wait()


def hold(value):
    return pl.pallas_call(
        hold_kernel,
        in_specs=[pl.BlockSpec(memory_space=pl.ANY)],
        out_specs=pl.BlockSpec(memory_space=pltpu.VMEM),
        out_shape=jax.ShapeDtypeStruct(value.shape, value.dtype),
        scratch_shapes=[pltpu.SemaphoreType.DMA],
        compiler_params=pltpu.CompilerParams(vmem_limit_bytes=HOLD_VMEM),
        name="hold_integrals",
    )(value)


def contract_kernel(count, block, *refs):
    parts, integrals = refs[:count], refs[count : count + 2]
    outs, rows_ref, sems = refs[count + 2 : -2], refs[-2], refs[-1]
    rows = rows_ref.shape[0] // count
    partners, ab, _ = integrals[0].shape
    copies = [
        pltpu.make_async_copy(part.at[pl.ds(0, rows)], rows_ref.at[pl.ds(n * rows, rows)], sems.at[n])
        for n, part in enumerate(parts)
    ]
    for copy in copies:
        copy.start()
    for copy in copies:
        copy.wait()
    for source, integ_ref in enumerate(integrals):

        @pl.loop(0, partners * ab // block)
        def _(at):
            k, begin = at // (ab // block), pl.multiple_of(at % (ab // block) * block, block)
            value = lax.dot_general(
                integ_ref[k, pl.ds(begin, block), :],
                rows_ref[...],
                (((1,), (1,)), ((), ())),
                preferred_element_type=jnp.float32,
            ).T.astype(jnp.bfloat16)
            column = pl.multiple_of((2 * k + source) * ab + begin, block)
            first = 0
            for out in outs:
                out[:, pl.ds(column, block)] = value[first : first + out.shape[0]]
                first += out.shape[0]


def contract(parts, rows, out_rows, own, other):
    width = parts[0].shape[1]
    partners, ab, _ = own.shape
    count = len(parts)
    vmem = pl.BlockSpec(memory_space=pltpu.VMEM)
    return pl.pallas_call(
        functools.partial(contract_kernel, count, min(ab, 512)),
        in_specs=[pl.BlockSpec(memory_space=pl.ANY)] * count + [vmem, vmem],
        out_specs=[vmem] * len(out_rows),
        out_shape=[
            jax.ShapeDtypeStruct((each, partners * 2 * ab), jnp.bfloat16) for each in out_rows
        ],
        scratch_shapes=[
            pltpu.VMEM((count * rows, width), parts[0].dtype),
            pltpu.SemaphoreType.DMA((count,)),
        ],
        compiler_params=pltpu.CompilerParams(vmem_limit_bytes=CONTRACT_VMEM),
        name="contract_rows",
    )(*parts, own, other)


def collect_kernel(partners, rows, places, owner_ref, targets_ref, counts_ref, *rest):
    parts, out_ref, sum_ref = rest[:-2], rest[-2], rest[-1]
    me, mine = lax.axis_index("wide"), lax.axis_index("blk")
    ab = parts[0].shape[1] // (2 * partners)
    sum_ref[...] = jnp.zeros_like(sum_ref)
    for m in range(len(places) // 2):
        tile = find_tile(owner_ref, lax.bitwise_xor(me, m))
        live = counts_ref[tile]
        for k in range(partners):
            target = targets_ref[tile, k]

            @pl.when(k < live)
            def _():
                for n in range(4):
                    part, first = places[2 * m + n // 2]
                    begin = pl.multiple_of(lax.bitwise_xor(mine, n) * ab, 128)
                    column = (2 * k + n % 2) * ab
                    value = parts[part][first : first + rows, column : column + ab]
                    sum_ref[target, :, pl.ds(begin, ab)] += value.astype(jnp.float32)

    outer, inner = out_ref.shape[1:3]
    for i in range(outer):
        out_ref[:, i] = sum_ref[:, i * inner : (i + 1) * inner, :].astype(out_ref.dtype)


def collect(parts, places, owner, targets, counts, shape):
    partners, rows = targets.shape[1], shape[1] * shape[2]
    return pl.pallas_call(
        functools.partial(collect_kernel, partners, rows, places),
        in_specs=[SMEM, SMEM, SMEM] + [pl.BlockSpec(memory_space=pltpu.VMEM)] * len(parts),
        out_specs=pl.BlockSpec(memory_space=pltpu.VMEM),
        out_shape=jax.ShapeDtypeStruct(shape, jnp.bfloat16),
        scratch_shapes=[pltpu.VMEM((shape[0], rows, shape[3]), jnp.float32)],
        compiler_params=pltpu.CompilerParams(vmem_limit_bytes=KERNEL_VMEM),
        name="collect_targets",
    )(owner, targets, counts, *parts)


def after(value, earlier):
    return lax.optimization_barrier((value, *earlier))[0] if earlier else value


def body(amplitudes, integrals, owner, targets, counts):
    wide = lax.axis_size("wide")
    i, j, tiles, width = amplitudes.shape
    rows = i * j
    own = integrals[0]
    done = {}

    def step(name, value, axis, mask, *earlier):
        pairs = [(s, s ^ mask) for s in range(lax.axis_size(axis))]
        value = done[value] if isinstance(value, str) else value
        done[name] = lax.ppermute(after(value, [done[e] for e in earlier]), axis, pairs)

    def chip(m, *earlier):
        step(f"chip{m}", done[f"to{m}"][:rows], "blk", 2, *earlier)

    def product(parts, out_rows, *earlier):
        parts = [done[name] for name in parts]
        parts[0] = after(parts[0], [done[e] for e in earlier])
        return contract(parts, rows, out_rows, done["own"], done["other"])

    def near_far(masks, *earlier):
        parts = [f"{at}{m}" for at in ("to", "chip") for m in masks]
        made = product(parts, [rows] * len(masks) + [rows * len(masks)], *earlier)
        done.update(zip([f"near{m}" for m in masks], made))
        return made[-1]

    def swap_far(name, value, masks, *earlier):
        step(name, value, "blk", 2, *earlier)
        for at, m in enumerate(masks):
            done[f"far{m}"] = done[name][at * rows : (at + 1) * rows]

    def back(m, *earlier):
        both = jnp.concatenate([done[f"near{m}"], done[f"far{m}"]])
        step(f"from{m}", both, "wide", m, *earlier)

    groups = ((0,), (1,), (2,), (3,), (4, 5), (6,), (7,))
    done["to0"], s1, s2, s3, s45, s6, s7 = select(amplitudes, owner, groups)
    step("other", own, "blk", 1)
    step("to4", s45, "wide", 4)
    chip(0, "other")
    step("to1", s1, "wide", 1, "other")
    step("to2", s2, "wide", 2)
    step("to3", s3, "wide", 3)
    done["own"] = hold(after(own, [done[e] for e in ("other",)]))
    chip(1)
    chip(2, "other", "chip0", "to1")
    chip(3)
    step("to6", s6, "wide", 6, "to4", "to1")
    step("to5", done["to4"][rows:], "wide", 1, "chip1")
    chip(5, "chip0", "chip1", "own", "to3")
    chip(4, "to6", "chip2")
    step("to7", s7, "wide", 7, "to6")
    (done["made45"],) = product(("to4", "chip4", "to5", "chip5"), [4 * rows])

    step("from4", "made45", "wide", 4)
    chip(6, "chip5")
    chip(7, "made45")
    near = [f"{at}{m}" for m in range(4) for at in ("to", "chip")]
    made = product(near, [2 * rows] * 4, "made45")
    done.update(zip([f"near{m}" for m in range(4)], made))
    step("from1", "near1", "wide", 1)
    step("from2", "near2", "wide", 2)
    step("from3", "near3", "wide", 3)
    far = near_far((6, 7), "chip6", "near0")
    swap_far("swap67", far, (6, 7))
    step("from5", done["from4"][2 * rows :], "wide", 1)
    back(6)
    back(7)
    far = [done["near0"]] + [done[f"from{m}"] for m in (1, 2, 3)]
    step("swap0123", jnp.concatenate([value[rows:] for value in far]), "blk", 2, "swap67")
    far = [done["from4"][: 2 * rows], done["from5"]]
    step("swap45", jnp.concatenate([value[rows:] for value in far]), "blk", 2)
    parts = [done["near0"]] + [done[f"from{m}"] for m in range(1, wide)]
    parts += [done["swap0123"], done["swap45"]]
    places = []
    for m in range(wide):
        places += [(m, 0), (wide, m * rows) if m < 4 else (wide + 1, (m - 4) * rows)]
        if m > 5:
            places[-1] = (m, rows)
    shape = (wide, i, j, lax.axis_size("blk") * own.shape[1])
    return collect(parts, places, owner, targets, counts, shape)


def body_large(amplitudes, integrals, owner, targets, counts):
    wide_count = lax.axis_size("wide")
    my_index = lax.axis_index("wide")
    tile_ids = jnp.arange(owner.shape[0], dtype=jnp.int32)
    holder = jnp.sum(jnp.where(owner[None, :] == tile_ids[:, None], tile_ids[None, :], 0), axis=1)
    ordered = jnp.take(amplitudes, holder, axis=2)
    my_tile = lax.all_to_all(ordered, "wide", split_axis=2, concat_axis=1, tiled=True)
    my_holder = lax.dynamic_index_in_dim(holder, my_index, 0, keepdims=False)
    my_count = lax.dynamic_index_in_dim(counts, my_holder, 0, keepdims=False)
    slot_ids = jnp.arange(targets.shape[1], dtype=jnp.int32)
    live_slots = (slot_ids < my_count).astype(jnp.float32)
    my_integrals = integrals[0]
    width = my_tile.shape[3]
    portion = lax.all_gather(my_tile, "blk", axis=0, tiled=True)
    flat_rows = portion.reshape(-1, width)
    result = jnp.einsum("rc,kac->rka", flat_rows, my_integrals, preferred_element_type=jnp.float32)
    partial_value = result.reshape(
        portion.shape[0], portion.shape[1], my_integrals.shape[0], my_integrals.shape[1]
    )
    shaped = (partial_value * live_slots[None, None, :, None]).astype(jnp.bfloat16)
    received = lax.all_to_all(
        lax.all_to_all(shaped, "wide", split_axis=1, concat_axis=2, tiled=True),
        "blk",
        split_axis=0,
        concat_axis=3,
        tiled=True,
    )
    slot_targets = jnp.take(targets, holder, axis=0).reshape(-1)
    window_ids = jnp.arange(wide_count, dtype=jnp.int32)
    selector = (slot_targets[None, :] == window_ids[:, None]).astype(jnp.bfloat16)
    ladder = jnp.einsum("ps,ijsa->pija", selector, received, preferred_element_type=jnp.float32)
    return ladder.astype(jnp.bfloat16)


def solution(mesh):
    few = mesh.shape["wide"] == 8 and mesh.shape["blk"] == 4
    placed = (P("blk", "wide", None, None), P("wide", None, "blk", None), P(), P(), P())
    return jax.shard_map(
        body if few else body_large,
        mesh=mesh,
        in_specs=placed,
        out_specs=P(None, "blk", "wide", None),
        check_vma=False,
    )
```

```python
import functools

import jax
import jax.numpy as jnp
from jax import lax
from jax.experimental import pallas as pl
from jax.experimental.pallas import tpu as pltpu
from jax.sharding import PartitionSpec as P

MIB = 1 << 20
KERNEL_VMEM = 16 * MIB
CONTRACT_VMEM = 20 * MIB
HOLD_VMEM = 44 * MIB
SMEM = pl.BlockSpec(memory_space=pltpu.SMEM)


def find_tile(owner_ref, slot):
    def step(q, found):
        return jnp.where(owner_ref[q] == slot, q, found)

    return lax.fori_loop(0, owner_ref.shape[0], step, jnp.int32(0))


def select_kernel(rows, groups, owner_ref, amp_ref, *rest):
    outs, pick_ref = rest[:-1], rest[-1]
    tiles = owner_ref.shape[0]

    @pl.when(pl.program_id(0) == 0)
    def _():
        me = lax.axis_index("wide")
        shape = pick_ref.shape
        out_row = lax.broadcasted_iota(jnp.int32, shape, 0)
        in_row = lax.broadcasted_iota(jnp.int32, shape, 1)
        slot = lax.bitwise_xor(out_row // rows, me)
        tile = in_row % tiles
        place = jnp.zeros(shape, jnp.int32)
        for q in range(tiles):
            place = jnp.where(tile == q, owner_ref[q], place)
        chosen = (place == slot) & (out_row % rows == in_row // tiles)
        pick_ref[...] = jnp.where(chosen, 1.0, 0.0).astype(pick_ref.dtype)

    moved = jnp.dot(pick_ref[...], amp_ref[...], preferred_element_type=jnp.float32)
    moved = moved.astype(amp_ref.dtype)
    for group, out in zip(groups, outs):
        for at, m in enumerate(group):
            out[at * rows : (at + 1) * rows] = moved[m * rows : (m + 1) * rows]


def select(amplitudes, owner, groups):
    i, j, tiles, width = amplitudes.shape
    rows = i * j
    wide = sum(map(len, groups))
    block = min(width, 1024)
    return pl.pallas_call(
        functools.partial(select_kernel, rows, groups),
        grid=(width // block,),
        in_specs=[SMEM, pl.BlockSpec((rows * tiles, block), lambda c: (0, c))],
        out_specs=[pl.BlockSpec((len(g) * rows, block), lambda c: (0, c)) for g in groups],
        out_shape=[jax.ShapeDtypeStruct((len(g) * rows, width), amplitudes.dtype) for g in groups],
        scratch_shapes=[pltpu.VMEM((wide * rows, rows * tiles), amplitudes.dtype)],
        compiler_params=pltpu.CompilerParams(vmem_limit_bytes=KERNEL_VMEM),
        cost_estimate=pl.CostEstimate(
            flops=2 * wide * rows * rows * tiles * width,
            bytes_accessed=4 * rows * tiles * width,
            transcendentals=0,
        ),
        name="select_tiles",
    )(owner, amplitudes.reshape(rows * tiles, width))


def hold_kernel(value_ref, held_ref, sem):
    copy = pltpu.make_async_copy(value_ref, held_ref, sem)
    copy.start()
    copy.wait()


def hold(value):
    return pl.pallas_call(
        hold_kernel,
        in_specs=[pl.BlockSpec(memory_space=pl.ANY)],
        out_specs=pl.BlockSpec(memory_space=pltpu.VMEM),
        out_shape=jax.ShapeDtypeStruct(value.shape, value.dtype),
        scratch_shapes=[pltpu.SemaphoreType.DMA],
        compiler_params=pltpu.CompilerParams(vmem_limit_bytes=HOLD_VMEM),
        name="hold_integrals",
    )(value)


def contract_kernel(count, block, *refs):
    parts, integrals = refs[:count], refs[count : count + 2]
    outs, rows_ref, sems = refs[count + 2 : -2], refs[-2], refs[-1]
    rows = rows_ref.shape[0] // count
    partners, ab, _ = integrals[0].shape
    copies = [
        pltpu.make_async_copy(part.at[pl.ds(0, rows)], rows_ref.at[pl.ds(n * rows, rows)], sems.at[n])
        for n, part in enumerate(parts)
    ]
    for copy in copies:
        copy.start()
    for copy in copies:
        copy.wait()
    for source, integ_ref in enumerate(integrals):

        @pl.loop(0, partners * ab // block)
        def _(at):
            k, begin = at // (ab // block), pl.multiple_of(at % (ab // block) * block, block)
            value = lax.dot_general(
                integ_ref[k, pl.ds(begin, block), :],
                rows_ref[...],
                (((1,), (1,)), ((), ())),
                preferred_element_type=jnp.float32,
            ).T.astype(jnp.bfloat16)
            column = pl.multiple_of((2 * k + source) * ab + begin, block)
            first = 0
            for out in outs:
                out[:, pl.ds(column, block)] = value[first : first + out.shape[0]]
                first += out.shape[0]


def contract(parts, rows, out_rows, own, other):
    width = parts[0].shape[1]
    partners, ab, _ = own.shape
    count = len(parts)
    vmem = pl.BlockSpec(memory_space=pltpu.VMEM)
    return pl.pallas_call(
        functools.partial(contract_kernel, count, min(ab, 512)),
        in_specs=[pl.BlockSpec(memory_space=pl.ANY)] * count + [vmem, vmem],
        out_specs=[vmem] * len(out_rows),
        out_shape=[
            jax.ShapeDtypeStruct((each, partners * 2 * ab), jnp.bfloat16) for each in out_rows
        ],
        scratch_shapes=[
            pltpu.VMEM((count * rows, width), parts[0].dtype),
            pltpu.SemaphoreType.DMA((count,)),
        ],
        compiler_params=pltpu.CompilerParams(vmem_limit_bytes=CONTRACT_VMEM),
        name="contract_rows",
    )(*parts, own, other)


def collect_kernel(partners, rows, places, owner_ref, targets_ref, counts_ref, *rest):
    parts, out_ref, sum_ref = rest[:-2], rest[-2], rest[-1]
    me, mine = lax.axis_index("wide"), lax.axis_index("blk")
    ab = parts[0].shape[1] // (2 * partners)
    sum_ref[...] = jnp.zeros_like(sum_ref)
    for m in range(len(places) // 2):
        tile = find_tile(owner_ref, lax.bitwise_xor(me, m))
        live = counts_ref[tile]
        for k in range(partners):
            target = targets_ref[tile, k]

            @pl.when(k < live)
            def _():
                for n in range(4):
                    part, first = places[2 * m + n // 2]
                    begin = pl.multiple_of(lax.bitwise_xor(mine, n) * ab, 128)
                    column = (2 * k + n % 2) * ab
                    value = parts[part][first : first + rows, column : column + ab]
                    sum_ref[target, :, pl.ds(begin, ab)] += value.astype(jnp.float32)

    outer, inner = out_ref.shape[1:3]
    for i in range(outer):
        out_ref[:, i] = sum_ref[:, i * inner : (i + 1) * inner, :].astype(out_ref.dtype)


def collect(parts, places, owner, targets, counts, shape):
    partners, rows = targets.shape[1], shape[1] * shape[2]
    return pl.pallas_call(
        functools.partial(collect_kernel, partners, rows, places),
        in_specs=[SMEM, SMEM, SMEM] + [pl.BlockSpec(memory_space=pltpu.VMEM)] * len(parts),
        out_specs=pl.BlockSpec(memory_space=pltpu.VMEM),
        out_shape=jax.ShapeDtypeStruct(shape, jnp.bfloat16),
        scratch_shapes=[pltpu.VMEM((shape[0], rows, shape[3]), jnp.float32)],
        compiler_params=pltpu.CompilerParams(vmem_limit_bytes=KERNEL_VMEM),
        name="collect_targets",
    )(owner, targets, counts, *parts)


def after(value, earlier):
    return lax.optimization_barrier((value, *earlier))[0] if earlier else value


def body(amplitudes, integrals, owner, targets, counts):
    wide = lax.axis_size("wide")
    i, j, tiles, width = amplitudes.shape
    rows = i * j
    own = integrals[0]
    done = {}

    def step(name, value, axis, mask, *earlier):
        pairs = [(s, s ^ mask) for s in range(lax.axis_size(axis))]
        value = done[value] if isinstance(value, str) else value
        done[name] = lax.ppermute(after(value, [done[e] for e in earlier]), axis, pairs)

    def chip(m, *earlier):
        step(f"chip{m}", done[f"to{m}"][:rows], "blk", 2, *earlier)

    def product(parts, out_rows, *earlier):
        parts = [done[name] for name in parts]
        parts[0] = after(parts[0], [done[e] for e in earlier])
        return contract(parts, rows, out_rows, done["own"], done["other"])

    def near_far(masks, *earlier):
        parts = [f"{at}{m}" for at in ("to", "chip") for m in masks]
        made = product(parts, [rows] * len(masks) + [rows * len(masks)], *earlier)
        done.update(zip([f"near{m}" for m in masks], made))
        return made[-1]

    def swap_far(name, value, masks, *earlier):
        step(name, value, "blk", 2, *earlier)
        for at, m in enumerate(masks):
            done[f"far{m}"] = done[name][at * rows : (at + 1) * rows]

    def back(m, *earlier):
        both = jnp.concatenate([done[f"near{m}"], done[f"far{m}"]])
        step(f"from{m}", both, "wide", m, *earlier)

    groups = ((0,), (1,), (2,), (3,), (4, 5), (6,), (7,))
    done["to0"], s1, s2, s3, s45, s6, s7 = select(amplitudes, owner, groups)
    step("other", own, "blk", 1)
    step("to4", s45, "wide", 4)
    chip(0, "other")
    step("to1", s1, "wide", 1, "other")
    step("to2", s2, "wide", 2)
    step("to3", s3, "wide", 3)
    done["own"] = hold(after(own, [done[e] for e in ("other",)]))
    chip(1)
    chip(2, "other", "chip0", "to1")
    chip(3)
    step("to6", s6, "wide", 6, "to4", "to1")
    step("to5", done["to4"][rows:], "wide", 1, "chip1", "chip0")
    chip(4, "chip1")
    chip(5, "own", "to2", "to3", "chip4", "to6")
    step("to7", s7, "wide", 7, "to6")
    (done["made45"],) = product(("to4", "chip4", "to5", "chip5"), [4 * rows])

    step("from4", "made45", "wide", 4)
    chip(6, "chip5")
    chip(7, "made45")
    near = [f"{at}{m}" for m in range(4) for at in ("to", "chip")]
    made = product(near, [2 * rows] * 4, "made45")
    done.update(zip([f"near{m}" for m in range(4)], made))
    step("from1", "near1", "wide", 1)
    step("from2", "near2", "wide", 2)
    step("from3", "near3", "wide", 3)
    far = near_far((6, 7), "chip6", "near0")
    swap_far("swap67", far, (6, 7))
    step("from5", done["from4"][2 * rows :], "wide", 1)
    back(6)
    back(7)
    far = [done["near0"]] + [done[f"from{m}"] for m in (1, 2, 3)]
    step("swap0123", jnp.concatenate([value[rows:] for value in far]), "blk", 2, "swap67")
    far = [done["from4"][: 2 * rows], done["from5"]]
    step("swap45", jnp.concatenate([value[rows:] for value in far]), "blk", 2)
    parts = [done["near0"]] + [done[f"from{m}"] for m in range(1, wide)]
    parts += [done["swap0123"], done["swap45"]]
    places = []
    for m in range(wide):
        places += [(m, 0), (wide, m * rows) if m < 4 else (wide + 1, (m - 4) * rows)]
        if m > 5:
            places[-1] = (m, rows)
    shape = (wide, i, j, lax.axis_size("blk") * own.shape[1])
    return collect(parts, places, owner, targets, counts, shape)


def body_large(amplitudes, integrals, owner, targets, counts):
    wide_count = lax.axis_size("wide")
    my_index = lax.axis_index("wide")
    tile_ids = jnp.arange(owner.shape[0], dtype=jnp.int32)
    holder = jnp.sum(jnp.where(owner[None, :] == tile_ids[:, None], tile_ids[None, :], 0), axis=1)
    ordered = jnp.take(amplitudes, holder, axis=2)
    my_tile = lax.all_to_all(ordered, "wide", split_axis=2, concat_axis=1, tiled=True)
    my_holder = lax.dynamic_index_in_dim(holder, my_index, 0, keepdims=False)
    my_count = lax.dynamic_index_in_dim(counts, my_holder, 0, keepdims=False)
    slot_ids = jnp.arange(targets.shape[1], dtype=jnp.int32)
    live_slots = (slot_ids < my_count).astype(jnp.float32)
    my_integrals = integrals[0]
    width = my_tile.shape[3]
    portion = lax.all_gather(my_tile, "blk", axis=0, tiled=True)
    flat_rows = portion.reshape(-1, width)
    result = jnp.einsum("rc,kac->rka", flat_rows, my_integrals, preferred_element_type=jnp.float32)
    partial_value = result.reshape(
        portion.shape[0], portion.shape[1], my_integrals.shape[0], my_integrals.shape[1]
    )
    shaped = (partial_value * live_slots[None, None, :, None]).astype(jnp.bfloat16)
    received = lax.all_to_all(
        lax.all_to_all(shaped, "wide", split_axis=1, concat_axis=2, tiled=True),
        "blk",
        split_axis=0,
        concat_axis=3,
        tiled=True,
    )
    slot_targets = jnp.take(targets, holder, axis=0).reshape(-1)
    window_ids = jnp.arange(wide_count, dtype=jnp.int32)
    selector = (slot_targets[None, :] == window_ids[:, None]).astype(jnp.bfloat16)
    ladder = jnp.einsum("ps,ijsa->pija", selector, received, preferred_element_type=jnp.float32)
    return ladder.astype(jnp.bfloat16)


def solution(mesh):
    few = mesh.shape["wide"] == 8 and mesh.shape["blk"] == 4
    placed = (P("blk", "wide", None, None), P("wide", None, "blk", None), P(), P(), P())
    return jax.shard_map(
        body if few else body_large,
        mesh=mesh,
        in_specs=placed,
        out_specs=P(None, "blk", "wide", None),
        check_vma=False,
    )
```

```python
import functools

import jax
import jax.numpy as jnp
from jax import lax
from jax.experimental import pallas as pl
from jax.experimental.pallas import tpu as pltpu
from jax.sharding import PartitionSpec as P

MIB = 1 << 20
KERNEL_VMEM = 16 * MIB
CONTRACT_VMEM = 20 * MIB
HOLD_VMEM = 44 * MIB
SMEM = pl.BlockSpec(memory_space=pltpu.SMEM)


def find_tile(owner_ref, slot):
    def step(q, found):
        return jnp.where(owner_ref[q] == slot, q, found)

    return lax.fori_loop(0, owner_ref.shape[0], step, jnp.int32(0))


def select_kernel(rows, groups, owner_ref, amp_ref, *rest):
    outs, pick_ref = rest[:-1], rest[-1]
    tiles = owner_ref.shape[0]

    @pl.when(pl.program_id(0) == 0)
    def _():
        me = lax.axis_index("wide")
        shape = pick_ref.shape
        out_row = lax.broadcasted_iota(jnp.int32, shape, 0)
        in_row = lax.broadcasted_iota(jnp.int32, shape, 1)
        slot = lax.bitwise_xor(out_row // rows, me)
        tile = in_row % tiles
        place = jnp.zeros(shape, jnp.int32)
        for q in range(tiles):
            place = jnp.where(tile == q, owner_ref[q], place)
        chosen = (place == slot) & (out_row % rows == in_row // tiles)
        pick_ref[...] = jnp.where(chosen, 1.0, 0.0).astype(pick_ref.dtype)

    moved = jnp.dot(pick_ref[...], amp_ref[...], preferred_element_type=jnp.float32)
    moved = moved.astype(amp_ref.dtype)
    for group, out in zip(groups, outs):
        for at, m in enumerate(group):
            out[at * rows : (at + 1) * rows] = moved[m * rows : (m + 1) * rows]


def select(amplitudes, owner, groups):
    i, j, tiles, width = amplitudes.shape
    rows = i * j
    wide = sum(map(len, groups))
    block = min(width, 1024)
    return pl.pallas_call(
        functools.partial(select_kernel, rows, groups),
        grid=(width // block,),
        in_specs=[SMEM, pl.BlockSpec((rows * tiles, block), lambda c: (0, c))],
        out_specs=[pl.BlockSpec((len(g) * rows, block), lambda c: (0, c)) for g in groups],
        out_shape=[jax.ShapeDtypeStruct((len(g) * rows, width), amplitudes.dtype) for g in groups],
        scratch_shapes=[pltpu.VMEM((wide * rows, rows * tiles), amplitudes.dtype)],
        compiler_params=pltpu.CompilerParams(vmem_limit_bytes=KERNEL_VMEM),
        cost_estimate=pl.CostEstimate(
            flops=2 * wide * rows * rows * tiles * width,
            bytes_accessed=4 * rows * tiles * width,
            transcendentals=0,
        ),
        name="select_tiles",
    )(owner, amplitudes.reshape(rows * tiles, width))


def hold_kernel(value_ref, held_ref, sem):
    copy = pltpu.make_async_copy(value_ref, held_ref, sem)
    copy.start()
    copy.wait()


def hold(value):
    return pl.pallas_call(
        hold_kernel,
        in_specs=[pl.BlockSpec(memory_space=pl.ANY)],
        out_specs=pl.BlockSpec(memory_space=pltpu.VMEM),
        out_shape=jax.ShapeDtypeStruct(value.shape, value.dtype),
        scratch_shapes=[pltpu.SemaphoreType.DMA],
        compiler_params=pltpu.CompilerParams(vmem_limit_bytes=HOLD_VMEM),
        name="hold_integrals",
    )(value)


def contract_kernel(count, block, *refs):
    parts, integrals = refs[:count], refs[count : count + 2]
    outs, rows_ref, sems = refs[count + 2 : -2], refs[-2], refs[-1]
    rows = rows_ref.shape[0] // count
    partners, ab, _ = integrals[0].shape
    copies = [
        pltpu.make_async_copy(part.at[pl.ds(0, rows)], rows_ref.at[pl.ds(n * rows, rows)], sems.at[n])
        for n, part in enumerate(parts)
    ]
    for copy in copies:
        copy.start()
    for copy in copies:
        copy.wait()
    for source, integ_ref in enumerate(integrals):

        @pl.loop(0, partners * ab // block)
        def _(at):
            k, begin = at // (ab // block), pl.multiple_of(at % (ab // block) * block, block)
            value = lax.dot_general(
                integ_ref[k, pl.ds(begin, block), :],
                rows_ref[...],
                (((1,), (1,)), ((), ())),
                preferred_element_type=jnp.float32,
            ).T.astype(jnp.bfloat16)
            column = pl.multiple_of((2 * k + source) * ab + begin, block)
            first = 0
            for out in outs:
                out[:, pl.ds(column, block)] = value[first : first + out.shape[0]]
                first += out.shape[0]


def contract(parts, rows, out_rows, own, other):
    width = parts[0].shape[1]
    partners, ab, _ = own.shape
    count = len(parts)
    vmem = pl.BlockSpec(memory_space=pltpu.VMEM)
    return pl.pallas_call(
        functools.partial(contract_kernel, count, min(ab, 512)),
        in_specs=[pl.BlockSpec(memory_space=pl.ANY)] * count + [vmem, vmem],
        out_specs=[vmem] * len(out_rows),
        out_shape=[
            jax.ShapeDtypeStruct((each, partners * 2 * ab), jnp.bfloat16) for each in out_rows
        ],
        scratch_shapes=[
            pltpu.VMEM((count * rows, width), parts[0].dtype),
            pltpu.SemaphoreType.DMA((count,)),
        ],
        compiler_params=pltpu.CompilerParams(vmem_limit_bytes=CONTRACT_VMEM),
        name="contract_rows",
    )(*parts, own, other)


def collect_kernel(partners, rows, places, owner_ref, targets_ref, counts_ref, *rest):
    parts, out_ref, sum_ref = rest[:-2], rest[-2], rest[-1]
    me, mine = lax.axis_index("wide"), lax.axis_index("blk")
    ab = parts[0].shape[1] // (2 * partners)
    sum_ref[...] = jnp.zeros_like(sum_ref)
    for m in range(len(places) // 2):
        tile = find_tile(owner_ref, lax.bitwise_xor(me, m))
        live = counts_ref[tile]
        for k in range(partners):
            target = targets_ref[tile, k]

            @pl.when(k < live)
            def _():
                for n in range(4):
                    part, first = places[2 * m + n // 2]
                    begin = pl.multiple_of(lax.bitwise_xor(mine, n) * ab, 128)
                    column = (2 * k + n % 2) * ab
                    value = parts[part][first : first + rows, column : column + ab]
                    sum_ref[target, :, pl.ds(begin, ab)] += value.astype(jnp.float32)

    outer, inner = out_ref.shape[1:3]
    for i in range(outer):
        out_ref[:, i] = sum_ref[:, i * inner : (i + 1) * inner, :].astype(out_ref.dtype)


def collect(parts, places, owner, targets, counts, shape):
    partners, rows = targets.shape[1], shape[1] * shape[2]
    return pl.pallas_call(
        functools.partial(collect_kernel, partners, rows, places),
        in_specs=[SMEM, SMEM, SMEM] + [pl.BlockSpec(memory_space=pltpu.VMEM)] * len(parts),
        out_specs=pl.BlockSpec(memory_space=pltpu.VMEM),
        out_shape=jax.ShapeDtypeStruct(shape, jnp.bfloat16),
        scratch_shapes=[pltpu.VMEM((shape[0], rows, shape[3]), jnp.float32)],
        compiler_params=pltpu.CompilerParams(vmem_limit_bytes=KERNEL_VMEM),
        name="collect_targets",
    )(owner, targets, counts, *parts)


def after(value, earlier):
    return lax.optimization_barrier((value, *earlier))[0] if earlier else value


def body(amplitudes, integrals, owner, targets, counts):
    wide = lax.axis_size("wide")
    i, j, tiles, width = amplitudes.shape
    rows = i * j
    own = integrals[0]
    done = {}

    def step(name, value, axis, mask, *earlier):
        pairs = [(s, s ^ mask) for s in range(lax.axis_size(axis))]
        value = done[value] if isinstance(value, str) else value
        done[name] = lax.ppermute(after(value, [done[e] for e in earlier]), axis, pairs)

    def chip(m, *earlier):
        step(f"chip{m}", done[f"to{m}"][:rows], "blk", 2, *earlier)

    def product(parts, out_rows, *earlier):
        parts = [done[name] for name in parts]
        parts[0] = after(parts[0], [done[e] for e in earlier])
        return contract(parts, rows, out_rows, done["own"], done["other"])

    def near_far(masks, *earlier):
        parts = [f"{at}{m}" for at in ("to", "chip") for m in masks]
        made = product(parts, [rows] * len(masks) + [rows * len(masks)], *earlier)
        done.update(zip([f"near{m}" for m in masks], made))
        return made[-1]

    def swap_far(name, value, masks, *earlier):
        step(name, value, "blk", 2, *earlier)
        for at, m in enumerate(masks):
            done[f"far{m}"] = done[name][at * rows : (at + 1) * rows]

    def back(m, *earlier):
        both = jnp.concatenate([done[f"near{m}"], done[f"far{m}"]])
        step(f"from{m}", both, "wide", m, *earlier)

    groups = ((0,), (1,), (2,), (3,), (4, 5), (6,), (7,))
    done["to0"], s1, s2, s3, s45, s6, s7 = select(amplitudes, owner, groups)
    step("other", own, "blk", 1)
    step("to4", s45, "wide", 4)
    chip(0, "other")
    step("to1", s1, "wide", 1, "other")
    step("to2", s2, "wide", 2)
    step("to3", s3, "wide", 3)
    done["own"] = hold(after(own, [done[e] for e in ("other",)]))
    chip(1)
    chip(2, "other")
    chip(3)
    step("to6", s6, "wide", 6, "to4", "chip0")
    step("to5", done["to4"][rows:], "wide", 1, "chip0", "chip1")
    near = [f"{at}{m}" for m in range(4) for at in ("to", "chip")]
    made = product(near, [2 * rows] * 4)
    done.update(zip([f"near{m}" for m in range(4)], made))
    chip(4, "chip0")
    chip(5, "near0", "to6", "chip4")
    step("to7", s7, "wide", 7, "to6")
    (done["made45"],) = product(("to4", "chip4", "to5", "chip5"), [4 * rows])

    step("from4", "made45", "wide", 4)
    chip(6, "chip5")
    chip(7, "made45")
    step("from1", "near1", "wide", 1)
    step("from2", "near2", "wide", 2)
    step("from3", "near3", "wide", 3)
    far = near_far((6, 7), "chip6")
    swap_far("swap67", far, (6, 7))
    step("from5", done["from4"][2 * rows :], "wide", 1)
    back(6)
    back(7)
    far = [done["near0"]] + [done[f"from{m}"] for m in (1, 2, 3)]
    step("swap0123", jnp.concatenate([value[rows:] for value in far]), "blk", 2, "swap67")
    far = [done["from4"][: 2 * rows], done["from5"]]
    step("swap45", jnp.concatenate([value[rows:] for value in far]), "blk", 2)
    parts = [done["near0"]] + [done[f"from{m}"] for m in range(1, wide)]
    parts += [done["swap0123"], done["swap45"]]
    places = []
    for m in range(wide):
        places += [(m, 0), (wide, m * rows) if m < 4 else (wide + 1, (m - 4) * rows)]
        if m > 5:
            places[-1] = (m, rows)
    shape = (wide, i, j, lax.axis_size("blk") * own.shape[1])
    return collect(parts, places, owner, targets, counts, shape)


def body_large(amplitudes, integrals, owner, targets, counts):
    wide_count = lax.axis_size("wide")
    my_index = lax.axis_index("wide")
    tile_ids = jnp.arange(owner.shape[0], dtype=jnp.int32)
    holder = jnp.sum(jnp.where(owner[None, :] == tile_ids[:, None], tile_ids[None, :], 0), axis=1)
    ordered = jnp.take(amplitudes, holder, axis=2)
    my_tile = lax.all_to_all(ordered, "wide", split_axis=2, concat_axis=1, tiled=True)
    my_holder = lax.dynamic_index_in_dim(holder, my_index, 0, keepdims=False)
    my_count = lax.dynamic_index_in_dim(counts, my_holder, 0, keepdims=False)
    slot_ids = jnp.arange(targets.shape[1], dtype=jnp.int32)
    live_slots = (slot_ids < my_count).astype(jnp.float32)
    my_integrals = integrals[0]
    width = my_tile.shape[3]
    portion = lax.all_gather(my_tile, "blk", axis=0, tiled=True)
    flat_rows = portion.reshape(-1, width)
    result = jnp.einsum("rc,kac->rka", flat_rows, my_integrals, preferred_element_type=jnp.float32)
    partial_value = result.reshape(
        portion.shape[0], portion.shape[1], my_integrals.shape[0], my_integrals.shape[1]
    )
    shaped = (partial_value * live_slots[None, None, :, None]).astype(jnp.bfloat16)
    received = lax.all_to_all(
        lax.all_to_all(shaped, "wide", split_axis=1, concat_axis=2, tiled=True),
        "blk",
        split_axis=0,
        concat_axis=3,
        tiled=True,
    )
    slot_targets = jnp.take(targets, holder, axis=0).reshape(-1)
    window_ids = jnp.arange(wide_count, dtype=jnp.int32)
    selector = (slot_targets[None, :] == window_ids[:, None]).astype(jnp.bfloat16)
    ladder = jnp.einsum("ps,ijsa->pija", selector, received, preferred_element_type=jnp.float32)
    return ladder.astype(jnp.bfloat16)


def solution(mesh):
    few = mesh.shape["wide"] == 8 and mesh.shape["blk"] == 4
    placed = (P("blk", "wide", None, None), P("wide", None, "blk", None), P(), P(), P())
    return jax.shard_map(
        body if few else body_large,
        mesh=mesh,
        in_specs=placed,
        out_specs=P(None, "blk", "wide", None),
        check_vma=False,
    )
```

```python
import functools

import jax
import jax.numpy as jnp
from jax import lax
from jax.experimental import pallas as pl
from jax.experimental.pallas import tpu as pltpu
from jax.sharding import PartitionSpec as P

MIB = 1 << 20
KERNEL_VMEM = 16 * MIB
CONTRACT_VMEM = 20 * MIB
HOLD_VMEM = 44 * MIB
SMEM = pl.BlockSpec(memory_space=pltpu.SMEM)


def find_tile(owner_ref, slot):
    def step(q, found):
        return jnp.where(owner_ref[q] == slot, q, found)

    return lax.fori_loop(0, owner_ref.shape[0], step, jnp.int32(0))


def select_kernel(rows, groups, owner_ref, amp_ref, *rest):
    outs, pick_ref = rest[:-1], rest[-1]
    tiles = owner_ref.shape[0]

    @pl.when(pl.program_id(0) == 0)
    def _():
        me = lax.axis_index("wide")
        shape = pick_ref.shape
        out_row = lax.broadcasted_iota(jnp.int32, shape, 0)
        in_row = lax.broadcasted_iota(jnp.int32, shape, 1)
        slot = lax.bitwise_xor(out_row // rows, me)
        tile = in_row % tiles
        place = jnp.zeros(shape, jnp.int32)
        for q in range(tiles):
            place = jnp.where(tile == q, owner_ref[q], place)
        chosen = (place == slot) & (out_row % rows == in_row // tiles)
        pick_ref[...] = jnp.where(chosen, 1.0, 0.0).astype(pick_ref.dtype)

    moved = jnp.dot(pick_ref[...], amp_ref[...], preferred_element_type=jnp.float32)
    moved = moved.astype(amp_ref.dtype)
    for group, out in zip(groups, outs):
        for at, m in enumerate(group):
            out[at * rows : (at + 1) * rows] = moved[m * rows : (m + 1) * rows]


def select(amplitudes, owner, groups):
    i, j, tiles, width = amplitudes.shape
    rows = i * j
    wide = sum(map(len, groups))
    block = min(width, 1024)
    return pl.pallas_call(
        functools.partial(select_kernel, rows, groups),
        grid=(width // block,),
        in_specs=[SMEM, pl.BlockSpec((rows * tiles, block), lambda c: (0, c))],
        out_specs=[pl.BlockSpec((len(g) * rows, block), lambda c: (0, c)) for g in groups],
        out_shape=[jax.ShapeDtypeStruct((len(g) * rows, width), amplitudes.dtype) for g in groups],
        scratch_shapes=[pltpu.VMEM((wide * rows, rows * tiles), amplitudes.dtype)],
        compiler_params=pltpu.CompilerParams(vmem_limit_bytes=KERNEL_VMEM),
        cost_estimate=pl.CostEstimate(
            flops=2 * wide * rows * rows * tiles * width,
            bytes_accessed=4 * rows * tiles * width,
            transcendentals=0,
        ),
        name="select_tiles",
    )(owner, amplitudes.reshape(rows * tiles, width))


def hold_kernel(value_ref, held_ref, sem):
    copy = pltpu.make_async_copy(value_ref, held_ref, sem)
    copy.start()
    copy.wait()


def hold(value):
    return pl.pallas_call(
        hold_kernel,
        in_specs=[pl.BlockSpec(memory_space=pl.ANY)],
        out_specs=pl.BlockSpec(memory_space=pltpu.VMEM),
        out_shape=jax.ShapeDtypeStruct(value.shape, value.dtype),
        scratch_shapes=[pltpu.SemaphoreType.DMA],
        compiler_params=pltpu.CompilerParams(vmem_limit_bytes=HOLD_VMEM),
        name="hold_integrals",
    )(value)


def contract_kernel(count, block, *refs):
    parts, integrals = refs[:count], refs[count : count + 2]
    outs, rows_ref, sems = refs[count + 2 : -2], refs[-2], refs[-1]
    rows = rows_ref.shape[0] // count
    partners, ab, _ = integrals[0].shape
    copies = [
        pltpu.make_async_copy(part.at[pl.ds(0, rows)], rows_ref.at[pl.ds(n * rows, rows)], sems.at[n])
        for n, part in enumerate(parts)
    ]
    for copy in copies:
        copy.start()
    for copy in copies:
        copy.wait()
    for source, integ_ref in enumerate(integrals):

        @pl.loop(0, partners * ab // block)
        def _(at):
            k, begin = at // (ab // block), pl.multiple_of(at % (ab // block) * block, block)
            value = lax.dot_general(
                integ_ref[k, pl.ds(begin, block), :],
                rows_ref[...],
                (((1,), (1,)), ((), ())),
                preferred_element_type=jnp.float32,
            ).T.astype(jnp.bfloat16)
            column = pl.multiple_of((2 * k + source) * ab + begin, block)
            first = 0
            for out in outs:
                out[:, pl.ds(column, block)] = value[first : first + out.shape[0]]
                first += out.shape[0]


def contract(parts, rows, out_rows, own, other):
    width = parts[0].shape[1]
    partners, ab, _ = own.shape
    count = len(parts)
    vmem = pl.BlockSpec(memory_space=pltpu.VMEM)
    return pl.pallas_call(
        functools.partial(contract_kernel, count, min(ab, 512)),
        in_specs=[pl.BlockSpec(memory_space=pl.ANY)] * count + [vmem, vmem],
        out_specs=[vmem] * len(out_rows),
        out_shape=[
            jax.ShapeDtypeStruct((each, partners * 2 * ab), jnp.bfloat16) for each in out_rows
        ],
        scratch_shapes=[
            pltpu.VMEM((count * rows, width), parts[0].dtype),
            pltpu.SemaphoreType.DMA((count,)),
        ],
        compiler_params=pltpu.CompilerParams(vmem_limit_bytes=CONTRACT_VMEM),
        name="contract_rows",
    )(*parts, own, other)


def collect_kernel(partners, rows, places, owner_ref, targets_ref, counts_ref, *rest):
    parts, out_ref, sum_ref = rest[:-2], rest[-2], rest[-1]
    me, mine = lax.axis_index("wide"), lax.axis_index("blk")
    ab = parts[0].shape[1] // (2 * partners)
    sum_ref[...] = jnp.zeros_like(sum_ref)
    for m in range(len(places) // 2):
        tile = find_tile(owner_ref, lax.bitwise_xor(me, m))
        live = counts_ref[tile]
        for k in range(partners):
            target = targets_ref[tile, k]

            @pl.when(k < live)
            def _():
                for n in range(4):
                    part, first = places[2 * m + n // 2]
                    begin = pl.multiple_of(lax.bitwise_xor(mine, n) * ab, 128)
                    column = (2 * k + n % 2) * ab
                    value = parts[part][first : first + rows, column : column + ab]
                    sum_ref[target, :, pl.ds(begin, ab)] += value.astype(jnp.float32)

    outer, inner = out_ref.shape[1:3]
    for i in range(outer):
        out_ref[:, i] = sum_ref[:, i * inner : (i + 1) * inner, :].astype(out_ref.dtype)


def collect(parts, places, owner, targets, counts, shape):
    partners, rows = targets.shape[1], shape[1] * shape[2]
    return pl.pallas_call(
        functools.partial(collect_kernel, partners, rows, places),
        in_specs=[SMEM, SMEM, SMEM] + [pl.BlockSpec(memory_space=pltpu.VMEM)] * len(parts),
        out_specs=pl.BlockSpec(memory_space=pltpu.VMEM),
        out_shape=jax.ShapeDtypeStruct(shape, jnp.bfloat16),
        scratch_shapes=[pltpu.VMEM((shape[0], rows, shape[3]), jnp.float32)],
        compiler_params=pltpu.CompilerParams(vmem_limit_bytes=KERNEL_VMEM),
        name="collect_targets",
    )(owner, targets, counts, *parts)


def after(value, earlier):
    return lax.optimization_barrier((value, *earlier))[0] if earlier else value


def body(amplitudes, integrals, owner, targets, counts):
    wide = lax.axis_size("wide")
    i, j, tiles, width = amplitudes.shape
    rows = i * j
    own = integrals[0]
    done = {}

    def step(name, value, axis, mask, *earlier):
        pairs = [(s, s ^ mask) for s in range(lax.axis_size(axis))]
        value = done[value] if isinstance(value, str) else value
        done[name] = lax.ppermute(after(value, [done[e] for e in earlier]), axis, pairs)

    def chip(m, *earlier):
        step(f"chip{m}", done[f"to{m}"][:rows], "blk", 2, *earlier)

    def product(parts, out_rows, *earlier):
        parts = [done[name] for name in parts]
        parts[0] = after(parts[0], [done[e] for e in earlier])
        return contract(parts, rows, out_rows, done["own"], done["other"])

    def near_far(masks, *earlier):
        parts = [f"{at}{m}" for at in ("to", "chip") for m in masks]
        made = product(parts, [rows] * len(masks) + [rows * len(masks)], *earlier)
        done.update(zip([f"near{m}" for m in masks], made))
        return made[-1]

    def swap_far(name, value, masks, *earlier):
        step(name, value, "blk", 2, *earlier)
        for at, m in enumerate(masks):
            done[f"far{m}"] = done[name][at * rows : (at + 1) * rows]

    def back(m, *earlier):
        both = jnp.concatenate([done[f"near{m}"], done[f"far{m}"]])
        step(f"from{m}", both, "wide", m, *earlier)

    groups = ((0,), (1,), (2,), (3,), (4, 5), (6,), (7,))
    done["to0"], s1, s2, s3, s45, s6, s7 = select(amplitudes, owner, groups)
    step("other", own, "blk", 1)
    step("to4", s45, "wide", 4)
    chip(0, "other")
    step("to1", s1, "wide", 1, "other")
    step("to2", s2, "wide", 2)
    step("to3", s3, "wide", 3)
    done["own"] = hold(after(own, [done[e] for e in ("other",)]))
    chip(1)
    chip(2, "other", "chip0", "to1")
    chip(3)
    step("to6", s6, "wide", 6, "to4", "to1")
    step("to5", done["to4"][rows:], "wide", 1, "chip1", "chip0")
    chip(4, "chip1")
    chip(5, "own", "to2", "to3", "chip4", "to6")
    step("to7", s7, "wide", 7, "to6")
    (done["made45"],) = product(("to4", "chip4", "to5", "chip5"), [4 * rows])

    step("from4", "made45", "wide", 4)
    chip(6, "chip5")
    chip(7, "made45")
    near = [f"{at}{m}" for m in range(4) for at in ("to", "chip")]
    made = product(near, [2 * rows] * 4, "made45", "chip6")
    done.update(zip([f"near{m}" for m in range(4)], made))
    step("from1", "near1", "wide", 1)
    step("from2", "near2", "wide", 2)
    step("from3", "near3", "wide", 3)
    far = near_far((6, 7), "chip6", "near0")
    swap_far("swap67", far, (6, 7))
    step("from5", done["from4"][2 * rows :], "wide", 1)
    back(6)
    back(7)
    far = [done["near0"], done["from1"]]
    step("swap01", jnp.concatenate([value[rows:] for value in far]), "blk", 2)
    far = [done["from2"], done["from3"]]
    step("swap23", jnp.concatenate([value[rows:] for value in far]), "blk", 2, "swap67")
    far = [done["from4"][: 2 * rows], done["from5"]]
    step("swap45", jnp.concatenate([value[rows:] for value in far]), "blk", 2)
    parts = [done["near0"]] + [done[f"from{m}"] for m in range(1, wide)]
    parts += [done["swap01"], done["swap23"], done["swap45"]]
    places = []
    for m in range(wide):
        places += [(m, 0), (wide + m // 2, m % 2 * rows)]
        if m > 5:
            places[-1] = (m, rows)
    shape = (wide, i, j, lax.axis_size("blk") * own.shape[1])
    return collect(parts, places, owner, targets, counts, shape)


def body_large(amplitudes, integrals, owner, targets, counts):
    wide_count = lax.axis_size("wide")
    my_index = lax.axis_index("wide")
    tile_ids = jnp.arange(owner.shape[0], dtype=jnp.int32)
    holder = jnp.sum(jnp.where(owner[None, :] == tile_ids[:, None], tile_ids[None, :], 0), axis=1)
    ordered = jnp.take(amplitudes, holder, axis=2)
    my_tile = lax.all_to_all(ordered, "wide", split_axis=2, concat_axis=1, tiled=True)
    my_holder = lax.dynamic_index_in_dim(holder, my_index, 0, keepdims=False)
    my_count = lax.dynamic_index_in_dim(counts, my_holder, 0, keepdims=False)
    slot_ids = jnp.arange(targets.shape[1], dtype=jnp.int32)
    live_slots = (slot_ids < my_count).astype(jnp.float32)
    my_integrals = integrals[0]
    width = my_tile.shape[3]
    portion = lax.all_gather(my_tile, "blk", axis=0, tiled=True)
    flat_rows = portion.reshape(-1, width)
    result = jnp.einsum("rc,kac->rka", flat_rows, my_integrals, preferred_element_type=jnp.float32)
    partial_value = result.reshape(
        portion.shape[0], portion.shape[1], my_integrals.shape[0], my_integrals.shape[1]
    )
    shaped = (partial_value * live_slots[None, None, :, None]).astype(jnp.bfloat16)
    received = lax.all_to_all(
        lax.all_to_all(shaped, "wide", split_axis=1, concat_axis=2, tiled=True),
        "blk",
        split_axis=0,
        concat_axis=3,
        tiled=True,
    )
    slot_targets = jnp.take(targets, holder, axis=0).reshape(-1)
    window_ids = jnp.arange(wide_count, dtype=jnp.int32)
    selector = (slot_targets[None, :] == window_ids[:, None]).astype(jnp.bfloat16)
    ladder = jnp.einsum("ps,ijsa->pija", selector, received, preferred_element_type=jnp.float32)
    return ladder.astype(jnp.bfloat16)


def solution(mesh):
    few = mesh.shape["wide"] == 8 and mesh.shape["blk"] == 4
    placed = (P("blk", "wide", None, None), P("wide", None, "blk", None), P(), P(), P())
    return jax.shard_map(
        body if few else body_large,
        mesh=mesh,
        in_specs=placed,
        out_specs=P(None, "blk", "wide", None),
        check_vma=False,
    )
```

```python
import functools

import jax
import jax.numpy as jnp
from jax import lax
from jax.experimental import pallas as pl
from jax.experimental.pallas import tpu as pltpu
from jax.sharding import PartitionSpec as P

MIB = 1 << 20
KERNEL_VMEM = 16 * MIB
CONTRACT_VMEM = 20 * MIB
HOLD_VMEM = 44 * MIB
SMEM = pl.BlockSpec(memory_space=pltpu.SMEM)


def find_tile(owner_ref, slot):
    def step(q, found):
        return jnp.where(owner_ref[q] == slot, q, found)

    return lax.fori_loop(0, owner_ref.shape[0], step, jnp.int32(0))


def select_kernel(rows, groups, owner_ref, amp_ref, *rest):
    outs, pick_ref = rest[:-1], rest[-1]
    tiles = owner_ref.shape[0]

    @pl.when(pl.program_id(0) == 0)
    def _():
        me = lax.axis_index("wide")
        shape = pick_ref.shape
        out_row = lax.broadcasted_iota(jnp.int32, shape, 0)
        in_row = lax.broadcasted_iota(jnp.int32, shape, 1)
        slot = lax.bitwise_xor(out_row // rows, me)
        tile = in_row % tiles
        place = jnp.zeros(shape, jnp.int32)
        for q in range(tiles):
            place = jnp.where(tile == q, owner_ref[q], place)
        chosen = (place == slot) & (out_row % rows == in_row // tiles)
        pick_ref[...] = jnp.where(chosen, 1.0, 0.0).astype(pick_ref.dtype)

    moved = jnp.dot(pick_ref[...], amp_ref[...], preferred_element_type=jnp.float32)
    moved = moved.astype(amp_ref.dtype)
    for group, out in zip(groups, outs):
        for at, m in enumerate(group):
            out[at * rows : (at + 1) * rows] = moved[m * rows : (m + 1) * rows]


def select(amplitudes, owner, groups):
    i, j, tiles, width = amplitudes.shape
    rows = i * j
    wide = sum(map(len, groups))
    block = min(width, 1024)
    return pl.pallas_call(
        functools.partial(select_kernel, rows, groups),
        grid=(width // block,),
        in_specs=[SMEM, pl.BlockSpec((rows * tiles, block), lambda c: (0, c))],
        out_specs=[pl.BlockSpec((len(g) * rows, block), lambda c: (0, c)) for g in groups],
        out_shape=[jax.ShapeDtypeStruct((len(g) * rows, width), amplitudes.dtype) for g in groups],
        scratch_shapes=[pltpu.VMEM((wide * rows, rows * tiles), amplitudes.dtype)],
        compiler_params=pltpu.CompilerParams(vmem_limit_bytes=KERNEL_VMEM),
        cost_estimate=pl.CostEstimate(
            flops=2 * wide * rows * rows * tiles * width,
            bytes_accessed=4 * rows * tiles * width,
            transcendentals=0,
        ),
        name="select_tiles",
    )(owner, amplitudes.reshape(rows * tiles, width))


def hold_kernel(value_ref, held_ref, sem):
    copy = pltpu.make_async_copy(value_ref, held_ref, sem)
    copy.start()
    copy.wait()


def hold(value):
    return pl.pallas_call(
        hold_kernel,
        in_specs=[pl.BlockSpec(memory_space=pl.ANY)],
        out_specs=pl.BlockSpec(memory_space=pltpu.VMEM),
        out_shape=jax.ShapeDtypeStruct(value.shape, value.dtype),
        scratch_shapes=[pltpu.SemaphoreType.DMA],
        compiler_params=pltpu.CompilerParams(vmem_limit_bytes=HOLD_VMEM),
        name="hold_integrals",
    )(value)


def contract_kernel(count, block, *refs):
    parts, integrals = refs[:count], refs[count : count + 2]
    outs, rows_ref, sems = refs[count + 2 : -2], refs[-2], refs[-1]
    rows = rows_ref.shape[0] // count
    partners, ab, _ = integrals[0].shape
    copies = [
        pltpu.make_async_copy(part.at[pl.ds(0, rows)], rows_ref.at[pl.ds(n * rows, rows)], sems.at[n])
        for n, part in enumerate(parts)
    ]
    for copy in copies:
        copy.start()
    for copy in copies:
        copy.wait()
    for source, integ_ref in enumerate(integrals):

        @pl.loop(0, partners * ab // block)
        def _(at):
            k, begin = at // (ab // block), pl.multiple_of(at % (ab // block) * block, block)
            value = lax.dot_general(
                integ_ref[k, pl.ds(begin, block), :],
                rows_ref[...],
                (((1,), (1,)), ((), ())),
                preferred_element_type=jnp.float32,
            ).T.astype(jnp.bfloat16)
            column = pl.multiple_of((2 * k + source) * ab + begin, block)
            first = 0
            for out in outs:
                out[:, pl.ds(column, block)] = value[first : first + out.shape[0]]
                first += out.shape[0]


def contract(parts, rows, out_rows, own, other):
    width = parts[0].shape[1]
    partners, ab, _ = own.shape
    count = len(parts)
    vmem = pl.BlockSpec(memory_space=pltpu.VMEM)
    return pl.pallas_call(
        functools.partial(contract_kernel, count, min(ab, 512)),
        in_specs=[pl.BlockSpec(memory_space=pl.ANY)] * count + [vmem, vmem],
        out_specs=[vmem] * len(out_rows),
        out_shape=[
            jax.ShapeDtypeStruct((each, partners * 2 * ab), jnp.bfloat16) for each in out_rows
        ],
        scratch_shapes=[
            pltpu.VMEM((count * rows, width), parts[0].dtype),
            pltpu.SemaphoreType.DMA((count,)),
        ],
        compiler_params=pltpu.CompilerParams(vmem_limit_bytes=CONTRACT_VMEM),
        name="contract_rows",
    )(*parts, own, other)


def collect_kernel(partners, rows, places, owner_ref, targets_ref, counts_ref, *rest):
    parts, out_ref, sum_ref = rest[:-2], rest[-2], rest[-1]
    me, mine = lax.axis_index("wide"), lax.axis_index("blk")
    ab = parts[0].shape[1] // (2 * partners)
    sum_ref[...] = jnp.zeros_like(sum_ref)
    for m in range(len(places) // 2):
        tile = find_tile(owner_ref, lax.bitwise_xor(me, m))
        live = counts_ref[tile]
        for k in range(partners):
            target = targets_ref[tile, k]

            @pl.when(k < live)
            def _():
                for n in range(4):
                    part, first = places[2 * m + n // 2]
                    begin = pl.multiple_of(lax.bitwise_xor(mine, n) * ab, 128)
                    column = (2 * k + n % 2) * ab
                    value = parts[part][first : first + rows, column : column + ab]
                    sum_ref[target, :, pl.ds(begin, ab)] += value.astype(jnp.float32)

    outer, inner = out_ref.shape[1:3]
    for i in range(outer):
        out_ref[:, i] = sum_ref[:, i * inner : (i + 1) * inner, :].astype(out_ref.dtype)


def collect(parts, places, owner, targets, counts, shape):
    partners, rows = targets.shape[1], shape[1] * shape[2]
    return pl.pallas_call(
        functools.partial(collect_kernel, partners, rows, places),
        in_specs=[SMEM, SMEM, SMEM] + [pl.BlockSpec(memory_space=pltpu.VMEM)] * len(parts),
        out_specs=pl.BlockSpec(memory_space=pltpu.VMEM),
        out_shape=jax.ShapeDtypeStruct(shape, jnp.bfloat16),
        scratch_shapes=[pltpu.VMEM((shape[0], rows, shape[3]), jnp.float32)],
        compiler_params=pltpu.CompilerParams(vmem_limit_bytes=KERNEL_VMEM),
        name="collect_targets",
    )(owner, targets, counts, *parts)


def after(value, earlier):
    return lax.optimization_barrier((value, *earlier))[0] if earlier else value


def body(amplitudes, integrals, owner, targets, counts):
    wide = lax.axis_size("wide")
    i, j, tiles, width = amplitudes.shape
    rows = i * j
    own = integrals[0]
    done = {}

    def step(name, value, axis, mask, *earlier):
        pairs = [(s, s ^ mask) for s in range(lax.axis_size(axis))]
        value = done[value] if isinstance(value, str) else value
        done[name] = lax.ppermute(after(value, [done[e] for e in earlier]), axis, pairs)

    def chip(m, *earlier):
        step(f"chip{m}", done[f"to{m}"][:rows], "blk", 2, *earlier)

    def product(parts, out_rows, *earlier):
        parts = [done[name] for name in parts]
        parts[0] = after(parts[0], [done[e] for e in earlier])
        return contract(parts, rows, out_rows, done["own"], done["other"])

    def near_far(masks, *earlier):
        parts = [f"{at}{m}" for at in ("to", "chip") for m in masks]
        made = product(parts, [rows] * len(masks) + [rows * len(masks)], *earlier)
        done.update(zip([f"near{m}" for m in masks], made))
        return made[-1]

    def swap_far(name, value, masks, *earlier):
        step(name, value, "blk", 2, *earlier)
        for at, m in enumerate(masks):
            done[f"far{m}"] = done[name][at * rows : (at + 1) * rows]

    def back(m, *earlier):
        both = jnp.concatenate([done[f"near{m}"], done[f"far{m}"]])
        step(f"from{m}", both, "wide", m, *earlier)

    groups = ((0,), (1,), (2,), (3,), (4, 5), (6,), (7,))
    done["to0"], s1, s2, s3, s45, s6, s7 = select(amplitudes, owner, groups)
    step("other", own, "blk", 1)
    step("to2", s2, "wide", 2)
    step("to3", s3, "wide", 3)
    step("to4", s45, "wide", 4)
    chip(0, "other")
    step("to1", s1, "wide", 1, "other")
    done["own"] = hold(after(own, [done["other"]]))
    chip(1, "other")
    chip(2, "other", "chip0", "to1")
    chip(3, "other")
    step("to6", s6, "wide", 6, "to4", "to1")
    step("to5", done["to4"][rows:], "wide", 1, "chip1")
    chip(4, "chip2")
    chip(5, "to6", "chip0", "chip1", "chip3", "own")
    step("to7", s7, "wide", 7, "chip4")
    (done["made45"],) = product(("to4", "chip4", "to5", "chip5"), [4 * rows])

    step("from4", "made45", "wide", 4)
    chip(6, "chip5")
    chip(7, "made45")
    near = [f"{at}{m}" for m in range(4) for at in ("to", "chip")]
    made = product(near, [2 * rows] * 4, "made45")
    done.update(zip([f"near{m}" for m in range(4)], made))
    step("from1", "near1", "wide", 1)
    step("from2", "near2", "wide", 2)
    step("from3", "near3", "wide", 3)
    far = near_far((6, 7), "chip6", "near0")
    swap_far("swap67", far, (6, 7))
    step("from5", done["from4"][2 * rows :], "wide", 1)
    back(6)
    back(7)
    far = [done["near0"]] + [done[f"from{m}"] for m in (1, 2, 3)]
    step("swap0123", jnp.concatenate([value[rows:] for value in far]), "blk", 2)
    far = [done["from4"][: 2 * rows], done["from5"]]
    step("swap45", jnp.concatenate([value[rows:] for value in far]), "blk", 2)
    parts = [done["near0"]] + [done[f"from{m}"] for m in range(1, wide)]
    parts += [done["swap0123"], done["swap45"]]
    places = []
    for m in range(wide):
        places += [(m, 0), (wide, m * rows) if m < 4 else (wide + 1, (m - 4) * rows)]
        if m > 5:
            places[-1] = (m, rows)
    shape = (wide, i, j, lax.axis_size("blk") * own.shape[1])
    return collect(parts, places, owner, targets, counts, shape)


def body_large(amplitudes, integrals, owner, targets, counts):
    wide_count = lax.axis_size("wide")
    my_index = lax.axis_index("wide")
    tile_ids = jnp.arange(owner.shape[0], dtype=jnp.int32)
    holder = jnp.sum(jnp.where(owner[None, :] == tile_ids[:, None], tile_ids[None, :], 0), axis=1)
    ordered = jnp.take(amplitudes, holder, axis=2)
    my_tile = lax.all_to_all(ordered, "wide", split_axis=2, concat_axis=1, tiled=True)
    my_holder = lax.dynamic_index_in_dim(holder, my_index, 0, keepdims=False)
    my_count = lax.dynamic_index_in_dim(counts, my_holder, 0, keepdims=False)
    slot_ids = jnp.arange(targets.shape[1], dtype=jnp.int32)
    live_slots = (slot_ids < my_count).astype(jnp.float32)
    my_integrals = integrals[0]
    width = my_tile.shape[3]
    portion = lax.all_gather(my_tile, "blk", axis=0, tiled=True)
    flat_rows = portion.reshape(-1, width)
    result = jnp.einsum("rc,kac->rka", flat_rows, my_integrals, preferred_element_type=jnp.float32)
    partial_value = result.reshape(
        portion.shape[0], portion.shape[1], my_integrals.shape[0], my_integrals.shape[1]
    )
    shaped = (partial_value * live_slots[None, None, :, None]).astype(jnp.bfloat16)
    received = lax.all_to_all(
        lax.all_to_all(shaped, "wide", split_axis=1, concat_axis=2, tiled=True),
        "blk",
        split_axis=0,
        concat_axis=3,
        tiled=True,
    )
    slot_targets = jnp.take(targets, holder, axis=0).reshape(-1)
    window_ids = jnp.arange(wide_count, dtype=jnp.int32)
    selector = (slot_targets[None, :] == window_ids[:, None]).astype(jnp.bfloat16)
    ladder = jnp.einsum("ps,ijsa->pija", selector, received, preferred_element_type=jnp.float32)
    return ladder.astype(jnp.bfloat16)


def solution(mesh):
    few = mesh.shape["wide"] == 8 and mesh.shape["blk"] == 4
    placed = (P("blk", "wide", None, None), P("wide", None, "blk", None), P(), P(), P())
    return jax.shard_map(
        body if few else body_large,
        mesh=mesh,
        in_specs=placed,
        out_specs=P(None, "blk", "wide", None),
        check_vma=False,
    )
```
